32 devices in a mesh: seq: 16 (over z, y, x), head: 2 (over core).
Axes of the slice: x: 2, y: 2, z: 4, core: 2. Of those that a mesh axis runs over, the one named last changes fastest.
Arguments:
- input_rows: bfloat16 [4096, 4096], P(('seq', 'head')), may hold values from -40 to 40
- doc_lengths: int32 [8], replicated, may hold values from 1 to 1024, 4096 in all
- w_query: bfloat16 [4096, 4096], P(None, 'head'), may hold values from -0.09375 to 0.09375
- key_weight: bfloat16 [4096, 1024], P(None, 'head'), may hold values from -0.09375 to 0.09375
- value_weight: bfloat16 [4096, 1024], P(None, 'head'), may hold values from -0.09375 to 0.09375
- w_out: bfloat16 [4096, 4096], P('head'), may hold values from -0.5 to 0.5
Outputs:
- mixed: bfloat16 [4096, 4096], P(('seq', 'head'))
The draws below stay inside these ranges and needn't reach their ends.
All inputs are finite; a program needn't handle non-finite values.
Results may differ from the reference program's by a relative error of at most 0.013.
Values may be sent and summed in bfloat16 or wider, within the bound.
No kernel may reach another device: no remote copies, remote signals or barrier semaphores. Data moves between devices by JAX's collectives and lax.ppermute only.
A program may use at most 192 MiB of HBM per device.

```python
import math
import jax
import jax.numpy as jnp
import numpy as np
from jax import lax

MODEL_WIDTH = 4096
QUERY_HEADS = 32
KEY_VALUE_HEADS = 8
HEAD_SIZE = 128
TOK_SEQ = 256
REACH = 4
WINDOW_TOKENS = 4096
DOC_MAX = 1024
DOCS = 8
N_SEQ = 16


def draw_input_rows(key, part):
    first = jax.random.fold_in(key, 0)
    base = jax.random.normal(first, (WINDOW_TOKENS, MODEL_WIDTH), jnp.float32)
    return jnp.clip(base, -6.0, 6.0).astype(jnp.bfloat16)


def steps_of(own_key, dims, cuts, low, largest):
    loudness = 1.0
    for position, shards_of in cuts:
        heights = jax.random.uniform(jax.random.fold_in(jax.random.fold_in(own_key, 6), position), (shards_of,), jnp.float32, low / len(cuts), largest / len(cuts))
        loudness = loudness * jnp.repeat(jnp.exp(heights), dims[position] // shards_of).reshape((-1,) + (1,) * (len(dims) - 1 - position))
    return loudness


def profile(count, total, most, slope):
    loads = [(1 << 20) // math.isqrt(grade ** slope) + 1 for grade in range(2, count + 1)]
    rest, given = total - most - (count - 1), [1] * (count - 1)
    while rest > 0:
        free = [i for i in range(count - 1) if given[i] < most]
        pool, budget = sum([loads[i] for i in free]), rest
        for i in free:
            more = min(most - given[i], max(1, budget * loads[i] // pool), rest)
            given[i] = given[i] + more
            rest = rest - more
    return np.array([most] + given)


def uneven_parts(key, number_of, total, reach, slope):
    if number_of == 2:
        one = jax.random.randint(key, (), max(1, total - reach), min(reach, total - 1) + 1)
        return jnp.stack([one, total - one])
    sizes = jnp.asarray(profile(number_of, total, reach, slope), jnp.int32)
    twos = (number_of - 1) // 2
    giver, sink = sizes[1:1 + 2 * twos:2], sizes[2:2 + 2 * twos:2]
    room = jnp.minimum(giver - 1, reach - sink)
    moved = jax.random.randint(jax.random.fold_in(key, 1), (twos,), 0, 1 << 20) % (room + 1)
    sizes = sizes.at[1:1 + 2 * twos:2].set(giver - moved).at[2:2 + 2 * twos:2].set(sink + moved)
    return sizes[jax.random.permutation(jax.random.fold_in(key, 2), number_of)]


def centred(own_key, shape, deviation, limit, pieces=(), held_as=jnp.bfloat16):
    entries = jax.random.normal(own_key, shape, jnp.float32) * deviation
    if len(pieces) > 0:
        entries = steps_of(own_key, shape, pieces, -0.22, 0.18) * entries
    return jnp.clip(entries, min=-limit, max=limit).astype(held_as)


def setup_inputs(seed: int = 0) -> dict:
    arg_keys = jax.random.split(jax.random.key(seed), 7)
    return {
        "input_rows": draw_input_rows(jax.random.fold_in(arg_keys[6], 71), 0),
        "doc_lengths": uneven_parts(arg_keys[1], DOCS, WINDOW_TOKENS, DOC_MAX, 2).astype(jnp.int32),
        "w_query": centred(arg_keys[2], (MODEL_WIDTH, QUERY_HEADS * HEAD_SIZE), MODEL_WIDTH ** -0.5, 0.09375, ((1, 2),)),
        "key_weight": centred(arg_keys[3], (MODEL_WIDTH, KEY_VALUE_HEADS * HEAD_SIZE), MODEL_WIDTH ** -0.5, 0.09375, ((1, 2),)),
        "value_weight": centred(arg_keys[4], (MODEL_WIDTH, KEY_VALUE_HEADS * HEAD_SIZE), MODEL_WIDTH ** -0.5, 0.09375, ((1, 2),)),
        "w_out": centred(arg_keys[5], (QUERY_HEADS * HEAD_SIZE, MODEL_WIDTH), HEAD_SIZE ** -0.5, 0.5, ((0, 2),)),
    }


NEG_FILL = -1.0e30


def inverse_frequency():
    table = []
    for number in range(HEAD_SIZE // 2):
        base_freq = 500000.0 ** (-(2.0 * number) / HEAD_SIZE)
        wavelength = 2.0 * math.pi / base_freq
        smooth = (8192.0 / wavelength - 1.0) / 3.0
        if wavelength < 2048.0:
            table.append(base_freq)
        elif wavelength > 8192.0:
            table.append(base_freq / 8.0)
        else:
            table.append((1.0 - smooth) * base_freq / 8.0 + smooth * base_freq)
    return jnp.asarray(table, dtype=jnp.float32)


def rotate(value_matrix, cosine, sine_table):
    half_size = value_matrix.shape[-1] // 2
    first = value_matrix[..., :half_size]
    second = value_matrix[..., half_size:]
    return jnp.concatenate([first * cosine - second * sine_table, second * cosine + first * sine_table], axis=-1)


def reference(input_rows, doc_lengths, w_query, key_weight, value_weight, w_out):
    positions = jnp.arange(WINDOW_TOKENS, dtype=jnp.int32)
    doc_ends = jnp.cumsum(doc_lengths).astype(jnp.int32)
    doc_ids = jnp.sum((positions[:, None] >= doc_ends[None, :]).astype(jnp.int32), axis=1).astype(jnp.int32)
    angles = positions.astype(jnp.float32)[:, None] * inverse_frequency()[None, :]
    cosine = jnp.cos(angles)[:, None, :]
    sine_table = jnp.sin(angles)[:, None, :]
    query_matrix = jnp.dot(input_rows, w_query, preferred_element_type=jnp.float32).reshape(WINDOW_TOKENS, QUERY_HEADS, HEAD_SIZE)
    query_matrix = rotate(query_matrix, cosine, sine_table).astype(jnp.bfloat16)
    key_matrix = jnp.dot(input_rows, key_weight, preferred_element_type=jnp.float32).reshape(WINDOW_TOKENS, KEY_VALUE_HEADS, HEAD_SIZE)
    key_matrix = rotate(key_matrix, cosine, sine_table).astype(jnp.bfloat16)
    value_matrix = jnp.dot(input_rows, value_weight, preferred_element_type=jnp.float32).astype(jnp.bfloat16).reshape(WINDOW_TOKENS, KEY_VALUE_HEADS, HEAD_SIZE)
    query_group = QUERY_HEADS // KEY_VALUE_HEADS
    grouped_queries = query_matrix.reshape(WINDOW_TOKENS, KEY_VALUE_HEADS, query_group, HEAD_SIZE)
    span = (REACH + 1) * TOK_SEQ
    scale = HEAD_SIZE ** -0.5

    def block(index):
        index = index.astype(jnp.int32)
        q_start = index * TOK_SEQ
        k_start = (jnp.clip(index - REACH, 0, N_SEQ - REACH - 1) * TOK_SEQ).astype(jnp.int32)
        q_block = lax.dynamic_slice_in_dim(grouped_queries, q_start, TOK_SEQ, 0).astype(jnp.float32)
        k_block = lax.dynamic_slice_in_dim(key_matrix, k_start, span, 0).astype(jnp.float32)
        v_block = lax.dynamic_slice_in_dim(value_matrix, k_start, span, 0).astype(jnp.float32)
        q_pos = q_start + jnp.arange(TOK_SEQ, dtype=jnp.int32)
        k_pos = k_start + jnp.arange(span, dtype=jnp.int32)
        q_doc = lax.dynamic_slice_in_dim(doc_ids, q_start, TOK_SEQ, 0)
        k_doc = lax.dynamic_slice_in_dim(doc_ids, k_start, span, 0)
        scores = jnp.einsum("tkgd,skd->kgts", q_block, k_block) * scale
        allowed = (q_doc[:, None] == k_doc[None, :]) & (k_pos[None, :] <= q_pos[:, None])
        scores = jnp.where(allowed, scores, NEG_FILL)
        row_max = jnp.max(scores, axis=-1, keepdims=True)
        weights = jnp.where(allowed, jnp.exp(scores - row_max), 0.0)
        totals = jnp.sum(weights, axis=-1)
        rounded = lax.optimization_barrier(weights.astype(jnp.bfloat16)).astype(jnp.float32)
        output = jnp.einsum("kgts,skd->kgtd", rounded, v_block) / totals[..., None]
        return output.transpose(2, 0, 1, 3).reshape(TOK_SEQ, QUERY_HEADS * HEAD_SIZE).astype(jnp.bfloat16)

    blocks = lax.map(block, jnp.arange(N_SEQ, dtype=jnp.int32))
    attended = blocks.reshape(WINDOW_TOKENS, QUERY_HEADS * HEAD_SIZE)
    return jnp.dot(attended, w_out, preferred_element_type=jnp.float32).astype(jnp.bfloat16)
```

```python
import functools
import math

import jax
import jax.numpy as jnp
from jax import lax
from jax.experimental import pallas as pl
from jax.experimental.pallas import tpu as pltpu
from jax.sharding import PartitionSpec as P

HEAD_SIZE = 128
LAYER = 4
MASKED = -1e30
SCORE_SCALE = math.log2(math.e) * HEAD_SIZE ** (-0.5)
SWAP = [(0, 1), (1, 0)]
VMEM = pl.BlockSpec(memory_space=pltpu.VMEM)
SMEM = pl.BlockSpec(memory_space=pltpu.SMEM)
ANY = pl.BlockSpec(memory_space=pl.ANY)


def inverse_frequency():
    table = []
    for number in range(HEAD_SIZE // 2):
        base_freq = 500000.0 ** (-(2.0 * number) / HEAD_SIZE)
        wavelength = 2.0 * math.pi / base_freq
        smooth = (8192.0 / wavelength - 1.0) / 3.0
        if wavelength < 2048.0:
            table.append(base_freq)
        elif wavelength > 8192.0:
            table.append(base_freq / 8.0)
        else:
            table.append((1.0 - smooth) * base_freq / 8.0 + smooth * base_freq)
    return table


def dot(a, b):
    return jnp.dot(a, b, preferred_element_type=jnp.float32)


def rotated(block, cosine, sine):
    return block * cosine + pltpu.roll(block, HEAD_SIZE // 2, 1) * sine


def first_half_kernel(chunks, place, lengths, own_hbm, key_hbm, value_hbm, key_sum, value_sum, own, w_key, w_value, cosine, sine, starts, sems):
    depth = w_key.shape[0] // chunks
    row_copy = pltpu.make_async_copy(own_hbm, own, sems.at[2 * chunks])
    row_copy.start()
    copies = []
    for number in range(chunks):
        at = pl.ds(number * depth, depth)
        pair = (
            pltpu.make_async_copy(key_hbm.at[at], w_key.at[at], sems.at[2 * number]),
            pltpu.make_async_copy(value_hbm.at[at], w_value.at[at], sems.at[2 * number + 1]),
        )
        for copy in pair:
            copy.start()
        copies.append(pair)
    tokens = cosine.shape[0]
    lane = lax.broadcasted_iota(jnp.int32, (1, HEAD_SIZE), 1)
    pair_of_lane = lane % (HEAD_SIZE // 2)
    freq = jnp.zeros((1, HEAD_SIZE), jnp.float32)
    for number, value in enumerate(inverse_frequency()):
        freq = jnp.where(pair_of_lane == number, jnp.float32(value), freq)
    positions = place[1] * tokens + lax.broadcasted_iota(jnp.int32, (tokens, HEAD_SIZE), 0)
    angles = positions.astype(jnp.float32) * freq
    cosine[...] = jnp.cos(angles)
    turned = jnp.sin(angles)
    sine[...] = jnp.where(lane < HEAD_SIZE // 2, -turned, turned)
    start = jnp.zeros((tokens, HEAD_SIZE), jnp.int32)
    end = jnp.int32(0)
    for number in range(lengths.shape[0]):
        end = end + lengths[number]
        start = jnp.where(positions >= end, end, start)
    starts[...] = start
    row_copy.wait()
    for number, pair in enumerate(copies):
        at = slice(number * depth, (number + 1) * depth)
        rows = own[:, at]
        for copy, weight, total in zip(pair, (w_key, w_value), (key_sum, value_sum)):
            copy.wait()
            product = dot(rows, weight[at, :])
            total[...] = product if number == 0 else total[...] + product


def second_half_kernel(place, other, w_key, w_value, key_own, value_own, cosine, sine, kv):
    half, width = key_own.shape
    mine = pl.multiple_of(place[0] * half, half)
    theirs = pl.multiple_of((1 - place[0]) * half, half)
    for weight, own, turn, offset in ((w_key, key_own, True, 0), (w_value, value_own, False, width)):
        result = dot(other[...], weight[...])
        for rows, block in ((mine, own[...]), (theirs, result)):
            here = pl.ds(rows, half)
            for head in range(width // HEAD_SIZE):
                at = slice(head * HEAD_SIZE, (head + 1) * HEAD_SIZE)
                out = slice(offset + head * HEAD_SIZE, offset + (head + 1) * HEAD_SIZE)
                piece = block[:, at]
                if turn:
                    piece = rotated(piece, cosine[here, :], sine[here, :])
                kv[here, out] = piece.astype(kv.dtype)


def query_kernel(place, own, other, weight, cosine, sine, query, rows):
    half = own.shape[0]
    rows[pl.ds(pl.multiple_of(place[0] * half, half), half), :] = own[...]
    rows[pl.ds(pl.multiple_of((1 - place[0]) * half, half), half), :] = other[...]
    wide = 4 * HEAD_SIZE
    for number in range(weight.shape[1] // wide):
        result = dot(rows[...], weight[:, number * wide : (number + 1) * wide])
        for head in range(wide // HEAD_SIZE):
            at = slice(head * HEAD_SIZE, (head + 1) * HEAD_SIZE)
            out = slice(number * wide + head * HEAD_SIZE, number * wide + (head + 1) * HEAD_SIZE)
            query[:, out] = rotated(result[:, at], cosine[...], sine[...]).astype(query.dtype)


def relay_kernel(place, kv, from_z, after, to_x, to_y):
    own, earlier = kv[...], from_z[...]
    to_x[...] = jnp.where(place[1] % 2 > 0, earlier, own)
    to_y[...] = jnp.where(place[1] % LAYER >= 2, earlier, own)


def attend_kernel(counts, distances, first, last, place, starts, query, *refs):
    refs = list(refs)
    blocks = [[refs.pop(0) for _ in range(copies)] for copies in counts]
    count = len(counts)

    def part(block, at):
        return block[0][:, at] if len(block) == 1 else block[0][:, at] + block[1][:, at]

    if not first:
        old_max, old_sum, old_acc = (refs.pop(0) for _ in range(3))
    if last:
        attended = refs.pop(0)
    else:
        new_max, new_sum, new_acc = (refs.pop(0) for _ in range(3))
    if first:
        done = refs.pop(0)
        done[...] = jnp.zeros_like(done)
    bias = refs.pop(0)
    tokens = query.shape[0]
    kv_heads = blocks[0][0].shape[1] // (2 * HEAD_SIZE)
    group = query.shape[1] // HEAD_SIZE // kv_heads
    base = place[1] * tokens
    query_pos = base + lax.broadcasted_iota(jnp.int32, (tokens, tokens), 0)
    start = jnp.concatenate([starts[...]] * (tokens // starts.shape[1]), axis=1)
    for number in range(count):
        even, odd = distances[number]
        key_pos = base - tokens * jnp.where(place[1] % 2 > 0, odd, even) + lax.broadcasted_iota(jnp.int32, (tokens, tokens), 1)
        allowed = (key_pos >= start) & (key_pos <= query_pos)
        bias[:, number * tokens : (number + 1) * tokens] = jnp.where(allowed, 0.0, MASKED)

    ones = jnp.ones((count * tokens, HEAD_SIZE), query.dtype)
    for kv_head in range(kv_heads):
        at = slice(kv_head * HEAD_SIZE, (kv_head + 1) * HEAD_SIZE)
        at_value = slice((kv_heads + kv_head) * HEAD_SIZE, (kv_heads + kv_head + 1) * HEAD_SIZE)
        keys = jnp.concatenate([part(block, at) for block in blocks], axis=0)
        values = jnp.concatenate([part(block, at_value) for block in blocks], axis=0)
        values = jnp.concatenate([values, ones], axis=1)
        for member in range(group):
            head = kv_head * group + member
            here = slice(head * HEAD_SIZE, (head + 1) * HEAD_SIZE)
            scores = lax.dot_general(
                query[:, here], keys, (((1,), (1,)), ((), ())), preferred_element_type=jnp.float32
            )
            scores = scores * SCORE_SCALE + bias[...]
            top = jnp.max(scores, axis=1, keepdims=True)
            if not first:
                before = old_max[head][:, :1]
                top = jnp.maximum(top, before)
                factor = jnp.exp2(before - top)
            weights = jnp.exp2(scores - top).astype(query.dtype)
            product = dot(weights, values)
            acc, total = product[:, :HEAD_SIZE], product[:, HEAD_SIZE:]
            if not first:
                acc = acc + old_acc[head] * factor
                total = total + old_sum[head] * factor
            if last:
                attended[:, here] = (acc / total).astype(attended.dtype)
            else:
                new_max[head] = jnp.broadcast_to(top, (tokens, HEAD_SIZE))
                new_sum[head] = total
                new_acc[head] = acc


def out_kernel(low, high, place, attended, weight, own, send):
    half = own.shape[0]
    on_high = place[0] > 0
    wide = 4 * HEAD_SIZE
    for number in range((high - low) // wide):
        at = slice(number * wide, (number + 1) * wide)
        result = dot(attended[...], weight[:, low + number * wide : low + (number + 1) * wide])
        own[:, at] = jnp.where(on_high, result[half:], result[:half])
        send[:, at] = jnp.where(on_high, result[:half], result[half:]).astype(send.dtype)


def add_kernel(own_low, own_high, got_low, got_high, mixed):
    cut = own_low.shape[1]
    for at, own, got in ((slice(0, cut), own_low, got_low), (slice(cut, mixed.shape[1]), own_high, got_high)):
        mixed[:, at] = (own[...] + got[...].astype(jnp.float32)).astype(mixed.dtype)


def call(kernel, name, outs, in_specs, flops, nbytes, limit, scratch=()):
    return pl.pallas_call(
        kernel,
        out_shape=outs,
        in_specs=in_specs,
        out_specs=[VMEM] * len(outs),
        scratch_shapes=list(scratch),
        name=name,
        cost_estimate=pl.CostEstimate(flops=flops, bytes_accessed=nbytes, transcendentals=0),
        compiler_params=pltpu.CompilerParams(vmem_limit_bytes=limit << 20),
    )


def in_hbm(array):
    return pltpu.with_memory_space_constraint(array, pltpu.HBM)


def body(input_rows, doc_lengths, w_query, key_weight, value_weight, w_out):
    half, model = input_rows.shape
    tokens = 2 * half
    width_q, width_k = w_query.shape[1], key_weight.shape[1]
    heads = width_q // HEAD_SIZE
    shards = lax.axis_size("seq")
    place = jnp.stack([lax.axis_index("head"), lax.axis_index("seq")]).astype(jnp.int32)
    bf16, f32 = jnp.bfloat16, jnp.float32
    shape = pltpu.VMEM

    other = lax.ppermute(input_rows, "head", SWAP)

    chunks = 8
    key_own, value_own, own, w_key, w_value, cosine, sine, starts = call(
        functools.partial(first_half_kernel, chunks), "keys_values_own",
        [
            shape((half, width_k), f32), shape((half, width_k), f32), shape((half, model), bf16),
            shape(key_weight.shape, bf16), shape(value_weight.shape, bf16),
            shape((tokens, HEAD_SIZE), f32), shape((tokens, HEAD_SIZE), f32), shape((tokens, HEAD_SIZE), jnp.int32),
        ],
        [SMEM, SMEM, ANY, ANY, ANY], 4 * half * model * width_k, 4 * model * width_k, 16,
        [pltpu.SemaphoreType.DMA((2 * chunks + 1,))],
    )(place, doc_lengths, in_hbm(input_rows), in_hbm(key_weight), in_hbm(value_weight))
    (kv,) = call(
        second_half_kernel, "keys_values_other", [shape((tokens, 2 * width_k), bf16)],
        [SMEM] + [VMEM] * 7, 16 * half * model * width_k, 4 * model * width_k, 16,
    )(place, other, w_key, w_value, key_own, value_own, cosine, sine)

    every = range(shards)

    def sent(value, pairs):
        return lax.ppermute(value, "seq", [(a, b) for a, b in pairs if 0 <= a < shards and 0 <= b < shards])

    from_z = sent(kv, [(i, i + LAYER) for i in every])
    from_d = sent(kv, [(i, i + (3 if i % 2 == 0 else 1)) for i in every])

    (query,) = call(
        query_kernel, "queries", [shape((tokens, width_q), bf16)], [SMEM] + [VMEM] * 5,
        2 * tokens * model * width_q, 2 * model * width_q, 16, [pltpu.VMEM((tokens, model), bf16)],
    )(place, own, other, w_query, cosine, sine)

    state_shape = [shape((heads, tokens, HEAD_SIZE), f32)] * 3
    pair_flops = 6 * heads * tokens * tokens * HEAD_SIZE

    def attend(name, distances, blocks, state, last):
        counts = tuple(len(block) for block in blocks)
        outs = [shape((tokens, width_q), bf16)] if last else state_shape
        return call(
            functools.partial(attend_kernel, counts, distances, state is None, last), name,
            outs + ([shape((8, HEAD_SIZE), f32)] if state is None else []),
            [SMEM] + [VMEM] * (2 + sum(counts) + (0 if state is None else 3)),
            len(counts) * pair_flops, 8 << 20, 16, [pltpu.VMEM((tokens, len(counts) * tokens), f32)],
        )(place, starts, query, *[array for block in blocks for array in block], *(state or ()))

    *state, done = attend("attend_own", ((0, 0),), [(kv,)], None, False)
    to_x, to_y = call(
        relay_kernel, "relay", [shape(kv.shape, bf16)] * 2, [SMEM] + [VMEM] * 3, 0, 2 << 20, 16,
    )(place, kv, from_z, done)
    from_x = sent(to_x, [(i, i ^ 1) for i in every])
    from_y = sent(to_y, [(i, i ^ 2) for i in every])
    state = attend("attend_z_diagonal", ((LAYER, LAYER), (1, 3)), [(from_z,), (from_d,)], state, False)
    (attended,) = attend("attend_x_y", ((3, 1), (2, 2)), [(from_x,), (from_y,)], state, True)

    columns = w_out.shape[1]
    cut = columns // 2
    parts = []
    for low, high in ((0, cut), (cut, columns)):
        own_part, send = call(
            functools.partial(out_kernel, low, high), "out_projection",
            [shape((half, high - low), f32), shape((half, high - low), bf16)],
            [SMEM] + [VMEM] * 2, 2 * tokens * width_q * (high - low), 2 * width_q * (high - low), 16,
        )(place, attended, w_out)
        parts.append((own_part, lax.ppermute(send, "head", SWAP)))
    (mixed,) = call(
        add_kernel, "add", [jax.ShapeDtypeStruct((half, columns), bf16)], [VMEM] * 4, half * columns, 4 << 20, 16,
    )(parts[0][0], parts[1][0], parts[0][1], parts[1][1])
    return mixed


def solution(mesh):
    in_specs = (
        P(("seq", "head"), None),
        P(),
        P(None, "head"),
        P(None, "head"),
        P(None, "head"),
        P("head", None),
    )
    out_specs = P(("seq", "head"), None)
    return jax.shard_map(body, mesh=mesh, in_specs=in_specs, out_specs=out_specs, check_vma=False)
```

```python
import functools
import math

import jax
import jax.numpy as jnp
from jax import lax
from jax.experimental import pallas as pl
from jax.experimental.pallas import tpu as pltpu
from jax.sharding import PartitionSpec as P

HEAD_SIZE = 128
LAYER = 4
MASKED = -1e30
SCORE_SCALE = math.log2(math.e) * HEAD_SIZE ** (-0.5)
SWAP = [(0, 1), (1, 0)]
VMEM = pl.BlockSpec(memory_space=pltpu.VMEM)
SMEM = pl.BlockSpec(memory_space=pltpu.SMEM)
ANY = pl.BlockSpec(memory_space=pl.ANY)


def inverse_frequency():
    table = []
    for number in range(HEAD_SIZE // 2):
        base_freq = 500000.0 ** (-(2.0 * number) / HEAD_SIZE)
        wavelength = 2.0 * math.pi / base_freq
        smooth = (8192.0 / wavelength - 1.0) / 3.0
        if wavelength < 2048.0:
            table.append(base_freq)
        elif wavelength > 8192.0:
            table.append(base_freq / 8.0)
        else:
            table.append((1.0 - smooth) * base_freq / 8.0 + smooth * base_freq)
    return table


def dot(a, b):
    return jnp.dot(a, b, preferred_element_type=jnp.float32)


def rotated(block, cosine, sine):
    return block * cosine + pltpu.roll(block, HEAD_SIZE // 2, 1) * sine


def first_keys_kernel(chunks, place, own_hbm, key_hbm, key_sum, own, w_key, cosine, sine, starts, sems):
    depth = w_key.shape[0] // chunks
    row_copy = pltpu.make_async_copy(own_hbm, own, sems.at[chunks])
    row_copy.start()
    copies = []
    for number in range(chunks):
        at = pl.ds(number * depth, depth)
        copies.append(pltpu.make_async_copy(key_hbm.at[at], w_key.at[at], sems.at[number]))
        copies[-1].start()
    tokens = cosine.shape[0]
    lane = lax.broadcasted_iota(jnp.int32, (1, HEAD_SIZE), 1)
    pair_of_lane = lane % (HEAD_SIZE // 2)
    freq = jnp.zeros((1, HEAD_SIZE), jnp.float32)
    for number, value in enumerate(inverse_frequency()):
        freq = jnp.where(pair_of_lane == number, jnp.float32(value), freq)
    positions = place[1] * tokens + lax.broadcasted_iota(jnp.int32, (tokens, HEAD_SIZE), 0)
    angles = positions.astype(jnp.float32) * freq
    cosine[...] = jnp.cos(angles)
    turned = jnp.sin(angles)
    sine[...] = jnp.where(lane < HEAD_SIZE // 2, -turned, turned)
    start = jnp.zeros((tokens, HEAD_SIZE), jnp.int32)
    end = jnp.int32(0)
    for number in range(2, place.shape[0]):
        end = end + place[number]
        start = jnp.where(positions >= end, end, start)
    starts[...] = start
    row_copy.wait()
    for number, copy in enumerate(copies):
        at = slice(number * depth, (number + 1) * depth)
        copy.wait()
        product = dot(own[:, at], w_key[at, :])
        key_sum[...] = product if number == 0 else key_sum[...] + product


def keys_kernel(place, other, w_key, key_own, cosine, sine, keys):
    half, width = key_own.shape
    mine = pl.multiple_of(place[0] * half, half)
    theirs = pl.multiple_of((1 - place[0]) * half, half)
    for rows, block in ((mine, key_own[...]), (theirs, dot(other[...], w_key[...]))):
        here = pl.ds(rows, half)
        for head in range(width // HEAD_SIZE):
            at = slice(head * HEAD_SIZE, (head + 1) * HEAD_SIZE)
            keys[here, at] = rotated(block[:, at], cosine[here, :], sine[here, :]).astype(keys.dtype)


def values_kernel(chunks, place, own, other, value_hbm, values, rows, done, w_value, total, sems):
    depth = value_hbm.shape[0] // chunks
    copies = []
    for number in range(chunks):
        at = pl.ds(number * depth, depth)
        copies.append(pltpu.make_async_copy(value_hbm.at[at], w_value.at[at], sems.at[number]))
        copies[-1].start()
    half = own.shape[0]
    rows[pl.ds(pl.multiple_of(place[0] * half, half), half), :] = own[...]
    rows[pl.ds(pl.multiple_of((1 - place[0]) * half, half), half), :] = other[...]
    done[...] = jnp.zeros_like(done)
    for number, copy in enumerate(copies):
        at = slice(number * depth, (number + 1) * depth)
        copy.wait()
        product = dot(rows[:, at], w_value[at, :])
        if number > 0:
            product = product + total[...]
        if number < chunks - 1:
            total[...] = product
        else:
            values[...] = product.astype(values.dtype)


def query_kernel(rows, weight, cosine, sine, after, query, done):
    done[...] = after[...]
    wide = 4 * HEAD_SIZE
    for number in range(weight.shape[1] // wide):
        result = dot(rows[...], weight[:, number * wide : (number + 1) * wide])
        for head in range(wide // HEAD_SIZE):
            at = slice(head * HEAD_SIZE, (head + 1) * HEAD_SIZE)
            out = slice(number * wide + head * HEAD_SIZE, number * wide + (head + 1) * HEAD_SIZE)
            query[:, out] = rotated(result[:, at], cosine[...], sine[...]).astype(query.dtype)


def relay_kernel(place, mine, from_z, after, to_x, to_y, to_d, *done):
    own, earlier = mine[...], from_z[...]
    upper_x, upper_y = place[1] % 2 > 0, place[1] % LAYER >= 2
    to_x[...] = jnp.where(upper_x, earlier, own)
    to_y[...] = jnp.where(upper_y, earlier, own)
    to_d[...] = jnp.where(upper_y, earlier, own)
    for flag in done:
        flag[...] = after[...]


def score_kernel(distances, near, place, starts, query, *refs):
    count = len(distances)
    keys, values = refs[:count], refs[count : count + near]
    weights_out, total, acc, bias = refs[count + near :]
    ones = jnp.ones((near * query.shape[0], HEAD_SIZE), query.dtype)
    tokens = query.shape[0]
    base = place[1] * tokens
    query_pos = base + lax.broadcasted_iota(jnp.int32, (tokens, tokens), 0)
    start = jnp.concatenate([starts[...]] * (tokens // starts.shape[1]), axis=1)
    for number, (even, odd) in enumerate(distances):
        first = base - tokens * jnp.where(place[1] % 2 > 0, odd, even)
        key_pos = first + lax.broadcasted_iota(jnp.int32, (tokens, tokens), 1)
        allowed = (key_pos >= start) & (key_pos <= query_pos)
        bias[:, number * tokens : (number + 1) * tokens] = jnp.where(allowed, 0.0, MASKED)
    group = query.shape[1] // keys[0].shape[1]
    for kv_head in range(keys[0].shape[1] // HEAD_SIZE):
        at = slice(kv_head * HEAD_SIZE, (kv_head + 1) * HEAD_SIZE)
        all_keys = jnp.concatenate([block[:, at] for block in keys], axis=0)
        near_values = jnp.concatenate([block[:, at] for block in values], axis=0)
        near_values = jnp.concatenate([near_values, ones], axis=1)
        for member in range(group):
            head = kv_head * group + member
            scores = lax.dot_general(
                query[:, head * HEAD_SIZE : (head + 1) * HEAD_SIZE], all_keys, (((1,), (1,)), ((), ())),
                preferred_element_type=jnp.float32,
            )
            scores = scores * SCORE_SCALE + bias[...]
            weights = jnp.exp2(scores - jnp.max(scores, axis=1, keepdims=True))
            weights = weights.astype(query.dtype)
            product = dot(weights[:, : near * tokens], near_values)
            acc[head], total[head] = product[:, :HEAD_SIZE], product[:, HEAD_SIZE:]
            weights_out[head] = weights[:, near * tokens :]


def mix_kernel(far, low, high, place, *refs):
    refs = list(refs)
    if far > 0:
        weights, total, acc = (refs.pop(0) for _ in range(3))
        blocks = [refs.pop(0) for _ in range(far)]
        weight, own, send, attended = refs
        group = weights.shape[0] * HEAD_SIZE // blocks[0].shape[1]
        for kv_head in range(blocks[0].shape[1] // HEAD_SIZE):
            values = jnp.concatenate([block[:, kv_head * HEAD_SIZE : (kv_head + 1) * HEAD_SIZE] for block in blocks], axis=0)
            values = jnp.concatenate([values, jnp.ones((values.shape[0], HEAD_SIZE), values.dtype)], axis=1)
            for head in range(kv_head * group, (kv_head + 1) * group):
                product = dot(weights[head], values)
                result = (acc[head] + product[:, :HEAD_SIZE]) / (total[head] + product[:, HEAD_SIZE:])
                attended[:, head * HEAD_SIZE : (head + 1) * HEAD_SIZE] = result.astype(attended.dtype)
    else:
        attended, weight, own, send = refs
    half = own.shape[0]
    on_high = place[0] > 0
    wide = 4 * HEAD_SIZE
    for number in range((high - low) // wide):
        at = slice(number * wide, (number + 1) * wide)
        result = dot(attended[...], weight[:, low + number * wide : low + (number + 1) * wide])
        own[:, at] = jnp.where(on_high, result[half:], result[:half])
        send[:, at] = jnp.where(on_high, result[:half], result[half:]).astype(send.dtype)


def add_kernel(own_low, own_high, got_low, got_high, mixed):
    cut = own_low.shape[1]
    for at, own, got in ((slice(0, cut), own_low, got_low), (slice(cut, mixed.shape[1]), own_high, got_high)):
        mixed[:, at] = (own[...] + got[...].astype(jnp.float32)).astype(mixed.dtype)


def call(kernel, name, outs, in_specs, flops, nbytes, limit, scratch=()):
    return pl.pallas_call(
        kernel,
        out_shape=outs,
        in_specs=in_specs,
        out_specs=[VMEM] * len(outs),
        scratch_shapes=list(scratch),
        name=name,
        cost_estimate=pl.CostEstimate(flops=flops, bytes_accessed=nbytes, transcendentals=0),
        compiler_params=pltpu.CompilerParams(vmem_limit_bytes=limit << 20),
    )


def in_hbm(array):
    return pltpu.with_memory_space_constraint(array, pltpu.HBM)


def body(input_rows, doc_lengths, w_query, key_weight, value_weight, w_out):
    half, model = input_rows.shape
    tokens = 2 * half
    width_q, width_k = w_query.shape[1], key_weight.shape[1]
    heads = width_q // HEAD_SIZE
    shards = lax.axis_size("seq")
    place = jnp.stack([lax.axis_index("head"), lax.axis_index("seq")]).astype(jnp.int32)
    place = jnp.concatenate([place, doc_lengths])
    bf16, f32 = jnp.bfloat16, jnp.float32
    shape = pltpu.VMEM

    other = lax.ppermute(input_rows, "head", SWAP)

    flag = shape((8, HEAD_SIZE), f32)
    table = shape((tokens, HEAD_SIZE), f32)
    kv_shape = shape((tokens, width_k), bf16)
    chunks = 8
    key_own, own, w_key, cosine, sine, starts = call(
        functools.partial(first_keys_kernel, chunks), "keys_own",
        [
            shape((half, width_k), f32), shape((half, model), bf16), shape(key_weight.shape, bf16),
            table, table, shape((tokens, HEAD_SIZE), jnp.int32),
        ],
        [SMEM, ANY, ANY], 2 * half * model * width_k, 2 * model * width_k, 4,
        [pltpu.SemaphoreType.DMA((chunks + 1,))],
    )(place, in_hbm(input_rows), in_hbm(key_weight))
    (keys,) = call(
        keys_kernel, "keys", [kv_shape], [SMEM] + [VMEM] * 5, 2 * half * model * width_k, 2 * model * width_k, 4,
    )(place, other, w_key, key_own, cosine, sine)

    every = range(shards)
    step_z = [(i, i + LAYER) for i in every if i + LAYER < shards]
    keys_z = lax.ppermute(keys, "seq", step_z)

    values, rows, done = call(
        functools.partial(values_kernel, chunks), "values", [kv_shape, shape((tokens, model), bf16), flag],
        [SMEM, VMEM, VMEM, ANY], 9 << 30, 2 * model * width_k, 10,
        [pltpu.VMEM(value_weight.shape, bf16), pltpu.VMEM((tokens, width_k), f32), pltpu.SemaphoreType.DMA((chunks,))],
    )(place, own, other, in_hbm(value_weight))
    values_z = lax.ppermute(values, "seq", step_z)

    def exchange(mine, from_z, after, flags, cost):
        *to, = call(
            relay_kernel, "relay", [kv_shape] * 3 + flags, [SMEM] + [VMEM] * 3, cost, 2 << 20, 4,
        )(place, mine, from_z, after)
        return [lax.ppermute(value, "seq", [(i, i ^ flip) for i in every]) for value, flip in zip(to, (1, 2, 3))], to[3:]

    keys_far, (done,) = exchange(keys, keys_z, done, [flag], 0)
    query, done = call(
        query_kernel, "queries", [shape((tokens, width_q), bf16), flag], [VMEM] * 5,
        2 * tokens * model * width_q, 2 * model * width_q, 8,
    )(rows, w_query, cosine, sine, done)
    values_far, _ = exchange(values, values_z, done, [], 9 << 30)

    far = len(keys_far)
    state = shape((heads, tokens, HEAD_SIZE), f32)
    weights, total, acc = call(
        functools.partial(score_kernel, ((0, 0), (LAYER, LAYER), (3, 1), (2, 2), (1, 3)), 2), "scores",
        [shape((heads, tokens, far * tokens), bf16), state, state], [SMEM] + [VMEM] * (4 + far + 2),
        14 * heads * tokens * tokens * HEAD_SIZE, 8 << 20, 12, [pltpu.VMEM((tokens, (far + 2) * tokens), f32)],
    )(place, starts, query, keys, keys_z, *keys_far, values, values_z)

    columns = w_out.shape[1]
    cut = columns // 2
    out_shape = [shape((half, cut), f32), shape((half, cut), bf16)]
    out_flops = 2 * tokens * width_q * cut
    own_low, send, attended = call(
        functools.partial(mix_kernel, far, 0, cut), "mix_low", out_shape + [shape((tokens, width_q), bf16)],
        [SMEM] + [VMEM] * (4 + far), out_flops + 2 * far * heads * tokens * tokens * HEAD_SIZE, 4 << 20, 6,
    )(place, weights, total, acc, *values_far, w_out)
    parts = [(own_low, lax.ppermute(send, "head", SWAP))]
    own_high, send = call(
        functools.partial(mix_kernel, 0, cut, columns), "mix_high", out_shape, [SMEM] + [VMEM] * 2, out_flops, 4 << 20, 6,
    )(place, attended, w_out)
    parts.append((own_high, lax.ppermute(send, "head", SWAP)))
    (mixed,) = call(
        add_kernel, "add", [jax.ShapeDtypeStruct((half, columns), bf16)], [VMEM] * 4, half * columns, 4 << 20, 16,
    )(parts[0][0], parts[1][0], parts[0][1], parts[1][1])
    return mixed


def solution(mesh):
    in_specs = (
        P(("seq", "head"), None),
        P(),
        P(None, "head"),
        P(None, "head"),
        P(None, "head"),
        P("head", None),
    )
    out_specs = P(("seq", "head"), None)
    return jax.shard_map(body, mesh=mesh, in_specs=in_specs, out_specs=out_specs, check_vma=False)
```

```python
import functools
import math

import jax
import jax.numpy as jnp
from jax import lax
from jax.experimental import pallas as pl
from jax.experimental.pallas import tpu as pltpu
from jax.sharding import PartitionSpec as P

HEAD_SIZE = 128
LAYER = 4
MASKED = -1e30
VALUES_COST = 4 << 30
RELAY_COST = 9 << 30
SCORE_SCALE = math.log2(math.e) * HEAD_SIZE ** (-0.5)
SWAP = [(0, 1), (1, 0)]
VMEM = pl.BlockSpec(memory_space=pltpu.VMEM)
ANY = pl.BlockSpec(memory_space=pl.ANY)


def inverse_frequency():
    table = []
    for number in range(HEAD_SIZE // 2):
        base_freq = 500000.0 ** (-(2.0 * number) / HEAD_SIZE)
        wavelength = 2.0 * math.pi / base_freq
        smooth = (8192.0 / wavelength - 1.0) / 3.0
        if wavelength < 2048.0:
            table.append(base_freq)
        elif wavelength > 8192.0:
            table.append(base_freq / 8.0)
        else:
            table.append((1.0 - smooth) * base_freq / 8.0 + smooth * base_freq)
    return table


def dot(a, b):
    return jnp.dot(a, b, preferred_element_type=jnp.float32)


def rotated(block, cosine, sine):
    return block * cosine + pltpu.roll(block, HEAD_SIZE // 2, 1) * sine


def first_keys_kernel(chunks, lengths_hbm, own_hbm, key_hbm, key_sum, own, w_key, cosine, sine, starts, lengths, sems):
    depth = w_key.shape[0] // chunks
    row_copy = pltpu.make_async_copy(own_hbm, own, sems.at[chunks])
    row_copy.start()
    copies = []
    for number in range(chunks):
        at = pl.ds(number * depth, depth)
        copies.append(pltpu.make_async_copy(key_hbm.at[at], w_key.at[at], sems.at[number]))
        copies[-1].start()
    tokens = cosine.shape[0]
    length_copy = pltpu.make_async_copy(lengths_hbm, lengths, sems.at[chunks + 1])
    length_copy.start()
    lane = lax.broadcasted_iota(jnp.int32, (1, HEAD_SIZE), 1)
    pair_of_lane = lane % (HEAD_SIZE // 2)
    freq = jnp.zeros((1, HEAD_SIZE), jnp.float32)
    for number, value in enumerate(inverse_frequency()):
        freq = jnp.where(pair_of_lane == number, jnp.float32(value), freq)
    positions = lax.axis_index("seq") * tokens + lax.broadcasted_iota(jnp.int32, (tokens, HEAD_SIZE), 0)
    angles = positions.astype(jnp.float32) * freq
    cosine[...] = jnp.cos(angles)
    turned = jnp.sin(angles)
    sine[...] = jnp.where(lane < HEAD_SIZE // 2, -turned, turned)
    length_copy.wait()
    start = jnp.zeros((tokens, HEAD_SIZE), jnp.int32)
    end = jnp.int32(0)
    for number in range(lengths.shape[0]):
        end = end + lengths[number]
        start = jnp.where(positions >= end, end, start)
    starts[...] = start
    row_copy.wait()
    for number, copy in enumerate(copies):
        at = slice(number * depth, (number + 1) * depth)
        copy.wait()
        product = dot(own[:, at], w_key[at, :])
        key_sum[...] = product if number == 0 else key_sum[...] + product


def halves(half):
    core = lax.axis_index("head")
    return pl.ds(pl.multiple_of(core * half, half), half), pl.ds(pl.multiple_of((1 - core) * half, half), half)


def keys_kernel(other, w_key, key_own, cosine, sine, keys):
    half, width = key_own.shape
    mine, theirs = halves(half)
    for here, block in ((mine, key_own[...]), (theirs, dot(other[...], w_key[...]))):
        for head in range(width // HEAD_SIZE):
            at = slice(head * HEAD_SIZE, (head + 1) * HEAD_SIZE)
            keys[here, at] = rotated(block[:, at], cosine[here, :], sine[here, :]).astype(keys.dtype)


def values_kernel(chunks, own, other, value_hbm, values, rows, done, w_value, total, sems):
    depth = w_value.shape[0] // chunks
    copies = []
    for number in range(chunks):
        at = pl.ds(number * depth, depth)
        copies.append(pltpu.make_async_copy(value_hbm.at[at], w_value.at[at], sems.at[number]))
        copies[-1].start()
    mine, theirs = halves(own.shape[0])
    rows[mine, :] = own[...]
    rows[theirs, :] = other[...]
    done[...] = jnp.zeros_like(done)
    for number, copy in enumerate(copies):
        at = slice(number * depth, (number + 1) * depth)
        copy.wait()
        product = dot(rows[:, at], w_value[at, :])
        if number > 0:
            product = product + total[...]
        if number < chunks - 1:
            total[...] = product
        else:
            values[...] = product.astype(values.dtype)


def query_kernel(rows, weight, cosine, sine, after, query, done):
    del after
    done[...] = jnp.zeros_like(done)
    wide = 4 * HEAD_SIZE
    for number in range(weight.shape[1] // wide):
        result = dot(rows[...], weight[:, number * wide : (number + 1) * wide])
        for head in range(wide // HEAD_SIZE):
            at = slice(head * HEAD_SIZE, (head + 1) * HEAD_SIZE)
            out = slice(number * wide + head * HEAD_SIZE, number * wide + (head + 1) * HEAD_SIZE)
            query[:, out] = rotated(result[:, at], cosine[...], sine[...]).astype(query.dtype)


def relay_kernel(plan, own, earlier, *refs):
    index = lax.axis_index("seq")
    outs = refs[len(refs) - len(plan) :]
    for (way, low), out in zip(plan, outs):
        upper = index % 2 > 0 if way == 1 else index % LAYER >= 2
        at = slice(low, low + out.shape[1])
        out[...] = jnp.where(upper, earlier[:, at], own[:, at])


def score_kernel(distances, near, starts, query, *refs):
    count = len(distances)
    keys, refs = refs[:count], refs[count:]
    values, refs = refs[:near], refs[near:]
    weights_a, total_a, acc_a, weights_b, total_b, acc_b, bias = refs
    tokens = query.shape[0]
    index = lax.axis_index("seq")
    base = index * tokens
    query_pos = base + lax.broadcasted_iota(jnp.int32, (tokens, tokens), 0)
    start = jnp.concatenate([starts[...]] * (tokens // starts.shape[1]), axis=1)
    blocks = [slice(number * tokens, (number + 1) * tokens) for number in range(count)]
    for block, (even, odd) in zip(blocks, distances):
        first = base - tokens * jnp.where(index % 2 > 0, odd, even)
        key_pos = first + lax.broadcasted_iota(jnp.int32, (tokens, tokens), 1)
        allowed = (key_pos >= start) & (key_pos <= query_pos)
        bias[:, block] = jnp.where(allowed, 0.0, MASKED)
    heads = query.shape[1] // HEAD_SIZE
    kv_heads = keys[0].shape[1] // HEAD_SIZE
    group = heads // kv_heads
    ones = jnp.ones((tokens, HEAD_SIZE), query.dtype)

    def column(number):
        return slice(number * HEAD_SIZE, (number + 1) * HEAD_SIZE)

    def scores_of(head):
        return [
            lax.dot_general(
                query[:, column(head)], key[:, column(head // group)], (((1,), (1,)), ((), ())),
                preferred_element_type=jnp.float32,
            )
            * SCORE_SCALE
            + bias[:, block]
            for key, block in zip(keys, blocks)
        ]

    scores = scores_of(0)
    for head in range(heads):
        ahead = scores_of(head + 1) if head + 1 < heads else None
        top = jnp.max(functools.reduce(jnp.maximum, scores), axis=1, keepdims=True)
        weights = [jnp.exp2(score - top).astype(query.dtype) for score in scores]
        late = head >= heads // 2
        at = head - heads // 2 if late else head
        product = None
        for number, block in enumerate(values):
            term = dot(weights[number], jnp.concatenate([block[:, column(head // group)], ones], axis=1))
            product = term if product is None else product + term
        weights_out, total, acc = (weights_b, total_b, acc_b) if late else (weights_a, total_a, acc_a)
        acc[at], total[at] = product[:, :HEAD_SIZE], product[:, HEAD_SIZE:]
        for number in range(near, count):
            weights_out[at, :, blocks[number - near]] = weights[number]
        scores = ahead


def attend_far(second, weights, total, acc, blocks, attended):
    heads = weights.shape[0]
    kv_heads = min(block.shape[1] for block in blocks) // HEAD_SIZE
    group = heads // kv_heads
    for kv_head in range(kv_heads):
        pieces = []
        for block in blocks:
            low = (kv_head + (kv_heads if second and block.shape[1] > kv_heads * HEAD_SIZE else 0)) * HEAD_SIZE
            pieces.append(block[:, low : low + HEAD_SIZE])
        values = jnp.concatenate(pieces, axis=0)
        values = jnp.concatenate([values, jnp.ones((values.shape[0], HEAD_SIZE), values.dtype)], axis=1)
        for head in range(kv_head * group, (kv_head + 1) * group):
            product = dot(weights[head], values)
            result = (acc[head] + product[:, :HEAD_SIZE]) / (total[head] + product[:, HEAD_SIZE:])
            attended[:, head * HEAD_SIZE : (head + 1) * HEAD_SIZE] = result.astype(attended.dtype)


WIDE = 4 * HEAD_SIZE


def mix_first_kernel(far, weights, total, acc, *refs):
    blocks, (weight, summed, attended) = refs[:far], refs[far:]
    attend_far(False, weights, total, acc, blocks, attended)
    depth = attended.shape[1]
    for number in range(summed.shape[1] // WIDE):
        at = slice(number * WIDE, (number + 1) * WIDE)
        summed[:, at] = dot(attended[...], weight[:depth, at])


def split_rows(result, own, send, at):
    half = own.shape[0]
    on_high = lax.axis_index("head") > 0
    own[:, at] = jnp.where(on_high, result[half:], result[:half])
    send[:, at] = jnp.where(on_high, result[:half], result[half:]).astype(send.dtype)


def mix_columns(attended, weight, summed, low, own, send):
    depth = attended.shape[1]
    for number in range(own.shape[1] // WIDE):
        here = slice(low + number * WIDE, low + (number + 1) * WIDE)
        result = summed[:, here] + dot(attended[...], weight[depth:, here])
        split_rows(result, own, send, slice(number * WIDE, (number + 1) * WIDE))


def mix_second_kernel(far, weights, total, acc, *refs):
    blocks, (weight, summed, own, send, attended) = refs[:far], refs[far:]
    attend_far(True, weights, total, acc, blocks, attended)
    mix_columns(attended, weight, summed, 0, own, send)


def mix_more_kernel(low, attended, weight, summed, own, send):
    mix_columns(attended, weight, summed, low, own, send)


def mix_last_kernel(low, attended, weight, summed, got_low, own, send):
    del got_low
    mix_columns(attended, weight, summed, low, own, send)


def add_low_kernel(own, got, mixed_hbm, mixed, sem):
    mixed[...] = (own[...] + got[...].astype(jnp.float32)).astype(mixed.dtype)
    copy = pltpu.make_async_copy(mixed, mixed_hbm.at[:, pl.ds(0, mixed.shape[1])], sem)
    copy.start()
    copy.wait()


def add_kernel(own_one, own_two, got_one, got_two, mixed_in, mixed_hbm, mixed, sems):
    del mixed_in
    width = own_one.shape[1]
    low = mixed_hbm.shape[1] - 2 * width
    copies = []
    for number, (own, got) in enumerate(((own_one, got_one), (own_two, got_two))):
        at = pl.ds(number * width, width)
        mixed[:, at] = (own[...] + got[...].astype(jnp.float32)).astype(mixed.dtype)
        copies.append(pltpu.make_async_copy(mixed.at[:, at], mixed_hbm.at[:, pl.ds(low + number * width, width)], sems.at[number]))
        copies[-1].start()
    for copy in copies:
        copy.wait()


def call(kernel, name, outs, in_specs, flops, nbytes, limit, scratch=(), out_specs=None, aliases=None):
    return pl.pallas_call(
        kernel,
        out_shape=outs,
        in_specs=in_specs,
        out_specs=out_specs or [VMEM] * len(outs),
        scratch_shapes=list(scratch),
        input_output_aliases=aliases or {},
        name=name,
        cost_estimate=pl.CostEstimate(flops=flops, bytes_accessed=nbytes, transcendentals=0),
        compiler_params=pltpu.CompilerParams(vmem_limit_bytes=limit << 20),
    )


def in_hbm(array):
    return pltpu.with_memory_space_constraint(array, pltpu.HBM)


def body(input_rows, doc_lengths, w_query, key_weight, value_weight, w_out):
    half, model = input_rows.shape
    tokens = 2 * half
    width_q, width_k = w_query.shape[1], key_weight.shape[1]
    heads = width_q // HEAD_SIZE
    shards = lax.axis_size("seq")
    bf16, f32 = jnp.bfloat16, jnp.float32
    shape = pltpu.VMEM

    other = lax.ppermute(input_rows, "head", SWAP)

    flag = shape((8, HEAD_SIZE), f32)
    table = shape((tokens, HEAD_SIZE), f32)
    kv_shape = shape((tokens, width_k), bf16)
    chunks = 8
    key_own, own, w_key, cosine, sine, starts = call(
        functools.partial(first_keys_kernel, chunks), "keys_own",
        [
            shape((half, width_k), f32), shape((half, model), bf16), shape(key_weight.shape, bf16),
            table, table, shape((tokens, HEAD_SIZE), jnp.int32),
        ],
        [ANY, ANY, ANY], 2 * half * model * width_k, 2 * model * width_k, 4,
        [pltpu.SMEM(doc_lengths.shape, jnp.int32), pltpu.SemaphoreType.DMA((chunks + 2,))],
    )(in_hbm(doc_lengths), in_hbm(input_rows), in_hbm(key_weight))
    (keys,) = call(
        keys_kernel, "keys", [kv_shape], [VMEM] * 5, 2 * half * model * width_k, 2 * model * width_k, 4,
    )(other, w_key, key_own, cosine, sine)

    every = range(shards)
    step_z = [(i, i + LAYER) for i in every if i + LAYER < shards]
    keys_z = lax.ppermute(keys, "seq", step_z)

    values, rows, done = call(
        functools.partial(values_kernel, 4), "values", [kv_shape, shape((tokens, model), bf16), flag], [VMEM, VMEM, ANY],
        VALUES_COST, 2 * model * width_k, 10,
        [pltpu.VMEM(value_weight.shape, bf16), pltpu.VMEM((tokens, width_k), f32), pltpu.SemaphoreType.DMA((4,))],
    )(own, other, in_hbm(value_weight))
    values_z = lax.ppermute(values, "seq", step_z)

    def exchange(mine, earlier, plan, wides, after, cost):
        to = call(
            functools.partial(relay_kernel, plan), "relay", [shape((tokens, wide), bf16) for wide in wides],
            [VMEM] * (2 + len(after)), cost, 2 << 20, 4,
        )(mine, earlier, *after)
        return [lax.ppermute(array, "seq", [(i, i ^ way) for i in every]) for (way, _), array in zip(plan, to)], to[0]

    part = width_k // 2
    keys_far, sent_first = exchange(keys, keys_z, ((1, 0), (2, 0), (3, 0)), [width_k] * 3, [done], RELAY_COST)
    query, done = call(
        query_kernel, "queries", [shape((tokens, width_q), bf16), flag], [VMEM] * 5,
        2 * tokens * model * width_q, 2 * model * width_q, 8,
    )(rows, w_query, cosine, sine, sent_first)
    (values_d, values_x, values_y), _ = exchange(
        values, values_z, ((3, 0), (1, 0), (2, 0)), [width_k, part, part], [done], 9 << 30
    )
    (values_x_more, values_y_more), _ = exchange(values, values_z, ((1, part), (2, part)), [part] * 2, keys_far, 0)
    far_a, far_b = (values_x, values_y, values_d), (values_x_more, values_y_more, values_d)

    far = len(keys_far)
    heads_half = heads // 2
    state = [shape((heads_half, tokens, far * tokens), bf16)] + [shape((heads_half, tokens, HEAD_SIZE), f32)] * 2
    *state_a, weights_b, total_b, acc_b = call(
        functools.partial(score_kernel, ((0, 0), (LAYER, LAYER), (3, 1), (2, 2), (1, 3)), 2), "scores",
        state * 2, [VMEM] * (2 + 2 + far + 2),
        14 * heads * tokens * tokens * HEAD_SIZE, 8 << 20, 16, [pltpu.VMEM((tokens, (far + 2) * tokens), f32)],
    )(starts, query, keys, keys_z, *keys_far, values, values_z)

    columns = w_out.shape[1]
    attended_shape = shape((tokens, width_q // 2), bf16)
    far_flops = far * heads * tokens * tokens * HEAD_SIZE
    out_flops = tokens * width_q * columns
    summed, _ = call(
        functools.partial(mix_first_kernel, far), "mix_first", [shape((tokens, columns), f32), attended_shape],
        [VMEM] * (4 + far), out_flops + far_flops, 4 << 20, 6,
    )(*state_a, *far_a, w_out)

    def out_shapes(wide):
        return [shape((half, wide), f32), shape((half, wide), bf16)]

    cut, wide = columns // 2, columns // 4
    own_low, send, attended = call(
        functools.partial(mix_second_kernel, far), "mix_second", out_shapes(cut) + [attended_shape],
        [VMEM] * (5 + far), out_flops // 2 + far_flops, 4 << 20, 6,
    )(weights_b, total_b, acc_b, *far_b, w_out, summed)
    got_low = lax.ppermute(send, "head", SWAP)
    own_one, send = call(
        functools.partial(mix_more_kernel, cut), "mix_more", out_shapes(wide), [VMEM] * 3, out_flops // 4, 4 << 20, 6,
    )(attended, w_out, summed)
    got_one = lax.ppermute(send, "head", SWAP)
    own_two, send = call(
        functools.partial(mix_last_kernel, cut + wide), "mix_last", out_shapes(wide), [VMEM] * 4, out_flops // 4, 4 << 20, 6,
    )(attended, w_out, summed, got_low)
    got_two = lax.ppermute(send, "head", SWAP)
    (mixed,) = call(
        add_low_kernel, "add_low", [pltpu.HBM((half, columns), bf16)], [VMEM] * 2, half * cut, 2 << 20, 4,
        [pltpu.VMEM((half, cut), bf16), pltpu.SemaphoreType.DMA(())], [ANY],
    )(own_low, got_low)
    (mixed,) = call(
        add_kernel, "add", [pltpu.HBM((half, columns), bf16)], [VMEM] * 4 + [ANY], half * columns, 4 << 20, 4,
        [pltpu.VMEM((half, 2 * wide), bf16), pltpu.SemaphoreType.DMA((2,))], [ANY], {4: 0},
    )(own_one, own_two, got_one, got_two, mixed)
    return mixed


def solution(mesh):
    in_specs = (
        P(("seq", "head"), None),
        P(),
        P(None, "head"),
        P(None, "head"),
        P(None, "head"),
        P("head", None),
    )
    out_specs = P(("seq", "head"), None)
    return jax.shard_map(body, mesh=mesh, in_specs=in_specs, out_specs=out_specs, check_vma=False)
```

```python
import functools
import math

import jax
import jax.numpy as jnp
from jax import lax
from jax.experimental import pallas as pl
from jax.experimental.pallas import tpu as pltpu
from jax.sharding import PartitionSpec as P

HEAD_SIZE = 128
LAYER = 4
MASKED = -1e30
VALUES_COST = 4 << 30
RELAY_COST = 9 << 30
SCORE_SCALE = math.log2(math.e) * HEAD_SIZE ** (-0.5)
SWAP = [(0, 1), (1, 0)]
VMEM = pl.BlockSpec(memory_space=pltpu.VMEM)
ANY = pl.BlockSpec(memory_space=pl.ANY)


def inverse_frequency():
    table = []
    for number in range(HEAD_SIZE // 2):
        base_freq = 500000.0 ** (-(2.0 * number) / HEAD_SIZE)
        wavelength = 2.0 * math.pi / base_freq
        smooth = (8192.0 / wavelength - 1.0) / 3.0
        if wavelength < 2048.0:
            table.append(base_freq)
        elif wavelength > 8192.0:
            table.append(base_freq / 8.0)
        else:
            table.append((1.0 - smooth) * base_freq / 8.0 + smooth * base_freq)
    return table


def dot(a, b):
    return jnp.dot(a, b, preferred_element_type=jnp.float32)


def rotated(block, cosine, sine):
    return block * cosine + pltpu.roll(block, HEAD_SIZE // 2, 1) * sine


def first_keys_kernel(chunks, lengths_hbm, own_hbm, key_hbm, key_sum, own, w_key, cosine, sine, starts, lengths, sems):
    depth = w_key.shape[0] // chunks
    row_copy = pltpu.make_async_copy(own_hbm, own, sems.at[chunks])
    row_copy.start()
    copies = []
    for number in range(chunks):
        at = pl.ds(number * depth, depth)
        copies.append(pltpu.make_async_copy(key_hbm.at[at], w_key.at[at], sems.at[number]))
        copies[-1].start()
    tokens = cosine.shape[0]
    length_copy = pltpu.make_async_copy(lengths_hbm, lengths, sems.at[chunks + 1])
    length_copy.start()
    lane = lax.broadcasted_iota(jnp.int32, (1, HEAD_SIZE), 1)
    pair_of_lane = lane % (HEAD_SIZE // 2)
    freq = jnp.zeros((1, HEAD_SIZE), jnp.float32)
    for number, value in enumerate(inverse_frequency()):
        freq = jnp.where(pair_of_lane == number, jnp.float32(value), freq)
    first = lax.axis_index("seq") * tokens
    half = tokens // 2
    low_lane = lane < HEAD_SIZE // 2
    packed = first + lax.broadcasted_iota(jnp.int32, (half, HEAD_SIZE), 0) + jnp.where(low_lane, 0, half)
    angles = packed.astype(jnp.float32) * freq
    turned = jnp.cos(angles)
    other = pltpu.roll(turned, HEAD_SIZE // 2, 1)
    cosine[:half, :] = jnp.where(low_lane, turned, other)
    cosine[half:, :] = jnp.where(low_lane, other, turned)
    turned = jnp.sin(angles)
    other = pltpu.roll(turned, HEAD_SIZE // 2, 1)
    sine[:half, :] = jnp.where(low_lane, -turned, other)
    sine[half:, :] = jnp.where(low_lane, -other, turned)
    positions = first + lax.broadcasted_iota(jnp.int32, (tokens, HEAD_SIZE), 0)
    length_copy.wait()
    start = jnp.zeros((tokens, HEAD_SIZE), jnp.int32)
    end = jnp.int32(0)
    for number in range(lengths.shape[0]):
        end = end + lengths[number]
        start = jnp.where(positions >= end, end, start)
    starts[...] = start
    row_copy.wait()
    for number, copy in enumerate(copies):
        at = slice(number * depth, (number + 1) * depth)
        copy.wait()
        product = dot(own[:, at], w_key[at, :])
        key_sum[...] = product if number == 0 else key_sum[...] + product


def halves(half):
    core = lax.axis_index("head")
    return pl.ds(pl.multiple_of(core * half, half), half), pl.ds(pl.multiple_of((1 - core) * half, half), half)


def keys_kernel(other, w_key, key_own, cosine, sine, keys):
    half, width = key_own.shape
    mine, theirs = halves(half)
    for here, block in ((mine, key_own[...]), (theirs, dot(other[...], w_key[...]))):
        for head in range(width // HEAD_SIZE):
            at = slice(head * HEAD_SIZE, (head + 1) * HEAD_SIZE)
            keys[here, at] = rotated(block[:, at], cosine[here, :], sine[here, :]).astype(keys.dtype)


def values_kernel(chunks, own, other, value_hbm, values, rows, done, w_value, total, sems):
    depth = w_value.shape[0] // chunks
    copies = []
    for number in range(chunks):
        at = pl.ds(number * depth, depth)
        copies.append(pltpu.make_async_copy(value_hbm.at[at], w_value.at[at], sems.at[number]))
        copies[-1].start()
    mine, theirs = halves(own.shape[0])
    rows[mine, :] = own[...]
    rows[theirs, :] = other[...]
    done[...] = jnp.zeros_like(done)
    for number, copy in enumerate(copies):
        at = slice(number * depth, (number + 1) * depth)
        copy.wait()
        product = dot(rows[:, at], w_value[at, :])
        if number > 0:
            product = product + total[...]
        if number < chunks - 1:
            total[...] = product
        else:
            values[...] = product.astype(values.dtype)


def query_kernel(rows, weight, cosine, sine, after, query, done):
    del after
    done[...] = jnp.zeros_like(done)
    wide = 4 * HEAD_SIZE
    for number in range(weight.shape[1] // wide):
        result = dot(rows[...], weight[:, number * wide : (number + 1) * wide])
        for head in range(wide // HEAD_SIZE):
            at = slice(head * HEAD_SIZE, (head + 1) * HEAD_SIZE)
            out = slice(number * wide + head * HEAD_SIZE, number * wide + (head + 1) * HEAD_SIZE)
            query[:, out] = rotated(result[:, at], cosine[...], sine[...]).astype(query.dtype)


def relay_kernel(plan, own, earlier, *refs):
    index = lax.axis_index("seq")
    outs = refs[len(refs) - len(plan) :]
    for (way, low), out in zip(plan, outs):
        upper = index % 2 > 0 if way == 1 else index % LAYER >= 2
        at = slice(low, low + out.shape[1])
        out[...] = jnp.where(upper, earlier[:, at], own[:, at])


def column(number):
    return slice(number * HEAD_SIZE, (number + 1) * HEAD_SIZE)


def fill_bias(bias, distances, starts):
    tokens = bias.shape[0]
    index = lax.axis_index("seq")
    base = index * tokens
    query_pos = base + lax.broadcasted_iota(jnp.int32, (tokens, tokens), 0)
    start = jnp.concatenate([starts[...]] * (tokens // starts.shape[1]), axis=1)
    for number, (even, odd) in enumerate(distances):
        first = base - tokens * jnp.where(index % 2 > 0, odd, even)
        key_pos = first + lax.broadcasted_iota(jnp.int32, (tokens, tokens), 1)
        allowed = (key_pos >= start) & (key_pos <= query_pos)
        bias[:, number * tokens : (number + 1) * tokens] = jnp.where(allowed, 0.0, MASKED)


def scores_of(query, keys, bias, head, group):
    tokens = bias.shape[0]
    return [
        lax.dot_general(
            query[:, column(head)], key[:, column(head // group)], (((1,), (1,)), ((), ())),
            preferred_element_type=jnp.float32,
        )
        * SCORE_SCALE
        + bias[:, number * tokens : (number + 1) * tokens]
        for number, key in enumerate(keys)
    ]


def near_kernel(distances, starts, query, *refs):
    count = len(distances)
    keys, values, (tops, totals, accs, bias) = refs[:count], refs[count : 2 * count], refs[2 * count :]
    fill_bias(bias, distances, starts)
    tokens = query.shape[0]
    heads = query.shape[1] // HEAD_SIZE
    group = heads * HEAD_SIZE // keys[0].shape[1]
    ones = jnp.ones((tokens, HEAD_SIZE), query.dtype)
    scores = scores_of(query, keys, bias, 0, group)
    for head in range(heads):
        ahead = scores_of(query, keys, bias, head + 1, group) if head + 1 < heads else None
        top = jnp.max(functools.reduce(jnp.maximum, scores), axis=1, keepdims=True)
        product = None
        for score, block in zip(scores, values):
            weights = jnp.exp2(score - top).astype(query.dtype)
            term = dot(weights, jnp.concatenate([block[:, column(head // group)], ones], axis=1))
            product = term if product is None else product + term
        tops[head] = jnp.broadcast_to(top, (tokens, HEAD_SIZE))
        accs[head], totals[head] = product[:, :HEAD_SIZE], product[:, HEAD_SIZE:]
        scores = ahead


def far_kernel(distances, starts, query, *refs):
    count = len(distances)
    keys, (tops, totals, accs) = refs[:count], refs[count : count + 3]
    outs = (refs[count + 3 : count + 6], refs[count + 6 : count + 9])
    bias = refs[-1]
    fill_bias(bias, distances, starts)
    tokens = query.shape[0]
    heads = query.shape[1] // HEAD_SIZE
    group = heads * HEAD_SIZE // keys[0].shape[1]
    scores = scores_of(query, keys, bias, 0, group)
    for head in range(heads):
        ahead = scores_of(query, keys, bias, head + 1, group) if head + 1 < heads else None
        top = jnp.max(functools.reduce(jnp.maximum, scores), axis=1, keepdims=True)
        before = tops[head]
        top = jnp.maximum(jnp.broadcast_to(top, (tokens, HEAD_SIZE)), before)
        factor = jnp.exp2(before - top)
        wide_top = jnp.concatenate([top] * (tokens // HEAD_SIZE), axis=1)
        weights_out, total, acc = outs[2 * head // heads]
        at = head % (heads // 2)
        acc[at], total[at] = accs[head] * factor, totals[head] * factor
        for number, score in enumerate(scores):
            weights_out[at, :, number * tokens : (number + 1) * tokens] = jnp.exp2(score - wide_top).astype(query.dtype)
        scores = ahead


def attend_far(second, weights, total, acc, blocks, attended):
    heads = weights.shape[0]
    kv_heads = min(block.shape[1] for block in blocks) // HEAD_SIZE
    group = heads // kv_heads
    for kv_head in range(kv_heads):
        pieces = []
        for block in blocks:
            low = (kv_head + (kv_heads if second and block.shape[1] > kv_heads * HEAD_SIZE else 0)) * HEAD_SIZE
            pieces.append(block[:, low : low + HEAD_SIZE])
        values = jnp.concatenate(pieces, axis=0)
        values = jnp.concatenate([values, jnp.ones((values.shape[0], HEAD_SIZE), values.dtype)], axis=1)
        for head in range(kv_head * group, (kv_head + 1) * group):
            product = dot(weights[head], values)
            result = (acc[head] + product[:, :HEAD_SIZE]) / (total[head] + product[:, HEAD_SIZE:])
            attended[:, head * HEAD_SIZE : (head + 1) * HEAD_SIZE] = result.astype(attended.dtype)


WIDE = 4 * HEAD_SIZE


def mix_first_kernel(far, weights, total, acc, *refs):
    blocks, (weight, summed, attended) = refs[:far], refs[far:]
    attend_far(False, weights, total, acc, blocks, attended)
    depth = attended.shape[1]
    for number in range(summed.shape[1] // WIDE):
        at = slice(number * WIDE, (number + 1) * WIDE)
        summed[:, at] = dot(attended[...], weight[:depth, at])


def rows_product(rows, low, attended, weight, summed, wide):
    depth = attended.shape[1]
    at = slice(low, low + wide)
    return summed[rows, at] + dot(attended[rows, :], weight[depth:, at])


def send_columns(low, attended, weight, summed, send):
    theirs = halves(send.shape[0])[1]
    for number in range(send.shape[1] // WIDE):
        result = rows_product(theirs, low + number * WIDE, attended, weight, summed, WIDE)
        send[:, number * WIDE : (number + 1) * WIDE] = result.astype(send.dtype)


def mix_second_kernel(far, weights, total, acc, *refs):
    blocks, (weight, summed, send, attended) = refs[:far], refs[far:]
    attend_far(True, weights, total, acc, blocks, attended)
    send_columns(0, attended, weight, summed, send)


def own_high_kernel(low, attended, weight, summed, own):
    mine = halves(own.shape[0])[0]
    for number in range(own.shape[1] // WIDE):
        result = rows_product(mine, low + number * WIDE, attended, weight, summed, WIDE)
        own[:, number * WIDE : (number + 1) * WIDE] = result


def own_low_kernel(attended, weight, summed, got, after, mixed_hbm, mixed, sems):
    del after
    mine = halves(got.shape[0])[0]
    copies = []
    for number in range(got.shape[1] // WIDE):
        at = slice(number * WIDE, (number + 1) * WIDE)
        result = rows_product(mine, number * WIDE, attended, weight, summed, WIDE)
        mixed[:, at] = (result + got[:, at].astype(jnp.float32)).astype(mixed.dtype)
        there = mixed_hbm.at[:, pl.ds(number * WIDE, WIDE)]
        copies.append(pltpu.make_async_copy(mixed.at[:, pl.ds(number * WIDE, WIDE)], there, sems.at[number]))
        copies[-1].start()
    for copy in copies:
        copy.wait()


def add_kernel(own, got, mixed_in, mixed_hbm, mixed, sems):
    del mixed_in
    width = own.shape[1]
    low = mixed_hbm.shape[1] - width
    copies = []
    for number in range(width // WIDE):
        at = slice(number * WIDE, (number + 1) * WIDE)
        mixed[:, at] = (own[:, at] + got[:, at].astype(jnp.float32)).astype(mixed.dtype)
        there = mixed_hbm.at[:, pl.ds(low + number * WIDE, WIDE)]
        copies.append(pltpu.make_async_copy(mixed.at[:, pl.ds(number * WIDE, WIDE)], there, sems.at[number]))
        copies[-1].start()
    for copy in copies:
        copy.wait()


def call(kernel, name, outs, in_specs, flops, nbytes, limit, scratch=(), out_specs=None, aliases=None):
    return pl.pallas_call(
        kernel,
        out_shape=outs,
        in_specs=in_specs,
        out_specs=out_specs or [VMEM] * len(outs),
        scratch_shapes=list(scratch),
        input_output_aliases=aliases or {},
        name=name,
        cost_estimate=pl.CostEstimate(flops=flops, bytes_accessed=nbytes, transcendentals=0),
        compiler_params=pltpu.CompilerParams(vmem_limit_bytes=limit << 20),
    )


def in_hbm(array):
    return pltpu.with_memory_space_constraint(array, pltpu.HBM)


def body(input_rows, doc_lengths, w_query, key_weight, value_weight, w_out):
    half, model = input_rows.shape
    tokens = 2 * half
    width_q, width_k = w_query.shape[1], key_weight.shape[1]
    heads = width_q // HEAD_SIZE
    shards = lax.axis_size("seq")
    bf16, f32 = jnp.bfloat16, jnp.float32
    shape = pltpu.VMEM

    other = lax.ppermute(input_rows, "head", SWAP)

    flag = shape((8, HEAD_SIZE), f32)
    table = shape((tokens, HEAD_SIZE), f32)
    kv_shape = shape((tokens, width_k), bf16)
    chunks = 8
    key_own, own, w_key, cosine, sine, starts = call(
        functools.partial(first_keys_kernel, chunks), "keys_own",
        [
            shape((half, width_k), f32), shape((half, model), bf16), shape(key_weight.shape, bf16),
            table, table, shape((tokens, HEAD_SIZE), jnp.int32),
        ],
        [ANY, ANY, ANY], 2 * half * model * width_k, 2 * model * width_k, 4,
        [pltpu.SMEM(doc_lengths.shape, jnp.int32), pltpu.SemaphoreType.DMA((chunks + 2,))],
    )(in_hbm(doc_lengths), in_hbm(input_rows), in_hbm(key_weight))
    (keys,) = call(
        keys_kernel, "keys", [kv_shape], [VMEM] * 5, 2 * half * model * width_k, 2 * model * width_k, 4,
    )(other, w_key, key_own, cosine, sine)

    every = range(shards)
    step_z = [(i, (i + LAYER) % shards) for i in every]
    keys_z = lax.ppermute(keys, "seq", [(a, b) for a, b in step_z if a < b])

    values, rows, done = call(
        functools.partial(values_kernel, 4), "values", [kv_shape, shape((tokens, model), bf16), flag], [VMEM, VMEM, ANY],
        VALUES_COST, 2 * model * width_k, 10,
        [pltpu.VMEM(value_weight.shape, bf16), pltpu.VMEM((tokens, width_k), f32), pltpu.SemaphoreType.DMA((4,))],
    )(own, other, in_hbm(value_weight))
    values_z = lax.ppermute(values, "seq", step_z)

    def exchange(mine, earlier, plan, wides, after, cost):
        to = call(
            functools.partial(relay_kernel, plan), "relay", [shape((tokens, wide), bf16) for wide in wides],
            [VMEM] * (2 + len(after)), cost, 2 << 20, 4,
        )(mine, earlier, *after)
        return [lax.ppermute(array, "seq", [(i, i ^ way) for i in every]) for (way, _), array in zip(plan, to)], to[0]

    part = width_k // 2
    keys_far, sent_first = exchange(keys, keys_z, ((1, 0), (2, 0), (3, 0)), [width_k] * 3, [done], RELAY_COST)
    query, done = call(
        query_kernel, "queries", [shape((tokens, width_q), bf16), flag], [VMEM] * 5,
        2 * tokens * model * width_q, 2 * model * width_q, 8,
    )(rows, w_query, cosine, sine, sent_first)
    far = len(keys_far)
    heads_half = heads // 2
    state = [shape((heads_half, tokens, far * tokens), bf16)] + [shape((heads_half, tokens, HEAD_SIZE), f32)] * 2
    near_state = call(
        functools.partial(near_kernel, ((0, 0), (LAYER, LAYER))), "scores_near", [shape((heads, tokens, HEAD_SIZE), f32)] * 3,
        [VMEM] * 6, 8 * heads * tokens * tokens * HEAD_SIZE, 8 << 20, 12, [pltpu.VMEM((tokens, 2 * tokens), f32)],
    )(starts, query, keys, keys_z, values, values_z)
    (values_d, values_x, values_y), _ = exchange(
        values, values_z, ((3, 0), (1, 0), (2, 0)), [width_k, part, part], [near_state[0]], 9 << 30
    )
    (values_x_more, values_y_more), _ = exchange(values, values_z, ((1, part), (2, part)), [part] * 2, keys_far, 0)
    far_a, far_b = (values_x, values_y, values_d), (values_x_more, values_y_more, values_d)

    *state_a, weights_b, total_b, acc_b = call(
        functools.partial(far_kernel, ((3, 1), (2, 2), (1, 3))), "scores_far", state * 2, [VMEM] * (2 + far + 3),
        6 * heads * tokens * tokens * HEAD_SIZE, 8 << 20, 12, [pltpu.VMEM((tokens, far * tokens), f32)],
    )(starts, query, *keys_far, *near_state)

    columns = w_out.shape[1]
    attended_shape = shape((tokens, width_q // 2), bf16)
    far_flops = far * heads * tokens * tokens * HEAD_SIZE
    out_flops = tokens * width_q * columns
    summed, _ = call(
        functools.partial(mix_first_kernel, far), "mix_first", [shape((tokens, columns), f32), attended_shape],
        [VMEM] * (4 + far), out_flops + far_flops, 4 << 20, 6,
    )(*state_a, *far_a, w_out)

    cut = columns // 2
    send_shape = shape((half, cut), bf16)
    quarter = out_flops // 4
    send, attended = call(
        functools.partial(mix_second_kernel, far), "mix_second", [send_shape, attended_shape],
        [VMEM] * (5 + far), quarter + far_flops, 4 << 20, 6,
    )(weights_b, total_b, acc_b, *far_b, w_out, summed)
    got_low = lax.ppermute(send, "head", SWAP)
    (send,) = call(
        functools.partial(send_columns, cut), "send_high", [send_shape], [VMEM] * 3, quarter, 4 << 20, 6,
    )(attended, w_out, summed)
    got_high = lax.ppermute(send, "head", SWAP)
    (own,) = call(
        functools.partial(own_high_kernel, cut), "own_high", [shape((half, columns - cut), f32)], [VMEM] * 3,
        quarter, 4 << 20, 6,
    )(attended, w_out, summed)
    mixed_shape = pltpu.HBM((half, columns), bf16)
    out_scratch = [pltpu.VMEM((half, cut), bf16), pltpu.SemaphoreType.DMA((cut // WIDE,))]
    (mixed,) = call(
        own_low_kernel, "own_low", [mixed_shape], [VMEM] * 5, quarter, 4 << 20, 6, out_scratch, [ANY],
    )(attended, w_out, summed, got_low, own)
    (mixed,) = call(
        add_kernel, "add", [mixed_shape], [VMEM] * 2 + [ANY], half * cut, 4 << 20, 4, out_scratch, [ANY], {2: 0},
    )(own, got_high, mixed)
    return mixed


def solution(mesh):
    in_specs = (
        P(("seq", "head"), None),
        P(),
        P(None, "head"),
        P(None, "head"),
        P(None, "head"),
        P("head", None),
    )
    out_specs = P(("seq", "head"), None)
    return jax.shard_map(body, mesh=mesh, in_specs=in_specs, out_specs=out_specs, check_vma=False)
```

```python
import functools
import math

import jax
import jax.numpy as jnp
from jax import lax
from jax.experimental import pallas as pl
from jax.experimental.pallas import tpu as pltpu
from jax.sharding import PartitionSpec as P

HEAD_SIZE = 128
LAYER = 4
MASKED = -1e30
VALUES_COST = 4 << 30
RELAY_COST = 5 << 30
SCORE_SCALE = math.log2(math.e) * HEAD_SIZE ** (-0.5)
SWAP = [(0, 1), (1, 0)]
VMEM = pl.BlockSpec(memory_space=pltpu.VMEM)
ANY = pl.BlockSpec(memory_space=pl.ANY)


def inverse_frequency():
    table = []
    for number in range(HEAD_SIZE // 2):
        base_freq = 500000.0 ** (-(2.0 * number) / HEAD_SIZE)
        wavelength = 2.0 * math.pi / base_freq
        smooth = (8192.0 / wavelength - 1.0) / 3.0
        if wavelength < 2048.0:
            table.append(base_freq)
        elif wavelength > 8192.0:
            table.append(base_freq / 8.0)
        else:
            table.append((1.0 - smooth) * base_freq / 8.0 + smooth * base_freq)
    return table


def dot(a, b):
    return jnp.dot(a, b, preferred_element_type=jnp.float32)


def rotated(block, cosine, sine):
    return block * cosine + pltpu.roll(block, HEAD_SIZE // 2, 1) * sine


def load_columns(low, hbms, buffers, sems, chunks):
    depth, wide = buffers[0].shape[0] // chunks, buffers[0].shape[1]
    copies = []
    for number in range(chunks):
        at = pl.ds(number * depth, depth)
        pair = [
            pltpu.make_async_copy(hbm.at[at, pl.ds(low, wide)], buffer.at[at], sems.at[number * len(hbms) + which])
            for which, (hbm, buffer) in enumerate(zip(hbms, buffers))
        ]
        for copy in pair:
            copy.start()
        copies.append(pair)
    return copies


def piecewise_product(rows, copies, buffers, total, put=None):
    depth, wide = buffers[0].shape[0] // len(copies), buffers[0].shape[1]
    for number, pair in enumerate(copies):
        at = slice(number * depth, (number + 1) * depth)
        for which, (copy, buffer) in enumerate(zip(pair, buffers)):
            copy.wait()
            columns = slice(which * wide, (which + 1) * wide)
            product = dot(rows[:, at], buffer[at, :])
            if number > 0:
                product = product + total[:, columns]
            if put is None or number < len(copies) - 1:
                total[:, columns] = product
            else:
                put(which, product)


def first_kernel(chunks, lengths_hbm, own_hbm, key_hbm, value_hbm, total, own, w_key, w_value, cosine, sine, starts, lengths, sems):
    row_copy = pltpu.make_async_copy(own_hbm, own, sems.at[2 * chunks])
    row_copy.start()
    copies = load_columns(0, (key_hbm, value_hbm), (w_key, w_value), sems, chunks)
    tokens = cosine.shape[0]
    length_copy = pltpu.make_async_copy(lengths_hbm, lengths, sems.at[2 * chunks + 1])
    length_copy.start()
    lane = lax.broadcasted_iota(jnp.int32, (1, HEAD_SIZE), 1)
    pair_of_lane = lane % (HEAD_SIZE // 2)
    freq = jnp.zeros((1, HEAD_SIZE), jnp.float32)
    for number, value in enumerate(inverse_frequency()):
        freq = jnp.where(pair_of_lane == number, jnp.float32(value), freq)
    first = lax.axis_index("seq") * tokens
    half = tokens // 2
    low_lane = lane < HEAD_SIZE // 2
    packed = first + lax.broadcasted_iota(jnp.int32, (half, HEAD_SIZE), 0) + jnp.where(low_lane, 0, half)
    angles = packed.astype(jnp.float32) * freq
    turned = jnp.cos(angles)
    other = pltpu.roll(turned, HEAD_SIZE // 2, 1)
    cosine[:half, :] = jnp.where(low_lane, turned, other)
    cosine[half:, :] = jnp.where(low_lane, other, turned)
    turned = jnp.sin(angles)
    other = pltpu.roll(turned, HEAD_SIZE // 2, 1)
    sine[:half, :] = jnp.where(low_lane, -turned, other)
    sine[half:, :] = jnp.where(low_lane, -other, turned)
    positions = first + lax.broadcasted_iota(jnp.int32, (tokens, HEAD_SIZE), 0)
    length_copy.wait()
    start = jnp.zeros((tokens, HEAD_SIZE), jnp.int32)
    end = jnp.int32(0)
    for number in range(lengths.shape[0]):
        end = end + lengths[number]
        start = jnp.where(positions >= end, end, start)
    starts[...] = start
    row_copy.wait()
    piecewise_product(own, copies, (w_key, w_value), total)


def halves(half):
    core = lax.axis_index("head")
    return pl.ds(pl.multiple_of(core * half, half), half), pl.ds(pl.multiple_of((1 - core) * half, half), half)


def put_block(kv, here, block, cosine, sine, is_key, low):
    for head in range(block.shape[1] // HEAD_SIZE):
        piece = block[:, head * HEAD_SIZE : (head + 1) * HEAD_SIZE]
        if is_key:
            piece = rotated(piece, cosine[here, :], sine[here, :])
        kv[here, low + head * HEAD_SIZE : low + (head + 1) * HEAD_SIZE] = piece.astype(kv.dtype)


def second_kernel(other, w_key, w_value, own_total, cosine, sine, kv):
    half, wide = own_total.shape[0], w_key.shape[1]
    mine, theirs = halves(half)
    for which, weight in enumerate((w_key, w_value)):
        low = which * wide
        put_block(kv, mine, own_total[:, low : low + wide], cosine, sine, which == 0, low)
        put_block(kv, theirs, dot(other[...], weight[...]), cosine, sine, which == 0, low)


def third_kernel(chunks, own, other, key_hbm, value_hbm, cosine, sine, kv, rows, done, w_key, w_value, total, sems):
    wide = w_key.shape[1]
    copies = load_columns(wide, (key_hbm, value_hbm), (w_key, w_value), sems, chunks)
    mine, theirs = halves(own.shape[0])
    rows[mine, :] = own[...]
    rows[theirs, :] = other[...]
    done[...] = jnp.zeros_like(done)
    everything = slice(0, rows.shape[0])

    def put(which, product):
        put_block(kv, everything, product, cosine, sine, which == 0, which * wide)

    piecewise_product(rows, copies, (w_key, w_value), total, put)


def query_kernel(rows, weight, cosine, sine, after, query, done):
    del after
    done[...] = jnp.zeros_like(done)
    wide = 4 * HEAD_SIZE
    for number in range(weight.shape[1] // wide):
        result = dot(rows[...], weight[:, number * wide : (number + 1) * wide])
        for head in range(wide // HEAD_SIZE):
            at = slice(head * HEAD_SIZE, (head + 1) * HEAD_SIZE)
            out = slice(number * wide + head * HEAD_SIZE, number * wide + (head + 1) * HEAD_SIZE)
            query[:, out] = rotated(result[:, at], cosine[...], sine[...]).astype(query.dtype)


def relay_kernel(own, earlier, after, to_x, to_y, to_d):
    del after
    index = lax.axis_index("seq")
    mine, theirs = own[...], earlier[...]
    to_x[...] = jnp.where(index % 2 > 0, theirs, mine)
    by_y = jnp.where(index % LAYER >= 2, theirs, mine)
    to_y[...] = by_y
    to_d[...] = by_y


def column(number):
    return slice(number * HEAD_SIZE, (number + 1) * HEAD_SIZE)


def fill_bias(bias, distances, starts):
    tokens = bias.shape[0]
    index = lax.axis_index("seq")
    base = index * tokens
    query_pos = base + lax.broadcasted_iota(jnp.int32, (tokens, tokens), 0)
    start = jnp.concatenate([starts[...]] * (tokens // starts.shape[1]), axis=1)
    for number, (even, odd) in enumerate(distances):
        first = base - tokens * jnp.where(index % 2 > 0, odd, even)
        key_pos = first + lax.broadcasted_iota(jnp.int32, (tokens, tokens), 1)
        allowed = (key_pos >= start) & (key_pos <= query_pos)
        bias[:, number * tokens : (number + 1) * tokens] = jnp.where(allowed, 0.0, MASKED)


def scores_of(query, keys, bias, head, at):
    tokens = bias.shape[0]
    return [
        lax.dot_general(
            query[:, column(head)], key[:, column(at)], (((1,), (1,)), ((), ())), preferred_element_type=jnp.float32
        )
        * SCORE_SCALE
        + bias[:, number * tokens : (number + 1) * tokens]
        for number, key in enumerate(keys)
    ]


def weighted(weights, blocks, at, ones):
    product = None
    for weight, block in zip(weights, blocks):
        term = dot(weight, jnp.concatenate([block[:, column(at)], ones], axis=1))
        product = term if product is None else product + term
    return product[:, :HEAD_SIZE], product[:, HEAD_SIZE:]


def row_max(scores):
    return jnp.max(functools.reduce(jnp.maximum, scores), axis=1, keepdims=True)


def near_kernel(distances, starts, query, *refs):
    count = len(distances)
    tops, totals, accs, bias = refs[-4:]
    parts = [refs[low : low + count] for low in range(0, len(refs) - 4, count)]
    fill_bias(bias, distances, starts)
    tokens = query.shape[0]
    heads = query.shape[1] // HEAD_SIZE
    kv_part = parts[0][0].shape[1] // (2 * HEAD_SIZE)
    group = heads // (kv_part * len(parts))
    ones = jnp.ones((tokens, HEAD_SIZE), query.dtype)

    def place(head):
        return parts[head // group // kv_part], head // group % kv_part

    def ask(head):
        blocks, at = place(head)
        return scores_of(query, blocks, bias, head, at)

    scores = ask(0)
    for head in range(heads):
        ahead = ask(head + 1) if head + 1 < heads else None
        top = row_max(scores)
        blocks, at = place(head)
        weights = [jnp.exp2(score - top).astype(query.dtype) for score in scores]
        tops[head] = jnp.broadcast_to(top, (tokens, HEAD_SIZE))
        accs[head], totals[head] = weighted(weights, blocks, kv_part + at, ones)
        scores = ahead


def attend_far(low, distances, starts, query, blocks, state, attended, bias):
    tops, totals, accs = state
    fill_bias(bias, distances, starts)
    tokens = query.shape[0]
    heads = attended.shape[1] // HEAD_SIZE
    kv_part = blocks[0].shape[1] // (2 * HEAD_SIZE)
    group = heads // kv_part
    ones = jnp.ones((tokens, HEAD_SIZE), query.dtype)
    scores = scores_of(query, blocks, bias, low, 0)
    for head in range(heads):
        ahead = scores_of(query, blocks, bias, low + head + 1, (head + 1) // group) if head + 1 < heads else None
        before = tops[low + head]
        top = jnp.maximum(jnp.broadcast_to(row_max(scores), (tokens, HEAD_SIZE)), before)
        factor = jnp.exp2(before - top)
        wide_top = jnp.concatenate([top] * (tokens // HEAD_SIZE), axis=1)
        weights = [jnp.exp2(score - wide_top).astype(query.dtype) for score in scores]
        acc, total = weighted(weights, blocks, kv_part + head // group, ones)
        result = (accs[low + head] * factor + acc) / (totals[low + head] * factor + total)
        attended[:, column(head)] = result.astype(attended.dtype)
        scores = ahead


WIDE = 4 * HEAD_SIZE


def mix_first_kernel(distances, starts, query, *refs):
    far = len(distances)
    blocks, state, (weight, summed, attended, bias) = refs[:far], refs[far : far + 3], refs[far + 3 :]
    attend_far(0, distances, starts, query, blocks, state, attended, bias)
    depth = attended.shape[1]
    for number in range(summed.shape[1] // WIDE):
        at = slice(number * WIDE, (number + 1) * WIDE)
        summed[:, at] = dot(attended[...], weight[:depth, at])


def rows_product(rows, low, attended, weight, summed, wide):
    depth = attended.shape[1]
    at = slice(low, low + wide)
    return summed[rows, at] + dot(attended[rows, :], weight[depth:, at])


def send_columns(low, attended, weight, summed, send):
    theirs = halves(send.shape[0])[1]
    for number in range(send.shape[1] // WIDE):
        result = rows_product(theirs, low + number * WIDE, attended, weight, summed, WIDE)
        send[:, number * WIDE : (number + 1) * WIDE] = result.astype(send.dtype)


def mix_second_kernel(low, distances, starts, query, *refs):
    far = len(distances)
    blocks, state, (weight, summed, send, attended, bias) = refs[:far], refs[far : far + 3], refs[far + 3 :]
    attend_far(low, distances, starts, query, blocks, state, attended, bias)
    send_columns(0, attended, weight, summed, send)


def own_high_kernel(low, attended, weight, summed, own):
    mine = halves(own.shape[0])[0]
    for number in range(own.shape[1] // WIDE):
        result = rows_product(mine, low + number * WIDE, attended, weight, summed, WIDE)
        own[:, number * WIDE : (number + 1) * WIDE] = result


def own_low_kernel(attended, weight, summed, got, after, mixed):
    del after
    mine = halves(got.shape[0])[0]
    for number in range(got.shape[1] // WIDE):
        at = slice(number * WIDE, (number + 1) * WIDE)
        result = rows_product(mine, number * WIDE, attended, weight, summed, WIDE)
        mixed[:, at] = (result + got[:, at].astype(jnp.float32)).astype(mixed.dtype)


def add_kernel(mixed_low, own, got, mixed_hbm, mixed, sems):
    low = mixed_low.shape[1]
    copies = [pltpu.make_async_copy(mixed_low, mixed_hbm.at[:, pl.ds(0, low)], sems.at[0])]
    copies[0].start()
    for number in range(own.shape[1] // WIDE):
        at = slice(number * WIDE, (number + 1) * WIDE)
        mixed[:, at] = (own[:, at] + got[:, at].astype(jnp.float32)).astype(mixed.dtype)
        there = mixed_hbm.at[:, pl.ds(low + number * WIDE, WIDE)]
        copies.append(pltpu.make_async_copy(mixed.at[:, pl.ds(number * WIDE, WIDE)], there, sems.at[number + 1]))
        copies[-1].start()
    for copy in copies:
        copy.wait()


def call(kernel, name, outs, in_specs, flops, nbytes, limit, scratch=(), out_specs=None):
    return pl.pallas_call(
        kernel,
        out_shape=outs,
        in_specs=in_specs,
        out_specs=out_specs or [VMEM] * len(outs),
        scratch_shapes=list(scratch),
        name=name,
        cost_estimate=pl.CostEstimate(flops=flops, bytes_accessed=nbytes, transcendentals=0),
        compiler_params=pltpu.CompilerParams(vmem_limit_bytes=limit << 20),
    )


def in_hbm(array):
    return pltpu.with_memory_space_constraint(array, pltpu.HBM)


def body(input_rows, doc_lengths, w_query, key_weight, value_weight, w_out):
    half, model = input_rows.shape
    tokens = 2 * half
    width_q, width_k = w_query.shape[1], key_weight.shape[1]
    heads = width_q // HEAD_SIZE
    shards = lax.axis_size("seq")
    bf16, f32 = jnp.bfloat16, jnp.float32
    shape = pltpu.VMEM

    other = lax.ppermute(input_rows, "head", SWAP)

    flag = shape((8, HEAD_SIZE), f32)
    table = shape((tokens, HEAD_SIZE), f32)
    part = width_k // 2
    kv_shape = shape((tokens, 2 * part), bf16)
    part_shape = shape((model, part), bf16)
    chunks = 4
    kv_flops = 4 * half * model * part
    total, own, w_key, w_value, cosine, sine, starts = call(
        functools.partial(first_kernel, chunks), "keys_values_own",
        [
            shape((half, 2 * part), f32), shape((half, model), bf16), part_shape, part_shape,
            table, table, shape((tokens, HEAD_SIZE), jnp.int32),
        ],
        [ANY] * 4, kv_flops, 2 * model * width_k, 4,
        [pltpu.SMEM(doc_lengths.shape, jnp.int32), pltpu.SemaphoreType.DMA((2 * chunks + 2,))],
    )(in_hbm(doc_lengths), in_hbm(input_rows), in_hbm(key_weight), in_hbm(value_weight))
    (kv_a,) = call(
        second_kernel, "keys_values", [kv_shape], [VMEM] * 6, kv_flops, 2 * model * width_k, 4,
    )(other, w_key, w_value, total, cosine, sine)

    every = range(shards)
    step_z = [(i, (i + LAYER) % shards) for i in every]
    z_a = lax.ppermute(kv_a, "seq", [(a, b) for a, b in step_z if a < b])

    kv_b, rows, done = call(
        functools.partial(third_kernel, chunks), "keys_values_more", [kv_shape, shape((tokens, model), bf16), flag],
        [VMEM, VMEM, ANY, ANY, VMEM, VMEM], VALUES_COST, 2 * model * width_k, 10,
        [part_shape, part_shape, pltpu.VMEM((tokens, 2 * part), f32), pltpu.SemaphoreType.DMA((2 * chunks,))],
    )(own, other, in_hbm(key_weight), in_hbm(value_weight), cosine, sine)
    z_b = lax.ppermute(kv_b, "seq", step_z)

    def exchange(mine, earlier, after, ways, cost):
        to = call(
            relay_kernel, "relay", [kv_shape] * 3, [VMEM] * 3, cost, 2 << 20, 4,
        )(mine, earlier, after)
        got = {way: lax.ppermute(to[way - 1], "seq", [(i, i ^ way) for i in every]) for way in ways}
        return [got[way] for way in (1, 2, 3)], to[0]

    far_a, done = exchange(kv_a, z_a, done, (1, 2, 3), RELAY_COST)
    query, done = call(
        query_kernel, "queries", [shape((tokens, width_q), bf16), flag], [VMEM] * 5,
        2 * tokens * model * width_q, 2 * model * width_q, 8,
    )(rows, w_query, cosine, sine, done)
    far_b, _ = exchange(kv_b, z_b, done, (3, 1, 2), 9 << 30)
    near = call(
        functools.partial(near_kernel, ((0, 0), (LAYER, LAYER))), "scores_near", [shape((heads, tokens, HEAD_SIZE), f32)] * 3,
        [VMEM] * 6, 8 * heads * tokens * tokens * HEAD_SIZE, 8 << 20, 12, [pltpu.VMEM((tokens, 2 * tokens), f32)],
    )(starts, query, kv_a, z_a, kv_b, z_b)

    far = len(far_a)
    distances = ((3, 1), (2, 2), (1, 3))
    bias = pltpu.VMEM((tokens, far * tokens), f32)
    columns = w_out.shape[1]
    attended_shape = shape((tokens, width_q // 2), bf16)
    far_flops = 3 * far * heads * tokens * tokens * HEAD_SIZE
    out_flops = tokens * width_q * columns
    summed, _ = call(
        functools.partial(mix_first_kernel, distances), "mix_first", [shape((tokens, columns), f32), attended_shape],
        [VMEM] * (6 + far), out_flops + far_flops, 4 << 20, 10, [bias],
    )(starts, query, *far_a, *near, w_out)

    cut = columns // 2
    send_shape = shape((half, cut), bf16)
    quarter = out_flops // 4
    send, attended = call(
        functools.partial(mix_second_kernel, heads // 2, distances), "mix_second", [send_shape, attended_shape],
        [VMEM] * (7 + far), quarter + far_flops, 4 << 20, 10, [bias],
    )(starts, query, *far_b, *near, w_out, summed)
    got_low = lax.ppermute(send, "head", SWAP)
    (send,) = call(
        functools.partial(send_columns, cut), "send_high", [send_shape], [VMEM] * 3, quarter, 4 << 20, 6,
    )(attended, w_out, summed)
    got_high = lax.ppermute(send, "head", SWAP)
    (own,) = call(
        functools.partial(own_high_kernel, cut), "own_high", [shape((half, columns - cut), f32)], [VMEM] * 3,
        quarter, 4 << 20, 6,
    )(attended, w_out, summed)
    (mixed,) = call(
        own_low_kernel, "own_low", [send_shape], [VMEM] * 5, quarter, 4 << 20, 6,
    )(attended, w_out, summed, got_low, own)
    (mixed,) = call(
        add_kernel, "add", [pltpu.HBM((half, columns), bf16)], [VMEM] * 3, half * cut, 4 << 20, 4,
        [pltpu.VMEM((half, columns - cut), bf16), pltpu.SemaphoreType.DMA(((columns - cut) // WIDE + 1,))], [ANY],
    )(mixed, own, got_high)
    return mixed


def solution(mesh):
    in_specs = (
        P(("seq", "head"), None),
        P(),
        P(None, "head"),
        P(None, "head"),
        P(None, "head"),
        P("head", None),
    )
    out_specs = P(("seq", "head"), None)
    return jax.shard_map(body, mesh=mesh, in_specs=in_specs, out_specs=out_specs, check_vma=False)
```

```python
import functools
import math

import jax
import jax.numpy as jnp
from jax import lax
from jax.experimental import pallas as pl
from jax.experimental.pallas import tpu as pltpu
from jax.sharding import PartitionSpec as P

HEAD_SIZE = 128
LAYER = 4
MASKED = -1e30
VALUES_COST = 4 << 30
RELAY_COST = 5 << 30
SCORE_SCALE = math.log2(math.e) * HEAD_SIZE ** (-0.5)
SWAP = [(0, 1), (1, 0)]
VMEM = pl.BlockSpec(memory_space=pltpu.VMEM)
ANY = pl.BlockSpec(memory_space=pl.ANY)


def inverse_frequency():
    table = []
    for number in range(HEAD_SIZE // 2):
        base_freq = 500000.0 ** (-(2.0 * number) / HEAD_SIZE)
        wavelength = 2.0 * math.pi / base_freq
        smooth = (8192.0 / wavelength - 1.0) / 3.0
        if wavelength < 2048.0:
            table.append(base_freq)
        elif wavelength > 8192.0:
            table.append(base_freq / 8.0)
        else:
            table.append((1.0 - smooth) * base_freq / 8.0 + smooth * base_freq)
    return table


def dot(a, b):
    return jnp.dot(a, b, preferred_element_type=jnp.float32)


def rotated(block, cosine, sine):
    return block * cosine + pltpu.roll(block, HEAD_SIZE // 2, 1) * sine


def load_columns(low, hbms, buffers, sems, chunks):
    depth, wide = buffers[0].shape[0] // chunks, buffers[0].shape[1]
    copies = []
    for number in range(chunks):
        at = pl.ds(number * depth, depth)
        pair = [
            pltpu.make_async_copy(hbm.at[at, pl.ds(low, wide)], buffer.at[at], sems.at[number * len(hbms) + which])
            for which, (hbm, buffer) in enumerate(zip(hbms, buffers))
        ]
        for copy in pair:
            copy.start()
        copies.append(pair)
    return copies


def piecewise_product(rows, copies, buffers, total, put=None):
    depth, wide = buffers[0].shape[0] // len(copies), buffers[0].shape[1]
    for number, pair in enumerate(copies):
        at = slice(number * depth, (number + 1) * depth)
        for which, (copy, buffer) in enumerate(zip(pair, buffers)):
            copy.wait()
            columns = slice(which * wide, (which + 1) * wide)
            product = dot(rows[:, at], buffer[at, :])
            if number > 0:
                product = product + total[:, columns]
            if put is None or number < len(copies) - 1:
                total[:, columns] = product
            else:
                put(which, product)


def first_kernel(chunks, lengths_hbm, own_hbm, key_hbm, value_hbm, total, own, w_key, w_value, cosine, sine, starts, lengths, sems):
    row_copy = pltpu.make_async_copy(own_hbm, own, sems.at[2 * chunks])
    row_copy.start()
    copies = load_columns(0, (key_hbm, value_hbm), (w_key, w_value), sems, chunks)
    tokens = cosine.shape[0]
    length_copy = pltpu.make_async_copy(lengths_hbm, lengths, sems.at[2 * chunks + 1])
    length_copy.start()
    lane = lax.broadcasted_iota(jnp.int32, (1, HEAD_SIZE), 1)
    pair_of_lane = lane % (HEAD_SIZE // 2)
    freq = jnp.zeros((1, HEAD_SIZE), jnp.float32)
    for number, value in enumerate(inverse_frequency()):
        freq = jnp.where(pair_of_lane == number, jnp.float32(value), freq)
    first = lax.axis_index("seq") * tokens
    half = tokens // 2
    low_lane = lane < HEAD_SIZE // 2
    packed = first + lax.broadcasted_iota(jnp.int32, (half, HEAD_SIZE), 0) + jnp.where(low_lane, 0, half)
    angles = packed.astype(jnp.float32) * freq
    turned = jnp.cos(angles)
    other = pltpu.roll(turned, HEAD_SIZE // 2, 1)
    cosine[:half, :] = jnp.where(low_lane, turned, other)
    cosine[half:, :] = jnp.where(low_lane, other, turned)
    turned = jnp.sin(angles)
    other = pltpu.roll(turned, HEAD_SIZE // 2, 1)
    sine[:half, :] = jnp.where(low_lane, -turned, other)
    sine[half:, :] = jnp.where(low_lane, -other, turned)
    positions = first + lax.broadcasted_iota(jnp.int32, (tokens, HEAD_SIZE), 0)
    length_copy.wait()
    start = jnp.zeros((tokens, HEAD_SIZE), jnp.int32)
    end = jnp.int32(0)
    for number in range(lengths.shape[0]):
        end = end + lengths[number]
        start = jnp.where(positions >= end, end, start)
    starts[...] = start
    row_copy.wait()
    piecewise_product(own, copies, (w_key, w_value), total)


def halves(half):
    core = lax.axis_index("head")
    return pl.ds(pl.multiple_of(core * half, half), half), pl.ds(pl.multiple_of((1 - core) * half, half), half)


def put_block(kv, here, block, cosine, sine, is_key, low):
    for head in range(block.shape[1] // HEAD_SIZE):
        piece = block[:, head * HEAD_SIZE : (head + 1) * HEAD_SIZE]
        if is_key:
            piece = rotated(piece, cosine[here, :], sine[here, :])
        kv[here, low + head * HEAD_SIZE : low + (head + 1) * HEAD_SIZE] = piece.astype(kv.dtype)


def second_kernel(other, w_key, w_value, own_total, cosine, sine, kv):
    half, wide = own_total.shape[0], w_key.shape[1]
    mine, theirs = halves(half)
    for which, weight in enumerate((w_key, w_value)):
        low = which * wide
        put_block(kv, mine, own_total[:, low : low + wide], cosine, sine, which == 0, low)
        put_block(kv, theirs, dot(other[...], weight[...]), cosine, sine, which == 0, low)


def third_kernel(chunks, own, other, key_hbm, value_hbm, cosine, sine, kv, rows, done, w_key, w_value, total, sems):
    wide = w_key.shape[1]
    copies = load_columns(wide, (key_hbm, value_hbm), (w_key, w_value), sems, chunks)
    mine, theirs = halves(own.shape[0])
    rows[mine, :] = own[...]
    rows[theirs, :] = other[...]
    done[...] = jnp.zeros_like(done)
    everything = slice(0, rows.shape[0])

    def put(which, product):
        put_block(kv, everything, product, cosine, sine, which == 0, which * wide)

    piecewise_product(rows, copies, (w_key, w_value), total, put)


def query_kernel(rows, weight, cosine, sine, after, query, done):
    del after
    done[...] = jnp.zeros_like(done)
    wide = 4 * HEAD_SIZE
    for number in range(weight.shape[1] // wide):
        result = dot(rows[...], weight[:, number * wide : (number + 1) * wide])
        for head in range(wide // HEAD_SIZE):
            at = slice(head * HEAD_SIZE, (head + 1) * HEAD_SIZE)
            out = slice(number * wide + head * HEAD_SIZE, number * wide + (head + 1) * HEAD_SIZE)
            query[:, out] = rotated(result[:, at], cosine[...], sine[...]).astype(query.dtype)


def relay_kernel(plan, own, earlier, *refs):
    outs = refs[len(refs) - len(plan) :]
    index = lax.axis_index("seq")
    for (way, heads), out in zip(plan, outs):
        upper = index % 2 > 0 if way == 1 else index % LAYER >= 2
        for number, head in enumerate(heads):
            out[:, column(number)] = jnp.where(upper, earlier[:, column(head)], own[:, column(head)])


def column(number):
    return slice(number * HEAD_SIZE, (number + 1) * HEAD_SIZE)


def fill_bias(bias, distances, starts):
    tokens = bias.shape[0]
    index = lax.axis_index("seq")
    base = index * tokens
    query_pos = base + lax.broadcasted_iota(jnp.int32, (tokens, tokens), 0)
    start = jnp.concatenate([starts[...]] * (tokens // starts.shape[1]), axis=1)
    for number, (even, odd) in enumerate(distances):
        first = base - tokens * jnp.where(index % 2 > 0, odd, even)
        key_pos = first + lax.broadcasted_iota(jnp.int32, (tokens, tokens), 1)
        allowed = (key_pos >= start) & (key_pos <= query_pos)
        bias[:, number * tokens : (number + 1) * tokens] = jnp.where(allowed, 0.0, MASKED)


def scores_of(query, keys, bias, head):
    tokens = bias.shape[0]
    return [
        lax.dot_general(
            query[:, column(head)], key[:, column(at)], (((1,), (1,)), ((), ())), preferred_element_type=jnp.float32
        )
        * SCORE_SCALE
        + bias[:, number * tokens : (number + 1) * tokens]
        for number, (key, at) in enumerate(keys)
    ]


def weighted(weights, blocks, ones):
    product = None
    for weight, (block, at) in zip(weights, blocks):
        term = dot(weight, jnp.concatenate([block[:, column(at)], ones], axis=1))
        product = term if product is None else product + term
    return product[:, :HEAD_SIZE], product[:, HEAD_SIZE:]


def row_max(scores):
    return jnp.max(functools.reduce(jnp.maximum, scores), axis=1, keepdims=True)


def near_kernel(distances, starts, query, *refs):
    count = len(distances)
    tops, totals, accs, bias = refs[-4:]
    parts = [refs[low : low + count] for low in range(0, len(refs) - 4, count)]
    fill_bias(bias, distances, starts)
    tokens = query.shape[0]
    heads = query.shape[1] // HEAD_SIZE
    kv_part = parts[0][0].shape[1] // (2 * HEAD_SIZE)
    group = heads // (kv_part * len(parts))
    ones = jnp.ones((tokens, HEAD_SIZE), query.dtype)

    def place(head):
        return parts[head // group // kv_part], head // group % kv_part

    def ask(head):
        blocks, at = place(head)
        return scores_of(query, [(block, at) for block in blocks], bias, head)

    scores = ask(0)
    for head in range(heads):
        ahead = ask(head + 1) if head + 1 < heads else None
        top = row_max(scores)
        blocks, at = place(head)
        weights = [jnp.exp2(score - top).astype(query.dtype) for score in scores]
        tops[head] = jnp.broadcast_to(top, (tokens, HEAD_SIZE))
        accs[head], totals[head] = weighted(weights, [(block, kv_part + at) for block in blocks], ones)
        scores = ahead


def attend_far(low, places, distances, starts, query, blocks, state, attended, bias):
    tops, totals, accs = state
    fill_bias(bias, distances, starts)
    tokens = query.shape[0]
    heads = attended.shape[1] // HEAD_SIZE
    group = heads // len(places)
    ones = jnp.ones((tokens, HEAD_SIZE), query.dtype)

    def ask(head):
        return scores_of(query, list(zip(blocks, places[head // group][0])), bias, low + head)

    scores = ask(0)
    for head in range(heads):
        ahead = ask(head + 1) if head + 1 < heads else None
        before = tops[low + head]
        top = jnp.maximum(jnp.broadcast_to(row_max(scores), (tokens, HEAD_SIZE)), before)
        factor = jnp.exp2(before - top)
        wide_top = jnp.concatenate([top] * (tokens // HEAD_SIZE), axis=1)
        weights = [jnp.exp2(score - wide_top).astype(query.dtype) for score in scores]
        acc, total = weighted(weights, list(zip(blocks, places[head // group][1])), ones)
        result = (accs[low + head] * factor + acc) / (totals[low + head] * factor + total)
        attended[:, column(head)] = result.astype(attended.dtype)
        scores = ahead


WIDE = 4 * HEAD_SIZE


def mix_first_kernel(places, distances, starts, query, *refs):
    far = len(distances)
    blocks, state, (weight, summed, attended, bias) = refs[:far], refs[far : far + 3], refs[far + 3 :]
    attend_far(0, places, distances, starts, query, blocks, state, attended, bias)
    for number in range(summed.shape[1] // WIDE):
        at = slice(number * WIDE, (number + 1) * WIDE)
        summed[:, at] = dot(attended[...], weight[: attended.shape[1], at])


def attend_kernel(low, places, distances, starts, query, *refs):
    far = len(distances)
    blocks, state, (attended, bias) = refs[:far], refs[far : far + 3], refs[far + 3 :]
    attend_far(low, places, distances, starts, query, blocks, state, attended, bias)


def rows_product(rows, low, attended, weight, summed, wide):
    depth = weight.shape[0] - attended.shape[1]
    at = slice(low, low + wide)
    return summed[rows, at] + dot(attended[rows, :], weight[depth:, at])


def send_columns(low, attended, weight, summed, send):
    theirs = halves(send.shape[0])[1]
    for number in range(send.shape[1] // WIDE):
        result = rows_product(theirs, low + number * WIDE, attended, weight, summed, WIDE)
        send[:, number * WIDE : (number + 1) * WIDE] = result.astype(send.dtype)


def mix_last_kernel(low, places, distances, starts, query, *refs):
    far = len(distances)
    blocks, state, refs = refs[:far], refs[far : far + 3], refs[far + 3 :]
    before, weight, summed, send, attended, bias = refs
    done = before.shape[1]
    attended[:, :done] = before[...]
    late = attended.at[:, pl.ds(done, attended.shape[1] - done)]
    attend_far(low, places, distances, starts, query, blocks, state, late, bias)
    send_columns(0, attended, weight, summed, send)


def own_high_kernel(low, attended, weight, summed, own):
    mine = halves(own.shape[0])[0]
    for number in range(own.shape[1] // WIDE):
        result = rows_product(mine, low + number * WIDE, attended, weight, summed, WIDE)
        own[:, number * WIDE : (number + 1) * WIDE] = result


def own_low_kernel(attended, weight, summed, got, after, mixed):
    del after
    mine = halves(got.shape[0])[0]
    for number in range(got.shape[1] // WIDE):
        at = slice(number * WIDE, (number + 1) * WIDE)
        result = rows_product(mine, number * WIDE, attended, weight, summed, WIDE)
        mixed[:, at] = (result + got[:, at].astype(jnp.float32)).astype(mixed.dtype)


def add_kernel(mixed_low, own, got, mixed_hbm, mixed, sems):
    low = mixed_low.shape[1]
    copies = [pltpu.make_async_copy(mixed_low, mixed_hbm.at[:, pl.ds(0, low)], sems.at[0])]
    copies[0].start()
    for number in range(own.shape[1] // WIDE):
        at = slice(number * WIDE, (number + 1) * WIDE)
        mixed[:, at] = (own[:, at] + got[:, at].astype(jnp.float32)).astype(mixed.dtype)
        there = mixed_hbm.at[:, pl.ds(low + number * WIDE, WIDE)]
        copies.append(pltpu.make_async_copy(mixed.at[:, pl.ds(number * WIDE, WIDE)], there, sems.at[number + 1]))
        copies[-1].start()
    for copy in copies:
        copy.wait()


def call(kernel, name, outs, in_specs, flops, nbytes, limit, scratch=(), out_specs=None):
    return pl.pallas_call(
        kernel,
        out_shape=outs,
        in_specs=in_specs,
        out_specs=out_specs or [VMEM] * len(outs),
        scratch_shapes=list(scratch),
        name=name,
        cost_estimate=pl.CostEstimate(flops=flops, bytes_accessed=nbytes, transcendentals=0),
        compiler_params=pltpu.CompilerParams(vmem_limit_bytes=limit << 20),
    )


def in_hbm(array):
    return pltpu.with_memory_space_constraint(array, pltpu.HBM)


def body(input_rows, doc_lengths, w_query, key_weight, value_weight, w_out):
    half, model = input_rows.shape
    tokens = 2 * half
    width_q, width_k = w_query.shape[1], key_weight.shape[1]
    heads = width_q // HEAD_SIZE
    shards = lax.axis_size("seq")
    bf16, f32 = jnp.bfloat16, jnp.float32
    shape = pltpu.VMEM

    other = lax.ppermute(input_rows, "head", SWAP)

    flag = shape((8, HEAD_SIZE), f32)
    table = shape((tokens, HEAD_SIZE), f32)
    part = width_k // 2
    kv_shape = shape((tokens, 2 * part), bf16)
    part_shape = shape((model, part), bf16)
    chunks = 4
    kv_flops = 4 * half * model * part
    total, own, w_key, w_value, cosine, sine, starts = call(
        functools.partial(first_kernel, chunks), "keys_values_own",
        [
            shape((half, 2 * part), f32), shape((half, model), bf16), part_shape, part_shape,
            table, table, shape((tokens, HEAD_SIZE), jnp.int32),
        ],
        [ANY] * 4, kv_flops, 2 * model * width_k, 4,
        [pltpu.SMEM(doc_lengths.shape, jnp.int32), pltpu.SemaphoreType.DMA((2 * chunks + 2,))],
    )(in_hbm(doc_lengths), in_hbm(input_rows), in_hbm(key_weight), in_hbm(value_weight))
    (kv_a,) = call(
        second_kernel, "keys_values", [kv_shape], [VMEM] * 6, kv_flops, 2 * model * width_k, 4,
    )(other, w_key, w_value, total, cosine, sine)

    every = range(shards)
    step_z = [(i, (i + LAYER) % shards) for i in every]
    z_a = lax.ppermute(kv_a, "seq", [(a, b) for a, b in step_z if a < b])

    kv_b, rows, done = call(
        functools.partial(third_kernel, chunks), "keys_values_more", [kv_shape, shape((tokens, model), bf16), flag],
        [VMEM, VMEM, ANY, ANY, VMEM, VMEM], VALUES_COST, 2 * model * width_k, 10,
        [part_shape, part_shape, pltpu.VMEM((tokens, 2 * part), f32), pltpu.SemaphoreType.DMA((2 * chunks,))],
    )(own, other, in_hbm(key_weight), in_hbm(value_weight), cosine, sine)
    z_b = lax.ppermute(kv_b, "seq", step_z)

    def exchange(mine, earlier, after, plan, cost):
        to = call(
            functools.partial(relay_kernel, plan), "relay",
            [shape((tokens, len(taken) * HEAD_SIZE), bf16) for _, taken in plan], [VMEM] * (2 + len(after)), cost, 2 << 20, 4,
        )(mine, earlier, *after)
        return [lax.ppermute(array, "seq", [(i, i ^ way) for i in every]) for (way, _), array in zip(plan, to)], to[0]

    kv_part = part // HEAD_SIZE
    kv_cut = kv_part // 2
    everything = tuple(range(2 * kv_part))
    early = tuple(range(kv_cut)) + tuple(range(kv_part, kv_part + kv_cut))
    late = tuple(range(kv_cut, kv_part)) + tuple(range(kv_part + kv_cut, 2 * kv_part))
    (x_a, y_a, d_a), done = exchange(kv_a, z_a, [kv_b], ((1, everything), (2, everything), (3, everything)), RELAY_COST)
    far_a = d_a, x_a, y_a
    query, done = call(
        query_kernel, "queries", [shape((tokens, width_q), bf16), flag], [VMEM] * 5,
        2 * tokens * model * width_q, 2 * model * width_q, 8,
    )(rows, w_query, cosine, sine, done)
    (d_b,), _ = exchange(kv_b, z_b, [done], ((3, everything),), 9 << 30)
    near = call(
        functools.partial(near_kernel, ((0, 0), (LAYER, LAYER))), "scores_near", [shape((heads, tokens, HEAD_SIZE), f32)] * 3,
        [VMEM] * 6, 8 * heads * tokens * tokens * HEAD_SIZE, 8 << 20, 12, [pltpu.VMEM((tokens, 2 * tokens), f32)],
    )(starts, query, kv_a, z_a, kv_b, z_b)
    (x_early, y_early), done = exchange(kv_b, z_b, [near[0]], ((1, early), (2, early)), 0)
    (x_late, y_late), _ = exchange(kv_b, z_b, [done, *far_a], ((1, late), (2, late)), 0)

    far = len(far_a)
    distances = ((1, 3), (3, 1), (2, 2))
    bias = pltpu.VMEM((tokens, far * tokens), f32)
    columns = w_out.shape[1]
    far_flops = 6 * far * heads * tokens * tokens * HEAD_SIZE
    out_flops = 2 * tokens * width_q * columns
    heads_part, heads_cut = heads // 2, heads // 2 // kv_part * kv_cut
    whole = [((head,) * far, (kv_part + head,) * far) for head in range(kv_part)]
    places_early = [((n, n, n), (kv_part + n, kv_cut + n, kv_cut + n)) for n in range(kv_cut)]
    rest = kv_part - kv_cut
    places_late = [((kv_cut + n, n, n), (kv_part + kv_cut + n, rest + n, rest + n)) for n in range(rest)]

    def attended_shape(count):
        return shape((tokens, count * HEAD_SIZE), bf16)

    summed, _ = call(
        functools.partial(mix_first_kernel, whole, distances), "mix_first",
        [shape((tokens, columns), f32), attended_shape(heads_part)], [VMEM] * (6 + far),
        (out_flops + far_flops) // 2, 4 << 20, 10, [bias],
    )(starts, query, *far_a, *near, w_out)
    (early_heads,) = call(
        functools.partial(attend_kernel, heads_part, places_early, distances), "attend_early",
        [attended_shape(heads_cut)], [VMEM] * (5 + far), far_flops // 4, 4 << 20, 10, [bias],
    )(starts, query, d_b, x_early, y_early, *near)

    cut = columns // 2
    send_shape = shape((half, cut), bf16)
    quarter = out_flops // 8
    low = heads_part + heads_cut
    send, attended = call(
        functools.partial(mix_last_kernel, low, places_late, distances), "mix_last",
        [send_shape, attended_shape(heads_part)], [VMEM] * (8 + far), quarter + far_flops // 4, 4 << 20, 10, [bias],
    )(starts, query, d_b, x_late, y_late, *near, early_heads, w_out, summed)
    got_low = lax.ppermute(send, "head", SWAP)
    (send,) = call(
        functools.partial(send_columns, cut), "send_high", [send_shape], [VMEM] * 3, quarter, 4 << 20, 6,
    )(attended, w_out, summed)
    got_high = lax.ppermute(send, "head", SWAP)
    (own,) = call(
        functools.partial(own_high_kernel, cut), "own_high", [shape((half, columns - cut), f32)], [VMEM] * 3,
        quarter, 4 << 20, 6,
    )(attended, w_out, summed)
    (mixed,) = call(
        own_low_kernel, "own_low", [send_shape], [VMEM] * 5, quarter, 4 << 20, 6,
    )(attended, w_out, summed, got_low, own)
    (mixed,) = call(
        add_kernel, "add", [pltpu.HBM((half, columns), bf16)], [VMEM] * 3, half * cut, 4 << 20, 4,
        [pltpu.VMEM((half, columns - cut), bf16), pltpu.SemaphoreType.DMA(((columns - cut) // WIDE + 1,))], [ANY],
    )(mixed, own, got_high)
    return mixed


def solution(mesh):
    in_specs = (
        P(("seq", "head"), None),
        P(),
        P(None, "head"),
        P(None, "head"),
        P(None, "head"),
        P("head", None),
    )
    out_specs = P(("seq", "head"), None)
    return jax.shard_map(body, mesh=mesh, in_specs=in_specs, out_specs=out_specs, check_vma=False)
```

```python
import functools
import math

import jax
import jax.numpy as jnp
from jax import lax
from jax.experimental import pallas as pl
from jax.experimental.pallas import tpu as pltpu
from jax.sharding import PartitionSpec as P

HEAD_SIZE = 128
LAYER = 4
MASKED = -1e30
VALUES_COST = 4 << 30
RELAY_COST = 5 << 30
SCORE_SCALE = math.log2(math.e) * HEAD_SIZE ** (-0.5)
SWAP = [(0, 1), (1, 0)]
VMEM = pl.BlockSpec(memory_space=pltpu.VMEM)
ANY = pl.BlockSpec(memory_space=pl.ANY)


def inverse_frequency():
    table = []
    for number in range(HEAD_SIZE // 2):
        base_freq = 500000.0 ** (-(2.0 * number) / HEAD_SIZE)
        wavelength = 2.0 * math.pi / base_freq
        smooth = (8192.0 / wavelength - 1.0) / 3.0
        if wavelength < 2048.0:
            table.append(base_freq)
        elif wavelength > 8192.0:
            table.append(base_freq / 8.0)
        else:
            table.append((1.0 - smooth) * base_freq / 8.0 + smooth * base_freq)
    return table


def dot(a, b):
    return jnp.dot(a, b, preferred_element_type=jnp.float32)


def rotated(block, cosine, sine):
    return block * cosine + pltpu.roll(block, HEAD_SIZE // 2, 1) * sine


def load_columns(low, hbms, buffers, sems, chunks):
    depth, wide = buffers[0].shape[0] // chunks, buffers[0].shape[1]
    copies = []
    for number in range(chunks):
        at = pl.ds(number * depth, depth)
        pair = [
            pltpu.make_async_copy(hbm.at[at, pl.ds(low, wide)], buffer.at[at], sems.at[number * len(hbms) + which])
            for which, (hbm, buffer) in enumerate(zip(hbms, buffers))
        ]
        for copy in pair:
            copy.start()
        copies.append(pair)
    return copies


def piecewise_product(rows, copies, buffers, total, put=None):
    depth, wide = buffers[0].shape[0] // len(copies), buffers[0].shape[1]
    for number, pair in enumerate(copies):
        at = slice(number * depth, (number + 1) * depth)
        for which, (copy, buffer) in enumerate(zip(pair, buffers)):
            copy.wait()
            columns = slice(which * wide, (which + 1) * wide)
            product = dot(rows[:, at], buffer[at, :])
            if number > 0:
                product = product + total[:, columns]
            if put is None or number < len(copies) - 1:
                total[:, columns] = product
            else:
                put(which, product)


def first_kernel(chunks, lengths_hbm, own_hbm, key_hbm, value_hbm, total, own, w_key, w_value, cosine, sine, starts, lengths, sems):
    row_copy = pltpu.make_async_copy(own_hbm, own, sems.at[2 * chunks])
    row_copy.start()
    copies = load_columns(0, (key_hbm, value_hbm), (w_key, w_value), sems, chunks)
    tokens = cosine.shape[0]
    length_copy = pltpu.make_async_copy(lengths_hbm, lengths, sems.at[2 * chunks + 1])
    length_copy.start()
    lane = lax.broadcasted_iota(jnp.int32, (1, HEAD_SIZE), 1)
    pair_of_lane = lane % (HEAD_SIZE // 2)
    freq = jnp.zeros((1, HEAD_SIZE), jnp.float32)
    for number, value in enumerate(inverse_frequency()):
        freq = jnp.where(pair_of_lane == number, jnp.float32(value), freq)
    first = lax.axis_index("seq") * tokens
    half = tokens // 2
    low_lane = lane < HEAD_SIZE // 2
    packed = first + lax.broadcasted_iota(jnp.int32, (half, HEAD_SIZE), 0) + jnp.where(low_lane, 0, half)
    angles = packed.astype(jnp.float32) * freq
    turned = jnp.cos(angles)
    other = pltpu.roll(turned, HEAD_SIZE // 2, 1)
    cosine[:half, :] = jnp.where(low_lane, turned, other)
    cosine[half:, :] = jnp.where(low_lane, other, turned)
    turned = jnp.sin(angles)
    other = pltpu.roll(turned, HEAD_SIZE // 2, 1)
    sine[:half, :] = jnp.where(low_lane, -turned, other)
    sine[half:, :] = jnp.where(low_lane, -other, turned)
    positions = first + lax.broadcasted_iota(jnp.int32, (tokens, HEAD_SIZE), 0)
    length_copy.wait()
    start = jnp.zeros((tokens, HEAD_SIZE), jnp.int32)
    end = jnp.int32(0)
    for number in range(lengths.shape[0]):
        end = end + lengths[number]
        start = jnp.where(positions >= end, end, start)
    starts[...] = start
    row_copy.wait()
    piecewise_product(own, copies, (w_key, w_value), total)


def halves(half):
    core = lax.axis_index("head")
    return pl.ds(pl.multiple_of(core * half, half), half), pl.ds(pl.multiple_of((1 - core) * half, half), half)


def put_block(kv, here, block, cosine, sine, is_key, low):
    for head in range(block.shape[1] // HEAD_SIZE):
        piece = block[:, head * HEAD_SIZE : (head + 1) * HEAD_SIZE]
        if is_key:
            piece = rotated(piece, cosine[here, :], sine[here, :])
        kv[here, low + head * HEAD_SIZE : low + (head + 1) * HEAD_SIZE] = piece.astype(kv.dtype)


def second_kernel(other, w_key, w_value, own_total, cosine, sine, kv):
    half, wide = own_total.shape[0], w_key.shape[1]
    mine, theirs = halves(half)
    for which, weight in enumerate((w_key, w_value)):
        low = which * wide
        put_block(kv, mine, own_total[:, low : low + wide], cosine, sine, which == 0, low)
        put_block(kv, theirs, dot(other[...], weight[...]), cosine, sine, which == 0, low)


def third_kernel(chunks, own, other, key_hbm, value_hbm, cosine, sine, kv, rows, done, w_key, w_value, total, sems):
    wide = w_key.shape[1]
    copies = load_columns(wide, (key_hbm, value_hbm), (w_key, w_value), sems, chunks)
    mine, theirs = halves(own.shape[0])
    rows[mine, :] = own[...]
    rows[theirs, :] = other[...]
    done[...] = jnp.zeros_like(done)
    everything = slice(0, rows.shape[0])

    def put(which, product):
        put_block(kv, everything, product, cosine, sine, which == 0, which * wide)

    piecewise_product(rows, copies, (w_key, w_value), total, put)


def query_kernel(rows, weight, cosine, sine, after, query, done):
    del after
    done[...] = jnp.zeros_like(done)
    wide = 4 * HEAD_SIZE
    for number in range(weight.shape[1] // wide):
        result = dot(rows[...], weight[:, number * wide : (number + 1) * wide])
        for head in range(wide // HEAD_SIZE):
            at = slice(head * HEAD_SIZE, (head + 1) * HEAD_SIZE)
            out = slice(number * wide + head * HEAD_SIZE, number * wide + (head + 1) * HEAD_SIZE)
            query[:, out] = rotated(result[:, at], cosine[...], sine[...]).astype(query.dtype)


def relay_kernel(ways, own, earlier, after, *outs):
    del after
    index = lax.axis_index("seq")
    mine, theirs = own[...], earlier[...]
    for way, out in zip(ways, outs):
        upper = index % 2 > 0 if way == 1 else index % LAYER >= 2
        out[...] = jnp.where(upper, theirs, mine)


def column(number):
    return slice(number * HEAD_SIZE, (number + 1) * HEAD_SIZE)


def fill_bias(bias, distances, starts):
    tokens = bias.shape[0]
    index = lax.axis_index("seq")
    base = index * tokens
    query_pos = base + lax.broadcasted_iota(jnp.int32, (tokens, tokens), 0)
    start = jnp.concatenate([starts[...]] * (tokens // starts.shape[1]), axis=1)
    for number, (even, odd) in enumerate(distances):
        first = base - tokens * jnp.where(index % 2 > 0, odd, even)
        key_pos = first + lax.broadcasted_iota(jnp.int32, (tokens, tokens), 1)
        allowed = (key_pos >= start) & (key_pos <= query_pos)
        bias[:, number * tokens : (number + 1) * tokens] = jnp.where(allowed, 0.0, MASKED)


def scores_of(query, keys, bias, head, at):
    tokens = bias.shape[0]
    return [
        lax.dot_general(
            query[:, column(head)], key[:, column(at)], (((1,), (1,)), ((), ())), preferred_element_type=jnp.float32
        )
        * SCORE_SCALE
        + bias[:, number * tokens : (number + 1) * tokens]
        for number, key in enumerate(keys)
    ]


def weighted(weights, blocks, at, ones):
    product = None
    for weight, block in zip(weights, blocks):
        term = dot(weight, jnp.concatenate([block[:, column(at)], ones], axis=1))
        product = term if product is None else product + term
    return product[:, :HEAD_SIZE], product[:, HEAD_SIZE:]


def row_max(scores):
    return jnp.max(functools.reduce(jnp.maximum, scores), axis=1, keepdims=True)


def near_kernel(distances, starts, query, *refs):
    count = len(distances)
    tops, totals, accs, bias = refs[-4:]
    parts = [refs[low : low + count] for low in range(0, len(refs) - 4, count)]
    fill_bias(bias, distances, starts)
    tokens = query.shape[0]
    heads = query.shape[1] // HEAD_SIZE
    kv_part = parts[0][0].shape[1] // (2 * HEAD_SIZE)
    group = heads // (kv_part * len(parts))
    ones = jnp.ones((tokens, HEAD_SIZE), query.dtype)

    def place(head):
        return parts[head // group // kv_part], head // group % kv_part

    def ask(head):
        blocks, at = place(head)
        return scores_of(query, blocks, bias, head, at)

    scores = ask(0)
    for head in range(heads):
        ahead = ask(head + 1) if head + 1 < heads else None
        top = row_max(scores)
        blocks, at = place(head)
        weights = [jnp.exp2(score - top).astype(query.dtype) for score in scores]
        tops[head] = jnp.broadcast_to(top, (tokens, HEAD_SIZE))
        accs[head], totals[head] = weighted(weights, blocks, kv_part + at, ones)
        scores = ahead


def join(scores, blocks, at, state, head, ones, dtype):
    tops, totals, accs = state
    before = tops[head]
    tokens = before.shape[0]
    top = jnp.maximum(jnp.broadcast_to(row_max(scores), before.shape), before)
    factor = jnp.exp2(before - top)
    wide_top = jnp.concatenate([top] * (tokens // HEAD_SIZE), axis=1)
    weights = [jnp.exp2(score - wide_top).astype(dtype) for score in scores]
    acc, total = weighted(weights, blocks, at, ones)
    return top, totals[head] * factor + total, accs[head] * factor + acc


def attend_far(low, skip, query, blocks, state, bias, put):
    tokens = query.shape[0]
    kv_part = blocks[0].shape[1] // (2 * HEAD_SIZE)
    heads = query.shape[1] // HEAD_SIZE // 2
    group = heads // kv_part
    ones = jnp.ones((tokens, HEAD_SIZE), query.dtype)
    scores = scores_of(query, blocks, bias, low, 0)
    for head in range(heads):
        ahead = scores_of(query, blocks, bias, low + head + 1, (head + 1) // group) if head + 1 < heads else None
        put(head, *join(scores, blocks, kv_part + head // group, state, skip + head, ones, query.dtype))
        scores = ahead


def into(attended):
    def put(head, top, total, acc):
        del top
        attended[:, column(head)] = (acc / total).astype(attended.dtype)

    return put


WIDE = 4 * HEAD_SIZE


def mix_first_kernel(distances, starts, query, *refs):
    far = len(distances)
    blocks, state, (weight, summed, attended, bias) = refs[:far], refs[far : far + 3], refs[far + 3 :]
    fill_bias(bias, distances, starts)
    attend_far(0, 0, query, blocks, state, bias, into(attended))
    depth = attended.shape[1]
    for number in range(summed.shape[1] // WIDE):
        at = slice(number * WIDE, (number + 1) * WIDE)
        summed[:, at] = dot(attended[...], weight[:depth, at])


def middle_kernel(low, query, block, tops, totals, accs, bias, new_tops, new_totals, new_accs):
    def put(head, top, total, acc):
        new_tops[head], new_totals[head], new_accs[head] = top, total, acc

    attend_far(low, low, query, [block], (tops, totals, accs), bias, put)


def rows_product(rows, low, attended, weight, summed, wide):
    depth = attended.shape[1]
    at = slice(low, low + wide)
    return summed[rows, at] + dot(attended[rows, :], weight[depth:, at])


def send_columns(low, attended, weight, summed, send):
    theirs = halves(send.shape[0])[1]
    for number in range(send.shape[1] // WIDE):
        result = rows_product(theirs, low + number * WIDE, attended, weight, summed, WIDE)
        send[:, number * WIDE : (number + 1) * WIDE] = result.astype(send.dtype)


def mix_second_kernel(low, query, *refs):
    blocks, state, (bias, weight, summed, send, attended) = refs[:-8], refs[-8:-5], refs[-5:]
    skipped = bias.shape[1] - len(blocks) * bias.shape[0]
    attend_far(low, 0, query, blocks, state, bias.at[:, pl.ds(skipped, len(blocks) * bias.shape[0])], into(attended))
    send_columns(0, attended, weight, summed, send)


def own_high_kernel(low, attended, weight, summed, own):
    mine = halves(own.shape[0])[0]
    for number in range(own.shape[1] // WIDE):
        result = rows_product(mine, low + number * WIDE, attended, weight, summed, WIDE)
        own[:, number * WIDE : (number + 1) * WIDE] = result


def own_low_kernel(attended, weight, summed, got, after, mixed):
    del after
    mine = halves(got.shape[0])[0]
    for number in range(got.shape[1] // WIDE):
        at = slice(number * WIDE, (number + 1) * WIDE)
        result = rows_product(mine, number * WIDE, attended, weight, summed, WIDE)
        mixed[:, at] = (result + got[:, at].astype(jnp.float32)).astype(mixed.dtype)


def add_kernel(mixed_low, own, got, mixed_hbm, mixed, sems):
    low = mixed_low.shape[1]
    copies = [pltpu.make_async_copy(mixed_low, mixed_hbm.at[:, pl.ds(0, low)], sems.at[0])]
    copies[0].start()
    for number in range(own.shape[1] // WIDE):
        at = slice(number * WIDE, (number + 1) * WIDE)
        mixed[:, at] = (own[:, at] + got[:, at].astype(jnp.float32)).astype(mixed.dtype)
        there = mixed_hbm.at[:, pl.ds(low + number * WIDE, WIDE)]
        copies.append(pltpu.make_async_copy(mixed.at[:, pl.ds(number * WIDE, WIDE)], there, sems.at[number + 1]))
        copies[-1].start()
    for copy in copies:
        copy.wait()


def call(kernel, name, outs, in_specs, flops, nbytes, limit, scratch=(), out_specs=None):
    return pl.pallas_call(
        kernel,
        out_shape=outs,
        in_specs=in_specs,
        out_specs=out_specs or [VMEM] * len(outs),
        scratch_shapes=list(scratch),
        name=name,
        cost_estimate=pl.CostEstimate(flops=flops, bytes_accessed=nbytes, transcendentals=0),
        compiler_params=pltpu.CompilerParams(vmem_limit_bytes=limit << 20),
    )


def in_hbm(array):
    return pltpu.with_memory_space_constraint(array, pltpu.HBM)


def body(input_rows, doc_lengths, w_query, key_weight, value_weight, w_out):
    half, model = input_rows.shape
    tokens = 2 * half
    width_q, width_k = w_query.shape[1], key_weight.shape[1]
    heads = width_q // HEAD_SIZE
    shards = lax.axis_size("seq")
    bf16, f32 = jnp.bfloat16, jnp.float32
    shape = pltpu.VMEM

    other = lax.ppermute(input_rows, "head", SWAP)

    flag = shape((8, HEAD_SIZE), f32)
    table = shape((tokens, HEAD_SIZE), f32)
    part = width_k // 2
    kv_shape = shape((tokens, 2 * part), bf16)
    part_shape = shape((model, part), bf16)
    chunks = 4
    kv_flops = 4 * half * model * part
    total, own, w_key, w_value, cosine, sine, starts = call(
        functools.partial(first_kernel, chunks), "keys_values_own",
        [
            shape((half, 2 * part), f32), shape((half, model), bf16), part_shape, part_shape,
            table, table, shape((tokens, HEAD_SIZE), jnp.int32),
        ],
        [ANY] * 4, kv_flops, 2 * model * width_k, 4,
        [pltpu.SMEM(doc_lengths.shape, jnp.int32), pltpu.SemaphoreType.DMA((2 * chunks + 2,))],
    )(in_hbm(doc_lengths), in_hbm(input_rows), in_hbm(key_weight), in_hbm(value_weight))
    (kv_a,) = call(
        second_kernel, "keys_values", [kv_shape], [VMEM] * 6, kv_flops, 2 * model * width_k, 4,
    )(other, w_key, w_value, total, cosine, sine)

    every = range(shards)
    step_z = [(i, (i + LAYER) % shards) for i in every]
    z_a = lax.ppermute(kv_a, "seq", [(a, b) for a, b in step_z if a < b])

    kv_b, rows, done = call(
        functools.partial(third_kernel, chunks), "keys_values_more", [kv_shape, shape((tokens, model), bf16), flag],
        [VMEM, VMEM, ANY, ANY, VMEM, VMEM], VALUES_COST, 2 * model * width_k, 10,
        [part_shape, part_shape, pltpu.VMEM((tokens, 2 * part), f32), pltpu.SemaphoreType.DMA((2 * chunks,))],
    )(own, other, in_hbm(key_weight), in_hbm(value_weight), cosine, sine)
    z_b = lax.ppermute(kv_b, "seq", step_z)

    def exchange(mine, earlier, after, ways, cost):
        to = call(
            functools.partial(relay_kernel, ways), "relay", [kv_shape] * len(ways), [VMEM] * 3, cost, 2 << 20, 4,
        )(mine, earlier, after)
        return [lax.ppermute(array, "seq", [(i, i ^ way) for i in every]) for way, array in zip(ways, to)], to[0]

    (x_a, y_a, d_a), done = exchange(kv_a, z_a, kv_b, (1, 2, 3), RELAY_COST)
    far_a = d_a, x_a, y_a
    query, done = call(
        query_kernel, "queries", [shape((tokens, width_q), bf16), flag], [VMEM] * 5,
        2 * tokens * model * width_q, 2 * model * width_q, 8,
    )(rows, w_query, cosine, sine, done)
    (d_b,), _ = exchange(kv_b, z_b, done, (3,), 9 << 30)
    near = call(
        functools.partial(near_kernel, ((0, 0), (LAYER, LAYER))), "scores_near", [shape((heads, tokens, HEAD_SIZE), f32)] * 3,
        [VMEM] * 6, 8 * heads * tokens * tokens * HEAD_SIZE, 8 << 20, 12, [pltpu.VMEM((tokens, 2 * tokens), f32)],
    )(starts, query, kv_a, z_a, kv_b, z_b)
    (x_b, y_b), _ = exchange(kv_b, z_b, near[0], (1, 2), 0)
    far_b = d_b, x_b, y_b

    far = len(far_a)
    distances = ((1, 3), (3, 1), (2, 2))
    bias_shape = shape((tokens, far * tokens), f32)
    columns = w_out.shape[1]
    attended_shape = shape((tokens, width_q // 2), bf16)
    far_flops = 3 * far * heads * tokens * tokens * HEAD_SIZE
    out_flops = tokens * width_q * columns
    summed, _, bias = call(
        functools.partial(mix_first_kernel, distances), "mix_first",
        [shape((tokens, columns), f32), attended_shape, bias_shape],
        [VMEM] * (6 + far), out_flops + far_flops, 4 << 20, 10,
    )(starts, query, *far_a, *near, w_out)
    middle = call(
        functools.partial(middle_kernel, heads // 2), "attend_middle", [shape((heads // 2, tokens, HEAD_SIZE), f32)] * 3,
        [VMEM] * 6, far_flops // far, 4 << 20, 10,
    )(query, far_b[0], *near, bias)

    cut = columns // 2
    send_shape = shape((half, cut), bf16)
    quarter = out_flops // 4
    send, attended = call(
        functools.partial(mix_second_kernel, heads // 2), "mix_second", [send_shape, attended_shape],
        [VMEM] * (6 + far), quarter + far_flops, 4 << 20, 10,
    )(query, *far_b[1:], *middle, bias, w_out, summed)
    got_low = lax.ppermute(send, "head", SWAP)
    (send,) = call(
        functools.partial(send_columns, cut), "send_high", [send_shape], [VMEM] * 3, quarter, 4 << 20, 6,
    )(attended, w_out, summed)
    got_high = lax.ppermute(send, "head", SWAP)
    (own,) = call(
        functools.partial(own_high_kernel, cut), "own_high", [shape((half, columns - cut), f32)], [VMEM] * 3,
        quarter, 4 << 20, 6,
    )(attended, w_out, summed)
    (mixed,) = call(
        own_low_kernel, "own_low", [send_shape], [VMEM] * 5, quarter, 4 << 20, 6,
    )(attended, w_out, summed, got_low, own)
    (mixed,) = call(
        add_kernel, "add", [pltpu.HBM((half, columns), bf16)], [VMEM] * 3, half * cut, 4 << 20, 4,
        [pltpu.VMEM((half, columns - cut), bf16), pltpu.SemaphoreType.DMA(((columns - cut) // WIDE + 1,))], [ANY],
    )(mixed, own, got_high)
    return mixed


def solution(mesh):
    in_specs = (
        P(("seq", "head"), None),
        P(),
        P(None, "head"),
        P(None, "head"),
        P(None, "head"),
        P("head", None),
    )
    out_specs = P(("seq", "head"), None)
    return jax.shard_map(body, mesh=mesh, in_specs=in_specs, out_specs=out_specs, check_vma=False)
```

```python
import functools
import math

import jax
import jax.numpy as jnp
from jax import lax
from jax.experimental import pallas as pl
from jax.experimental.pallas import tpu as pltpu
from jax.sharding import PartitionSpec as P

HEAD_SIZE = 128
LAYER = 4
MASKED = -1e30
VALUES_COST = 4 << 30
RELAY_COST = 5 << 30
SCORE_SCALE = math.log2(math.e) * HEAD_SIZE ** (-0.5)
SWAP = [(0, 1), (1, 0)]
VMEM = pl.BlockSpec(memory_space=pltpu.VMEM)
ANY = pl.BlockSpec(memory_space=pl.ANY)


def inverse_frequency():
    table = []
    for number in range(HEAD_SIZE // 2):
        base_freq = 500000.0 ** (-(2.0 * number) / HEAD_SIZE)
        wavelength = 2.0 * math.pi / base_freq
        smooth = (8192.0 / wavelength - 1.0) / 3.0
        if wavelength < 2048.0:
            table.append(base_freq)
        elif wavelength > 8192.0:
            table.append(base_freq / 8.0)
        else:
            table.append((1.0 - smooth) * base_freq / 8.0 + smooth * base_freq)
    return table


def dot(a, b):
    return jnp.dot(a, b, preferred_element_type=jnp.float32)


def rotated(block, cosine, sine):
    return block * cosine + pltpu.roll(block, HEAD_SIZE // 2, 1) * sine


def load_columns(low, hbms, buffers, sems, chunks):
    depth, wide = buffers[0].shape[0] // chunks, buffers[0].shape[1]
    copies = []
    for number in range(chunks):
        at = pl.ds(number * depth, depth)
        pair = [
            pltpu.make_async_copy(hbm.at[at, pl.ds(low, wide)], buffer.at[at], sems.at[number * len(hbms) + which])
            for which, (hbm, buffer) in enumerate(zip(hbms, buffers))
        ]
        for copy in pair:
            copy.start()
        copies.append(pair)
    return copies


def piecewise_product(rows, copies, buffers, total, put=None):
    depth, wide = buffers[0].shape[0] // len(copies), buffers[0].shape[1]
    for number, pair in enumerate(copies):
        at = slice(number * depth, (number + 1) * depth)
        for which, (copy, buffer) in enumerate(zip(pair, buffers)):
            copy.wait()
            columns = slice(which * wide, (which + 1) * wide)
            product = dot(rows[:, at], buffer[at, :])
            if number > 0:
                product = product + total[:, columns]
            if put is None or number < len(copies) - 1:
                total[:, columns] = product
            else:
                put(which, product)


def first_kernel(chunks, lengths_hbm, own_hbm, key_hbm, value_hbm, total, own, w_key, w_value, cosine, sine, starts, lengths, sems):
    row_copy = pltpu.make_async_copy(own_hbm, own, sems.at[2 * chunks])
    row_copy.start()
    copies = load_columns(0, (key_hbm, value_hbm), (w_key, w_value), sems, chunks)
    tokens = cosine.shape[0]
    length_copy = pltpu.make_async_copy(lengths_hbm, lengths, sems.at[2 * chunks + 1])
    length_copy.start()
    lane = lax.broadcasted_iota(jnp.int32, (1, HEAD_SIZE), 1)
    pair_of_lane = lane % (HEAD_SIZE // 2)
    freq = jnp.zeros((1, HEAD_SIZE), jnp.float32)
    for number, value in enumerate(inverse_frequency()):
        freq = jnp.where(pair_of_lane == number, jnp.float32(value), freq)
    first = lax.axis_index("seq") * tokens
    half = tokens // 2
    low_lane = lane < HEAD_SIZE // 2
    packed = first + lax.broadcasted_iota(jnp.int32, (half, HEAD_SIZE), 0) + jnp.where(low_lane, 0, half)
    angles = packed.astype(jnp.float32) * freq
    turned = jnp.cos(angles)
    other = pltpu.roll(turned, HEAD_SIZE // 2, 1)
    cosine[:half, :] = jnp.where(low_lane, turned, other)
    cosine[half:, :] = jnp.where(low_lane, other, turned)
    turned = jnp.sin(angles)
    other = pltpu.roll(turned, HEAD_SIZE // 2, 1)
    sine[:half, :] = jnp.where(low_lane, -turned, other)
    sine[half:, :] = jnp.where(low_lane, -other, turned)
    positions = first + lax.broadcasted_iota(jnp.int32, (tokens, HEAD_SIZE), 0)
    length_copy.wait()
    start = jnp.zeros((tokens, HEAD_SIZE), jnp.int32)
    end = jnp.int32(0)
    for number in range(lengths.shape[0]):
        end = end + lengths[number]
        start = jnp.where(positions >= end, end, start)
    starts[...] = start
    row_copy.wait()
    piecewise_product(own, copies, (w_key, w_value), total)


def halves(half):
    core = lax.axis_index("head")
    return pl.ds(pl.multiple_of(core * half, half), half), pl.ds(pl.multiple_of((1 - core) * half, half), half)


def put_block(kv, here, block, cosine, sine, is_key, low):
    for head in range(block.shape[1] // HEAD_SIZE):
        piece = block[:, head * HEAD_SIZE : (head + 1) * HEAD_SIZE]
        if is_key:
            piece = rotated(piece, cosine[here, :], sine[here, :])
        kv[here, low + head * HEAD_SIZE : low + (head + 1) * HEAD_SIZE] = piece.astype(kv.dtype)


def second_kernel(other, w_key, w_value, own_total, cosine, sine, kv):
    half, wide = own_total.shape[0], w_key.shape[1]
    mine, theirs = halves(half)
    for which, weight in enumerate((w_key, w_value)):
        low = which * wide
        put_block(kv, mine, own_total[:, low : low + wide], cosine, sine, which == 0, low)
        put_block(kv, theirs, dot(other[...], weight[...]), cosine, sine, which == 0, low)


def third_kernel(chunks, own, other, key_hbm, value_hbm, cosine, sine, kv, rows, done, w_key, w_value, total, sems):
    wide = w_key.shape[1]
    copies = load_columns(wide, (key_hbm, value_hbm), (w_key, w_value), sems, chunks)
    mine, theirs = halves(own.shape[0])
    rows[mine, :] = own[...]
    rows[theirs, :] = other[...]
    done[...] = jnp.zeros_like(done)
    everything = slice(0, rows.shape[0])

    def put(which, product):
        put_block(kv, everything, product, cosine, sine, which == 0, which * wide)

    piecewise_product(rows, copies, (w_key, w_value), total, put)


def query_kernel(rows, weight, cosine, sine, after, query, done):
    del after
    done[...] = jnp.zeros_like(done)
    wide = 4 * HEAD_SIZE
    for number in range(weight.shape[1] // wide):
        result = dot(rows[...], weight[:, number * wide : (number + 1) * wide])
        for head in range(wide // HEAD_SIZE):
            at = slice(head * HEAD_SIZE, (head + 1) * HEAD_SIZE)
            out = slice(number * wide + head * HEAD_SIZE, number * wide + (head + 1) * HEAD_SIZE)
            query[:, out] = rotated(result[:, at], cosine[...], sine[...]).astype(query.dtype)


def relay_kernel(ways, own, earlier, after, *outs):
    del after
    index = lax.axis_index("seq")
    mine, theirs = own[...], earlier[...]
    for way, out in zip(ways, outs):
        upper = index % 2 > 0 if way == 1 else index % LAYER >= 2
        out[...] = jnp.where(upper, theirs, mine)


def column(number):
    return slice(number * HEAD_SIZE, (number + 1) * HEAD_SIZE)


def fill_bias(bias, distances, starts):
    tokens = bias.shape[0]
    index = lax.axis_index("seq")
    base = index * tokens
    query_pos = base + lax.broadcasted_iota(jnp.int32, (tokens, tokens), 0)
    start = jnp.concatenate([starts[...]] * (tokens // starts.shape[1]), axis=1)
    for number, (even, odd) in enumerate(distances):
        first = base - tokens * jnp.where(index % 2 > 0, odd, even)
        key_pos = first + lax.broadcasted_iota(jnp.int32, (tokens, tokens), 1)
        allowed = (key_pos >= start) & (key_pos <= query_pos)
        bias[:, number * tokens : (number + 1) * tokens] = jnp.where(allowed, 0.0, MASKED)


def scores_of(query, keys, bias, head, at):
    tokens = bias.shape[0]
    return [
        lax.dot_general(
            query[:, column(head)], key[:, column(at)], (((1,), (1,)), ((), ())), preferred_element_type=jnp.float32
        )
        * SCORE_SCALE
        + bias[:, number * tokens : (number + 1) * tokens]
        for number, key in enumerate(keys)
    ]


def weighted(weights, blocks, at, ones):
    product = None
    for weight, block in zip(weights, blocks):
        term = dot(weight, jnp.concatenate([block[:, column(at)], ones], axis=1))
        product = term if product is None else product + term
    return product[:, :HEAD_SIZE], product[:, HEAD_SIZE:]


def row_max(scores):
    return jnp.max(functools.reduce(jnp.maximum, scores), axis=1, keepdims=True)


def near_kernel(distances, starts, query, *refs):
    count = len(distances)
    tops, totals, accs, bias = refs[-4:]
    parts = [refs[low : low + count] for low in range(0, len(refs) - 4, count)]
    fill_bias(bias, distances, starts)
    tokens = query.shape[0]
    heads = query.shape[1] // HEAD_SIZE
    kv_part = parts[0][0].shape[1] // (2 * HEAD_SIZE)
    group = heads // (kv_part * len(parts))
    ones = jnp.ones((tokens, HEAD_SIZE), query.dtype)

    def place(head):
        return parts[head // group // kv_part], head // group % kv_part

    def ask(head):
        blocks, at = place(head)
        return scores_of(query, blocks, bias, head, at)

    scores = ask(0)
    for head in range(heads):
        ahead = ask(head + 1) if head + 1 < heads else None
        top = row_max(scores)
        blocks, at = place(head)
        weights = [jnp.exp2(score - top).astype(query.dtype) for score in scores]
        tops[head] = jnp.broadcast_to(top, (tokens, HEAD_SIZE))
        accs[head], totals[head] = weighted(weights, blocks, kv_part + at, ones)
        scores = ahead


def join(scores, blocks, at, state, head, ones, dtype):
    tops, totals, accs = state
    before = tops[head]
    tokens = before.shape[0]
    top = jnp.maximum(jnp.broadcast_to(row_max(scores), before.shape), before)
    factor = jnp.exp2(before - top)
    wide_top = jnp.concatenate([top] * (tokens // HEAD_SIZE), axis=1)
    weights = [jnp.exp2(score - wide_top).astype(dtype) for score in scores]
    acc, total = weighted(weights, blocks, at, ones)
    return top, totals[head] * factor + total, accs[head] * factor + acc


def attend_far(low, skip, query, blocks, state, bias, put):
    tokens = query.shape[0]
    kv_part = blocks[0].shape[1] // (2 * HEAD_SIZE)
    heads = query.shape[1] // HEAD_SIZE // 2
    group = heads // kv_part
    ones = jnp.ones((tokens, HEAD_SIZE), query.dtype)
    scores = scores_of(query, blocks, bias, low, 0)
    for head in range(heads):
        ahead = scores_of(query, blocks, bias, low + head + 1, (head + 1) // group) if head + 1 < heads else None
        put(head, *join(scores, blocks, kv_part + head // group, state, skip + head, ones, query.dtype))
        scores = ahead


def into(attended):
    def put(head, top, total, acc):
        del top
        attended[:, column(head)] = (acc / total).astype(attended.dtype)

    return put


WIDE = 4 * HEAD_SIZE


def mix_first_kernel(distances, starts, query, *refs):
    far = len(distances)
    blocks, state, (weight, summed, attended, bias) = refs[:far], refs[far : far + 3], refs[far + 3 :]
    fill_bias(bias, distances, starts)
    attend_far(0, 0, query, blocks, state, bias, into(attended))
    depth = attended.shape[1]
    for number in range(summed.shape[1] // WIDE):
        at = slice(number * WIDE, (number + 1) * WIDE)
        summed[:, at] = dot(attended[...], weight[:depth, at])


def middle_kernel(low, query, first, second, tops, totals, accs, bias, new_tops, new_totals, new_accs):
    tokens = bias.shape[0]
    late = bias.at[:, pl.ds(bias.shape[1] - 2 * tokens, 2 * tokens)]

    def put(head, top, total, acc):
        new_tops[head], new_totals[head], new_accs[head] = top, total, acc

    attend_far(low, low, query, [first, second], (tops, totals, accs), late, put)


def rows_product(rows, low, attended, weight, summed, wide):
    depth = attended.shape[1]
    at = slice(low, low + wide)
    return summed[rows, at] + dot(attended[rows, :], weight[depth:, at])


def send_columns(low, attended, weight, summed, send):
    theirs = halves(send.shape[0])[1]
    for number in range(send.shape[1] // WIDE):
        result = rows_product(theirs, low + number * WIDE, attended, weight, summed, WIDE)
        send[:, number * WIDE : (number + 1) * WIDE] = result.astype(send.dtype)


def mix_second_kernel(low, query, block, tops, totals, accs, bias, weight, summed, send, attended):
    first = bias.at[:, pl.ds(0, bias.shape[0])]
    attend_far(low, 0, query, [block], (tops, totals, accs), first, into(attended))
    send_columns(0, attended, weight, summed, send)


def own_high_kernel(low, attended, weight, summed, own):
    mine = halves(own.shape[0])[0]
    for number in range(own.shape[1] // WIDE):
        result = rows_product(mine, low + number * WIDE, attended, weight, summed, WIDE)
        own[:, number * WIDE : (number + 1) * WIDE] = result


def own_low_kernel(attended, weight, summed, got, after, mixed):
    del after
    mine = halves(got.shape[0])[0]
    for number in range(got.shape[1] // WIDE):
        at = slice(number * WIDE, (number + 1) * WIDE)
        result = rows_product(mine, number * WIDE, attended, weight, summed, WIDE)
        mixed[:, at] = (result + got[:, at].astype(jnp.float32)).astype(mixed.dtype)


def add_kernel(mixed_low, own, got, mixed_hbm, mixed, sems):
    low = mixed_low.shape[1]
    copies = [pltpu.make_async_copy(mixed_low, mixed_hbm.at[:, pl.ds(0, low)], sems.at[0])]
    copies[0].start()
    for number in range(own.shape[1] // WIDE):
        at = slice(number * WIDE, (number + 1) * WIDE)
        mixed[:, at] = (own[:, at] + got[:, at].astype(jnp.float32)).astype(mixed.dtype)
        there = mixed_hbm.at[:, pl.ds(low + number * WIDE, WIDE)]
        copies.append(pltpu.make_async_copy(mixed.at[:, pl.ds(number * WIDE, WIDE)], there, sems.at[number + 1]))
        copies[-1].start()
    for copy in copies:
        copy.wait()


def call(kernel, name, outs, in_specs, flops, nbytes, limit, scratch=(), out_specs=None):
    return pl.pallas_call(
        kernel,
        out_shape=outs,
        in_specs=in_specs,
        out_specs=out_specs or [VMEM] * len(outs),
        scratch_shapes=list(scratch),
        name=name,
        cost_estimate=pl.CostEstimate(flops=flops, bytes_accessed=nbytes, transcendentals=0),
        compiler_params=pltpu.CompilerParams(vmem_limit_bytes=limit << 20),
    )


def in_hbm(array):
    return pltpu.with_memory_space_constraint(array, pltpu.HBM)


def body(input_rows, doc_lengths, w_query, key_weight, value_weight, w_out):
    half, model = input_rows.shape
    tokens = 2 * half
    width_q, width_k = w_query.shape[1], key_weight.shape[1]
    heads = width_q // HEAD_SIZE
    shards = lax.axis_size("seq")
    bf16, f32 = jnp.bfloat16, jnp.float32
    shape = pltpu.VMEM

    other = lax.ppermute(input_rows, "head", SWAP)

    flag = shape((8, HEAD_SIZE), f32)
    table = shape((tokens, HEAD_SIZE), f32)
    part = width_k // 2
    kv_shape = shape((tokens, 2 * part), bf16)
    part_shape = shape((model, part), bf16)
    chunks = 2
    kv_flops = 4 * half * model * part
    total, own, w_key, w_value, cosine, sine, starts = call(
        functools.partial(first_kernel, chunks), "keys_values_own",
        [
            shape((half, 2 * part), f32), shape((half, model), bf16), part_shape, part_shape,
            table, table, shape((tokens, HEAD_SIZE), jnp.int32),
        ],
        [ANY] * 4, kv_flops, 2 * model * width_k, 4,
        [pltpu.SMEM(doc_lengths.shape, jnp.int32), pltpu.SemaphoreType.DMA((2 * chunks + 2,))],
    )(in_hbm(doc_lengths), in_hbm(input_rows), in_hbm(key_weight), in_hbm(value_weight))
    (kv_a,) = call(
        second_kernel, "keys_values", [kv_shape], [VMEM] * 6, kv_flops, 2 * model * width_k, 4,
    )(other, w_key, w_value, total, cosine, sine)

    every = range(shards)
    step_z = [(i, (i + LAYER) % shards) for i in every]
    z_a = lax.ppermute(kv_a, "seq", [(a, b) for a, b in step_z if a < b])

    kv_b, rows, done = call(
        functools.partial(third_kernel, chunks), "keys_values_more", [kv_shape, shape((tokens, model), bf16), flag],
        [VMEM, VMEM, ANY, ANY, VMEM, VMEM], VALUES_COST, 2 * model * width_k, 10,
        [part_shape, part_shape, pltpu.VMEM((tokens, 2 * part), f32), pltpu.SemaphoreType.DMA((2 * chunks,))],
    )(own, other, in_hbm(key_weight), in_hbm(value_weight), cosine, sine)
    z_b = lax.ppermute(kv_b, "seq", step_z)

    def exchange(mine, earlier, after, ways, cost):
        to = call(
            functools.partial(relay_kernel, ways), "relay", [kv_shape] * len(ways), [VMEM] * 3, cost, 2 << 20, 4,
        )(mine, earlier, after)
        return [lax.ppermute(array, "seq", [(i, i ^ way) for i in every]) for way, array in zip(ways, to)], to[0]

    (x_a, y_a, d_a), done = exchange(kv_a, z_a, kv_b, (1, 2, 3), RELAY_COST)
    far_a = d_a, x_a, y_a
    query, done = call(
        query_kernel, "queries", [shape((tokens, width_q), bf16), flag], [VMEM] * 5,
        2 * tokens * model * width_q, 2 * model * width_q, 8,
    )(rows, w_query, cosine, sine, done)
    (x_b, y_b), _ = exchange(kv_b, z_b, done, (1, 2), 9 << 30)
    near = call(
        functools.partial(near_kernel, ((0, 0), (LAYER, LAYER))), "scores_near", [shape((heads, tokens, HEAD_SIZE), f32)] * 3,
        [VMEM] * 6, 8 * heads * tokens * tokens * HEAD_SIZE, 8 << 20, 12, [pltpu.VMEM((tokens, 2 * tokens), f32)],
    )(starts, query, kv_a, z_a, kv_b, z_b)
    (d_b,), _ = exchange(kv_b, z_b, near[0], (3,), 0)

    far = len(far_a)
    distances = ((1, 3), (3, 1), (2, 2))
    bias_shape = shape((tokens, far * tokens), f32)
    columns = w_out.shape[1]
    attended_shape = shape((tokens, width_q // 2), bf16)
    far_flops = 3 * far * heads * tokens * tokens * HEAD_SIZE
    out_flops = tokens * width_q * columns
    summed, _, bias = call(
        functools.partial(mix_first_kernel, distances), "mix_first",
        [shape((tokens, columns), f32), attended_shape, bias_shape],
        [VMEM] * (6 + far), out_flops + far_flops, 4 << 20, 10,
    )(starts, query, *far_a, *near, w_out)
    middle = call(
        functools.partial(middle_kernel, heads // 2), "attend_middle", [shape((heads // 2, tokens, HEAD_SIZE), f32)] * 3,
        [VMEM] * 7, far_flops // far * 2, 4 << 20, 10,
    )(query, x_b, y_b, *near, bias)

    cut = columns // 2
    send_shape = shape((half, cut), bf16)
    quarter = out_flops // 4
    send, attended = call(
        functools.partial(mix_second_kernel, heads // 2), "mix_second", [send_shape, attended_shape],
        [VMEM] * 8, quarter + far_flops // far, 4 << 20, 10,
    )(query, d_b, *middle, bias, w_out, summed)
    got_low = lax.ppermute(send, "head", SWAP)
    (send,) = call(
        functools.partial(send_columns, cut), "send_high", [send_shape], [VMEM] * 3, quarter, 4 << 20, 6,
    )(attended, w_out, summed)
    got_high = lax.ppermute(send, "head", SWAP)
    (own,) = call(
        functools.partial(own_high_kernel, cut), "own_high", [shape((half, columns - cut), f32)], [VMEM] * 3,
        quarter, 4 << 20, 6,
    )(attended, w_out, summed)
    (mixed,) = call(
        own_low_kernel, "own_low", [send_shape], [VMEM] * 5, quarter, 4 << 20, 6,
    )(attended, w_out, summed, got_low, own)
    (mixed,) = call(
        add_kernel, "add", [pltpu.HBM((half, columns), bf16)], [VMEM] * 3, half * cut, 4 << 20, 4,
        [pltpu.VMEM((half, columns - cut), bf16), pltpu.SemaphoreType.DMA(((columns - cut) // WIDE + 1,))], [ANY],
    )(mixed, own, got_high)
    return mixed


def solution(mesh):
    in_specs = (
        P(("seq", "head"), None),
        P(),
        P(None, "head"),
        P(None, "head"),
        P(None, "head"),
        P("head", None),
    )
    out_specs = P(("seq", "head"), None)
    return jax.shard_map(body, mesh=mesh, in_specs=in_specs, out_specs=out_specs, check_vma=False)
```

```python
import functools
import math

import jax
import jax.numpy as jnp
from jax import lax
from jax.experimental import pallas as pl
from jax.experimental.pallas import tpu as pltpu
from jax.sharding import PartitionSpec as P

HEAD_SIZE = 128
LAYER = 4
MASKED = -1e30
VALUES_COST = 4 << 30
RELAY_COST = 5 << 30
SCORE_SCALE = math.log2(math.e) * HEAD_SIZE ** (-0.5)
SWAP = [(0, 1), (1, 0)]
VMEM = pl.BlockSpec(memory_space=pltpu.VMEM)
ANY = pl.BlockSpec(memory_space=pl.ANY)


def inverse_frequency():
    table = []
    for number in range(HEAD_SIZE // 2):
        base_freq = 500000.0 ** (-(2.0 * number) / HEAD_SIZE)
        wavelength = 2.0 * math.pi / base_freq
        smooth = (8192.0 / wavelength - 1.0) / 3.0
        if wavelength < 2048.0:
            table.append(base_freq)
        elif wavelength > 8192.0:
            table.append(base_freq / 8.0)
        else:
            table.append((1.0 - smooth) * base_freq / 8.0 + smooth * base_freq)
    return table


def dot(a, b):
    return jnp.dot(a, b, preferred_element_type=jnp.float32)


def rotated(block, cosine, sine):
    return block * cosine + pltpu.roll(block, HEAD_SIZE // 2, 1) * sine


def load_columns(low, hbms, buffers, sems, chunks):
    depth, wide = buffers[0].shape[0] // chunks, buffers[0].shape[1]
    copies = []
    for number in range(chunks):
        at = pl.ds(number * depth, depth)
        pair = [
            pltpu.make_async_copy(hbm.at[at, pl.ds(low, wide)], buffer.at[at], sems.at[number * len(hbms) + which])
            for which, (hbm, buffer) in enumerate(zip(hbms, buffers))
        ]
        for copy in pair:
            copy.start()
        copies.append(pair)
    return copies


def piecewise_product(rows, copies, buffers, total, put=None):
    depth, wide = buffers[0].shape[0] // len(copies), buffers[0].shape[1]
    for number, pair in enumerate(copies):
        at = slice(number * depth, (number + 1) * depth)
        for which, (copy, buffer) in enumerate(zip(pair, buffers)):
            copy.wait()
            columns = slice(which * wide, (which + 1) * wide)
            product = dot(rows[:, at], buffer[at, :])
            if number > 0:
                product = product + total[:, columns]
            if put is None or number < len(copies) - 1:
                total[:, columns] = product
            else:
                put(which, product)


def first_kernel(chunks, lengths_hbm, own_hbm, key_hbm, value_hbm, total, own, w_key, w_value, cosine, sine, starts, lengths, sems):
    row_copy = pltpu.make_async_copy(own_hbm, own, sems.at[2 * chunks])
    row_copy.start()
    copies = load_columns(0, (key_hbm, value_hbm), (w_key, w_value), sems, chunks)
    tokens = cosine.shape[0]
    length_copy = pltpu.make_async_copy(lengths_hbm, lengths, sems.at[2 * chunks + 1])
    length_copy.start()
    lane = lax.broadcasted_iota(jnp.int32, (1, HEAD_SIZE), 1)
    pair_of_lane = lane % (HEAD_SIZE // 2)
    freq = jnp.zeros((1, HEAD_SIZE), jnp.float32)
    for number, value in enumerate(inverse_frequency()):
        freq = jnp.where(pair_of_lane == number, jnp.float32(value), freq)
    first = lax.axis_index("seq") * tokens
    half = tokens // 2
    low_lane = lane < HEAD_SIZE // 2
    packed = first + lax.broadcasted_iota(jnp.int32, (half, HEAD_SIZE), 0) + jnp.where(low_lane, 0, half)
    angles = packed.astype(jnp.float32) * freq
    turned = jnp.cos(angles)
    other = pltpu.roll(turned, HEAD_SIZE // 2, 1)
    cosine[:half, :] = jnp.where(low_lane, turned, other)
    cosine[half:, :] = jnp.where(low_lane, other, turned)
    turned = jnp.sin(angles)
    other = pltpu.roll(turned, HEAD_SIZE // 2, 1)
    sine[:half, :] = jnp.where(low_lane, -turned, other)
    sine[half:, :] = jnp.where(low_lane, -other, turned)
    positions = first + lax.broadcasted_iota(jnp.int32, (tokens, HEAD_SIZE), 0)
    length_copy.wait()
    start = jnp.zeros((tokens, HEAD_SIZE), jnp.int32)
    end = jnp.int32(0)
    for number in range(lengths.shape[0]):
        end = end + lengths[number]
        start = jnp.where(positions >= end, end, start)
    starts[...] = start
    row_copy.wait()
    piecewise_product(own, copies, (w_key, w_value), total)


def halves(half):
    core = lax.axis_index("head")
    return pl.ds(pl.multiple_of(core * half, half), half), pl.ds(pl.multiple_of((1 - core) * half, half), half)


def put_block(kv, here, block, cosine, sine, is_key, low):
    for head in range(block.shape[1] // HEAD_SIZE):
        piece = block[:, head * HEAD_SIZE : (head + 1) * HEAD_SIZE]
        if is_key:
            piece = rotated(piece, cosine[here, :], sine[here, :])
        kv[here, low + head * HEAD_SIZE : low + (head + 1) * HEAD_SIZE] = piece.astype(kv.dtype)


def second_kernel(other, w_key, w_value, own_total, cosine, sine, kv):
    half, wide = own_total.shape[0], w_key.shape[1]
    mine, theirs = halves(half)
    for which, weight in enumerate((w_key, w_value)):
        low = which * wide
        put_block(kv, mine, own_total[:, low : low + wide], cosine, sine, which == 0, low)
        put_block(kv, theirs, dot(other[...], weight[...]), cosine, sine, which == 0, low)


def third_kernel(chunks, own, other, key_hbm, value_hbm, cosine, sine, kv, rows, done, w_key, w_value, total, sems):
    wide = w_key.shape[1]
    copies = load_columns(wide, (key_hbm, value_hbm), (w_key, w_value), sems, chunks)
    mine, theirs = halves(own.shape[0])
    rows[mine, :] = own[...]
    rows[theirs, :] = other[...]
    done[...] = jnp.zeros_like(done)
    everything = slice(0, rows.shape[0])

    def put(which, product):
        put_block(kv, everything, product, cosine, sine, which == 0, which * wide)

    piecewise_product(rows, copies, (w_key, w_value), total, put)


def query_kernel(rows, weight, cosine, sine, after, query, done):
    del after
    done[...] = jnp.zeros_like(done)
    wide = 4 * HEAD_SIZE
    for number in range(weight.shape[1] // wide):
        result = dot(rows[...], weight[:, number * wide : (number + 1) * wide])
        for head in range(wide // HEAD_SIZE):
            at = slice(head * HEAD_SIZE, (head + 1) * HEAD_SIZE)
            out = slice(number * wide + head * HEAD_SIZE, number * wide + (head + 1) * HEAD_SIZE)
            query[:, out] = rotated(result[:, at], cosine[...], sine[...]).astype(query.dtype)


def relay_kernel(ways, own, earlier, after, *outs):
    del after
    index = lax.axis_index("seq")
    mine, theirs = own[...], earlier[...]
    for way, out in zip(ways, outs):
        upper = index % 2 > 0 if way == 1 else index % LAYER >= 2
        out[...] = jnp.where(upper, theirs, mine)


def column(number):
    return slice(number * HEAD_SIZE, (number + 1) * HEAD_SIZE)


def fill_bias(bias, distances, starts):
    tokens = bias.shape[0]
    index = lax.axis_index("seq")
    base = index * tokens
    query_pos = base + lax.broadcasted_iota(jnp.int32, (tokens, tokens), 0)
    start = jnp.concatenate([starts[...]] * (tokens // starts.shape[1]), axis=1)
    for number, (even, odd) in enumerate(distances):
        first = base - tokens * jnp.where(index % 2 > 0, odd, even)
        key_pos = first + lax.broadcasted_iota(jnp.int32, (tokens, tokens), 1)
        allowed = (key_pos >= start) & (key_pos <= query_pos)
        bias[:, number * tokens : (number + 1) * tokens] = jnp.where(allowed, 0.0, MASKED)


def scores_of(query, keys, bias, head, at):
    tokens = bias.shape[0]
    return [
        lax.dot_general(
            query[:, column(head)], key[:, column(at)], (((1,), (1,)), ((), ())), preferred_element_type=jnp.float32
        )
        * SCORE_SCALE
        + bias[:, number * tokens : (number + 1) * tokens]
        for number, key in enumerate(keys)
    ]


def weighted(weights, blocks, at, ones):
    product = None
    for weight, block in zip(weights, blocks):
        term = dot(weight, jnp.concatenate([block[:, column(at)], ones], axis=1))
        product = term if product is None else product + term
    return product[:, :HEAD_SIZE], product[:, HEAD_SIZE:]


def row_max(scores):
    return jnp.max(functools.reduce(jnp.maximum, scores), axis=1, keepdims=True)


def near_kernel(distances, starts, query, *refs):
    count = len(distances)
    tops, totals, accs, bias = refs[-4:]
    parts = [refs[low : low + count] for low in range(0, len(refs) - 4, count)]
    fill_bias(bias, distances, starts)
    tokens = query.shape[0]
    heads = query.shape[1] // HEAD_SIZE
    kv_part = parts[0][0].shape[1] // (2 * HEAD_SIZE)
    group = heads // (kv_part * len(parts))
    ones = jnp.ones((tokens, HEAD_SIZE), query.dtype)

    def place(head):
        return parts[head // group // kv_part], head // group % kv_part

    def ask(head):
        blocks, at = place(head)
        return scores_of(query, blocks, bias, head, at)

    scores = ask(0)
    for head in range(heads):
        ahead = ask(head + 1) if head + 1 < heads else None
        top = row_max(scores)
        blocks, at = place(head)
        weights = [jnp.exp2(score - top).astype(query.dtype) for score in scores]
        tops[head] = jnp.broadcast_to(top, (tokens, HEAD_SIZE))
        accs[head], totals[head] = weighted(weights, blocks, kv_part + at, ones)
        scores = ahead


def join(scores, blocks, at, state, head, ones, dtype):
    tops, totals, accs = state
    before = tops[head]
    tokens = before.shape[0]
    top = jnp.maximum(jnp.broadcast_to(row_max(scores), before.shape), before)
    factor = jnp.exp2(before - top)
    wide_top = jnp.concatenate([top] * (tokens // HEAD_SIZE), axis=1)
    weights = [jnp.exp2(score - wide_top).astype(dtype) for score in scores]
    acc, total = weighted(weights, blocks, at, ones)
    return top, totals[head] * factor + total, accs[head] * factor + acc


def attend_far(low, skip, query, blocks, state, bias, put):
    tokens = query.shape[0]
    kv_part = blocks[0].shape[1] // (2 * HEAD_SIZE)
    heads = query.shape[1] // HEAD_SIZE // 2
    group = heads // kv_part
    ones = jnp.ones((tokens, HEAD_SIZE), query.dtype)
    scores = scores_of(query, blocks, bias, low, 0)
    for head in range(heads):
        ahead = scores_of(query, blocks, bias, low + head + 1, (head + 1) // group) if head + 1 < heads else None
        put(head, *join(scores, blocks, kv_part + head // group, state, skip + head, ones, query.dtype))
        scores = ahead


def into(attended):
    def put(head, top, total, acc):
        del top
        attended[:, column(head)] = (acc / total).astype(attended.dtype)

    return put


WIDE = 4 * HEAD_SIZE


def mix_first_kernel(distances, starts, query, *refs):
    far = len(distances)
    blocks, state, (weight, summed, attended, bias) = refs[:far], refs[far : far + 3], refs[far + 3 :]
    fill_bias(bias, distances, starts)
    attend_far(0, 0, query, blocks, state, bias, into(attended))
    depth = attended.shape[1]
    for number in range(summed.shape[1] // WIDE):
        at = slice(number * WIDE, (number + 1) * WIDE)
        summed[:, at] = dot(attended[...], weight[:depth, at])


def middle_kernel(low, query, second, first, tops, totals, accs, bias, new_tops, new_totals, new_accs):
    tokens = bias.shape[0]
    late = bias.at[:, pl.ds(bias.shape[1] - 2 * tokens, 2 * tokens)]

    def put(head, top, total, acc):
        new_tops[head], new_totals[head], new_accs[head] = top, total, acc

    attend_far(low, low, query, [first, second], (tops, totals, accs), late, put)


def rows_product(rows, low, attended, weight, summed, wide):
    depth = attended.shape[1]
    at = slice(low, low + wide)
    return summed[rows, at] + dot(attended[rows, :], weight[depth:, at])


def send_columns(low, attended, weight, summed, send):
    theirs = halves(send.shape[0])[1]
    for number in range(send.shape[1] // WIDE):
        result = rows_product(theirs, low + number * WIDE, attended, weight, summed, WIDE)
        send[:, number * WIDE : (number + 1) * WIDE] = result.astype(send.dtype)


def mix_second_kernel(low, query, block, tops, totals, accs, bias, weight, summed, send, attended):
    first = bias.at[:, pl.ds(0, bias.shape[0])]
    attend_far(low, 0, query, [block], (tops, totals, accs), first, into(attended))
    send_columns(0, attended, weight, summed, send)


def own_high_kernel(low, attended, weight, summed, own):
    mine = halves(own.shape[0])[0]
    for number in range(own.shape[1] // WIDE):
        result = rows_product(mine, low + number * WIDE, attended, weight, summed, WIDE)
        own[:, number * WIDE : (number + 1) * WIDE] = result


def own_low_kernel(attended, weight, summed, got, after, mixed):
    del after
    mine = halves(got.shape[0])[0]
    for number in range(got.shape[1] // WIDE):
        at = slice(number * WIDE, (number + 1) * WIDE)
        result = rows_product(mine, number * WIDE, attended, weight, summed, WIDE)
        mixed[:, at] = (result + got[:, at].astype(jnp.float32)).astype(mixed.dtype)


def add_kernel(mixed_low, own, got, mixed_hbm, mixed, sems):
    low = mixed_low.shape[1]
    copies = [pltpu.make_async_copy(mixed_low, mixed_hbm.at[:, pl.ds(0, low)], sems.at[0])]
    copies[0].start()
    for number in range(own.shape[1] // (2 * WIDE)):
        at = slice(number * 2 * WIDE, (number + 1) * (2 * WIDE))
        mixed[:, at] = (own[:, at] + got[:, at].astype(jnp.float32)).astype(mixed.dtype)
        there = mixed_hbm.at[:, pl.ds(low + number * 2 * WIDE, 2 * WIDE)]
        copies.append(pltpu.make_async_copy(mixed.at[:, pl.ds(number * 2 * WIDE, 2 * WIDE)], there, sems.at[number + 1]))
        copies[-1].start()
    for copy in copies:
        copy.wait()


def call(kernel, name, outs, in_specs, flops, nbytes, limit, scratch=(), out_specs=None):
    return pl.pallas_call(
        kernel,
        out_shape=outs,
        in_specs=in_specs,
        out_specs=out_specs or [VMEM] * len(outs),
        scratch_shapes=list(scratch),
        name=name,
        cost_estimate=pl.CostEstimate(flops=flops, bytes_accessed=nbytes, transcendentals=0),
        compiler_params=pltpu.CompilerParams(vmem_limit_bytes=limit << 20),
    )


def in_hbm(array):
    return pltpu.with_memory_space_constraint(array, pltpu.HBM)


def body(input_rows, doc_lengths, w_query, key_weight, value_weight, w_out):
    half, model = input_rows.shape
    tokens = 2 * half
    width_q, width_k = w_query.shape[1], key_weight.shape[1]
    heads = width_q // HEAD_SIZE
    shards = lax.axis_size("seq")
    bf16, f32 = jnp.bfloat16, jnp.float32
    shape = pltpu.VMEM

    other = lax.ppermute(input_rows, "head", SWAP)

    flag = shape((8, HEAD_SIZE), f32)
    table = shape((tokens, HEAD_SIZE), f32)
    part = width_k // 2
    kv_shape = shape((tokens, 2 * part), bf16)
    part_shape = shape((model, part), bf16)
    chunks = 2
    kv_flops = 4 * half * model * part
    total, own, w_key, w_value, cosine, sine, starts = call(
        functools.partial(first_kernel, chunks), "keys_values_own",
        [
            shape((half, 2 * part), f32), shape((half, model), bf16), part_shape, part_shape,
            table, table, shape((tokens, HEAD_SIZE), jnp.int32),
        ],
        [ANY] * 4, kv_flops, 2 * model * width_k, 4,
        [pltpu.SMEM(doc_lengths.shape, jnp.int32), pltpu.SemaphoreType.DMA((2 * chunks + 2,))],
    )(in_hbm(doc_lengths), in_hbm(input_rows), in_hbm(key_weight), in_hbm(value_weight))
    (kv_a,) = call(
        second_kernel, "keys_values", [kv_shape], [VMEM] * 6, kv_flops, 2 * model * width_k, 4,
    )(other, w_key, w_value, total, cosine, sine)

    every = range(shards)
    step_z = [(i, (i + LAYER) % shards) for i in every]
    z_a = lax.ppermute(kv_a, "seq", [(a, b) for a, b in step_z if a < b])

    kv_b, rows, done = call(
        functools.partial(third_kernel, chunks), "keys_values_more", [kv_shape, shape((tokens, model), bf16), flag],
        [VMEM, VMEM, ANY, ANY, VMEM, VMEM], VALUES_COST, 2 * model * width_k, 10,
        [part_shape, part_shape, pltpu.VMEM((tokens, 2 * part), f32), pltpu.SemaphoreType.DMA((2 * chunks,))],
    )(own, other, in_hbm(key_weight), in_hbm(value_weight), cosine, sine)
    z_b = lax.ppermute(kv_b, "seq", step_z)

    def exchange(mine, earlier, after, ways, cost):
        to = call(
            functools.partial(relay_kernel, ways), "relay", [kv_shape] * len(ways), [VMEM] * 3, cost, 2 << 20, 4,
        )(mine, earlier, after)
        return [lax.ppermute(array, "seq", [(i, i ^ way) for i in every]) for way, array in zip(ways, to)], to[0]

    (d_a,), done = exchange(kv_a, z_a, kv_b, (3,), RELAY_COST)
    (x_a, y_a), done = exchange(kv_a, z_a, done, (1, 2), 0)
    far_a = d_a, x_a, y_a
    query, done = call(
        query_kernel, "queries", [shape((tokens, width_q), bf16), flag], [VMEM] * 5,
        2 * tokens * model * width_q, 2 * model * width_q, 8,
    )(rows, w_query, cosine, sine, done)
    (x_b, y_b), _ = exchange(kv_b, z_b, done, (1, 2), 9 << 30)
    near = call(
        functools.partial(near_kernel, ((0, 0), (LAYER, LAYER))), "scores_near", [shape((heads, tokens, HEAD_SIZE), f32)] * 3,
        [VMEM] * 6, 8 * heads * tokens * tokens * HEAD_SIZE, 8 << 20, 12, [pltpu.VMEM((tokens, 2 * tokens), f32)],
    )(starts, query, kv_a, z_a, kv_b, z_b)
    (d_b,), _ = exchange(kv_b, z_b, near[0], (3,), 0)

    far = len(far_a)
    distances = ((1, 3), (3, 1), (2, 2))
    bias_shape = shape((tokens, far * tokens), f32)
    columns = w_out.shape[1]
    attended_shape = shape((tokens, width_q // 2), bf16)
    far_flops = 3 * far * heads * tokens * tokens * HEAD_SIZE
    out_flops = tokens * width_q * columns
    summed, _, bias = call(
        functools.partial(mix_first_kernel, distances), "mix_first",
        [shape((tokens, columns), f32), attended_shape, bias_shape],
        [VMEM] * (6 + far), out_flops + far_flops, 4 << 20, 10,
    )(starts, query, *far_a, *near, w_out)
    middle = call(
        functools.partial(middle_kernel, heads // 2), "attend_middle", [shape((heads // 2, tokens, HEAD_SIZE), f32)] * 3,
        [VMEM] * 7, far_flops // far * 2, 4 << 20, 10,
    )(query, y_b, x_b, *near, bias)

    cut = columns // 2
    send_shape = shape((half, cut), bf16)
    quarter = out_flops // 4
    send, attended = call(
        functools.partial(mix_second_kernel, heads // 2), "mix_second", [send_shape, attended_shape],
        [VMEM] * 8, quarter + far_flops // far, 4 << 20, 10,
    )(query, d_b, *middle, bias, w_out, summed)
    got_low = lax.ppermute(send, "head", SWAP)
    (send,) = call(
        functools.partial(send_columns, cut), "send_high", [send_shape], [VMEM] * 3, quarter, 4 << 20, 6,
    )(attended, w_out, summed)
    got_high = lax.ppermute(send, "head", SWAP)
    (own,) = call(
        functools.partial(own_high_kernel, cut), "own_high", [shape((half, columns - cut), f32)], [VMEM] * 3,
        quarter, 4 << 20, 6,
    )(attended, w_out, summed)
    (mixed,) = call(
        own_low_kernel, "own_low", [send_shape], [VMEM] * 5, quarter, 4 << 20, 6,
    )(attended, w_out, summed, got_low, own)
    (mixed,) = call(
        add_kernel, "add", [pltpu.HBM((half, columns), bf16)], [VMEM] * 3, half * cut, 4 << 20, 4,
        [pltpu.VMEM((half, columns - cut), bf16), pltpu.SemaphoreType.DMA(((columns - cut) // (2 * WIDE) + 1,))], [ANY],
    )(mixed, own, got_high)
    return mixed


def solution(mesh):
    in_specs = (
        P(("seq", "head"), None),
        P(),
        P(None, "head"),
        P(None, "head"),
        P(None, "head"),
        P("head", None),
    )
    out_specs = P(("seq", "head"), None)
    return jax.shard_map(body, mesh=mesh, in_specs=in_specs, out_specs=out_specs, check_vma=False)
```

```python
import functools
import math

import jax
import jax.numpy as jnp
from jax import lax
from jax.experimental import pallas as pl
from jax.experimental.pallas import tpu as pltpu
from jax.sharding import PartitionSpec as P

HEAD_SIZE = 128
LAYER = 4
MASKED = -1e30
VALUES_COST = 4 << 30
RELAY_COST = 5 << 30
SCORE_SCALE = math.log2(math.e) * HEAD_SIZE ** (-0.5)
SWAP = [(0, 1), (1, 0)]
VMEM = pl.BlockSpec(memory_space=pltpu.VMEM)
ANY = pl.BlockSpec(memory_space=pl.ANY)


def inverse_frequency():
    table = []
    for number in range(HEAD_SIZE // 2):
        base_freq = 500000.0 ** (-(2.0 * number) / HEAD_SIZE)
        wavelength = 2.0 * math.pi / base_freq
        smooth = (8192.0 / wavelength - 1.0) / 3.0
        if wavelength < 2048.0:
            table.append(base_freq)
        elif wavelength > 8192.0:
            table.append(base_freq / 8.0)
        else:
            table.append((1.0 - smooth) * base_freq / 8.0 + smooth * base_freq)
    return table


def dot(a, b):
    return jnp.dot(a, b, preferred_element_type=jnp.float32)


def rotated(block, cosine, sine):
    return block * cosine + pltpu.roll(block, HEAD_SIZE // 2, 1) * sine


def piece_bounds(depth, chunks):
    cuts = [0, depth * 3 // 4, depth] if chunks == 2 else [depth * number // chunks for number in range(chunks + 1)]
    return list(zip(cuts[:-1], cuts[1:]))


def load_columns(low, hbms, buffers, sems, chunks):
    depth, wide = buffers[0].shape
    copies = []
    for number, (first, last) in enumerate(piece_bounds(depth, chunks)):
        at = pl.ds(first, last - first)
        pair = [
            pltpu.make_async_copy(hbm.at[at, pl.ds(low, wide)], buffer.at[at], sems.at[number * len(hbms) + which])
            for which, (hbm, buffer) in enumerate(zip(hbms, buffers))
        ]
        for copy in pair:
            copy.start()
        copies.append(pair)
    return copies


def piecewise_product(rows, copies, buffers, total, put=None):
    depth, wide = buffers[0].shape
    for number, (pair, (first, last)) in enumerate(zip(copies, piece_bounds(depth, len(copies)))):
        at = slice(first, last)
        for which, (copy, buffer) in enumerate(zip(pair, buffers)):
            copy.wait()
            columns = slice(which * wide, (which + 1) * wide)
            product = dot(rows[:, at], buffer[at, :])
            if number > 0:
                product = product + total[:, columns]
            if put is None or number < len(copies) - 1:
                total[:, columns] = product
            else:
                put(which, product)


def first_kernel(chunks, lengths_hbm, own_hbm, key_hbm, value_hbm, total, own, w_key, w_value, cosine, sine, starts, lengths, sems):
    row_copy = pltpu.make_async_copy(own_hbm, own, sems.at[2 * chunks])
    row_copy.start()
    copies = load_columns(0, (key_hbm, value_hbm), (w_key, w_value), sems, chunks)
    tokens = cosine.shape[0]
    length_copy = pltpu.make_async_copy(lengths_hbm, lengths, sems.at[2 * chunks + 1])
    length_copy.start()
    lane = lax.broadcasted_iota(jnp.int32, (1, HEAD_SIZE), 1)
    pair_of_lane = lane % (HEAD_SIZE // 2)
    freq = jnp.zeros((1, HEAD_SIZE), jnp.float32)
    for number, value in enumerate(inverse_frequency()):
        freq = jnp.where(pair_of_lane == number, jnp.float32(value), freq)
    first = lax.axis_index("seq") * tokens
    half = tokens // 2
    low_lane = lane < HEAD_SIZE // 2
    packed = first + lax.broadcasted_iota(jnp.int32, (half, HEAD_SIZE), 0) + jnp.where(low_lane, 0, half)
    angles = packed.astype(jnp.float32) * freq
    turned = jnp.cos(angles)
    other = pltpu.roll(turned, HEAD_SIZE // 2, 1)
    cosine[:half, :] = jnp.where(low_lane, turned, other)
    cosine[half:, :] = jnp.where(low_lane, other, turned)
    turned = jnp.sin(angles)
    other = pltpu.roll(turned, HEAD_SIZE // 2, 1)
    sine[:half, :] = jnp.where(low_lane, -turned, other)
    sine[half:, :] = jnp.where(low_lane, -other, turned)
    positions = first + lax.broadcasted_iota(jnp.int32, (tokens, HEAD_SIZE), 0)
    length_copy.wait()
    start = jnp.zeros((tokens, HEAD_SIZE), jnp.int32)
    end = jnp.int32(0)
    for number in range(lengths.shape[0]):
        end = end + lengths[number]
        start = jnp.where(positions >= end, end, start)
    starts[...] = start
    row_copy.wait()
    piecewise_product(own, copies, (w_key, w_value), total)


def halves(half):
    core = lax.axis_index("head")
    return pl.ds(pl.multiple_of(core * half, half), half), pl.ds(pl.multiple_of((1 - core) * half, half), half)


def put_block(kv, here, block, cosine, sine, is_key, low):
    for head in range(block.shape[1] // HEAD_SIZE):
        piece = block[:, head * HEAD_SIZE : (head + 1) * HEAD_SIZE]
        if is_key:
            piece = rotated(piece, cosine[here, :], sine[here, :])
        kv[here, low + head * HEAD_SIZE : low + (head + 1) * HEAD_SIZE] = piece.astype(kv.dtype)


def second_kernel(other, w_key, w_value, own_total, cosine, sine, kv):
    half, wide = own_total.shape[0], w_key.shape[1]
    mine, theirs = halves(half)
    for which, weight in enumerate((w_key, w_value)):
        low = which * wide
        put_block(kv, mine, own_total[:, low : low + wide], cosine, sine, which == 0, low)
        put_block(kv, theirs, dot(other[...], weight[...]), cosine, sine, which == 0, low)


def third_kernel(chunks, own, other, key_hbm, value_hbm, cosine, sine, kv, rows, done, w_key, w_value, total, sems):
    wide = w_key.shape[1]
    copies = load_columns(wide, (key_hbm, value_hbm), (w_key, w_value), sems, chunks)
    mine, theirs = halves(own.shape[0])
    rows[mine, :] = own[...]
    rows[theirs, :] = other[...]
    done[...] = jnp.zeros_like(done)
    everything = slice(0, rows.shape[0])

    def put(which, product):
        put_block(kv, everything, product, cosine, sine, which == 0, which * wide)

    piecewise_product(rows, copies, (w_key, w_value), total, put)


def query_kernel(rows, weight, cosine, sine, after, query, done):
    del after
    done[...] = jnp.zeros_like(done)
    wide = 4 * HEAD_SIZE
    for number in range(weight.shape[1] // wide):
        result = dot(rows[...], weight[:, number * wide : (number + 1) * wide])
        for head in range(wide // HEAD_SIZE):
            at = slice(head * HEAD_SIZE, (head + 1) * HEAD_SIZE)
            out = slice(number * wide + head * HEAD_SIZE, number * wide + (head + 1) * HEAD_SIZE)
            query[:, out] = rotated(result[:, at], cosine[...], sine[...]).astype(query.dtype)


def relay_kernel(ways, own, earlier, after, *outs):
    del after
    index = lax.axis_index("seq")
    mine, theirs = own[...], earlier[...]
    for way, out in zip(ways, outs):
        upper = index % 2 > 0 if way == 1 else index % LAYER >= 2
        out[...] = jnp.where(upper, theirs, mine)


def column(number):
    return slice(number * HEAD_SIZE, (number + 1) * HEAD_SIZE)


def fill_bias(bias, distances, starts):
    tokens = bias.shape[0]
    index = lax.axis_index("seq")
    base = index * tokens
    query_pos = base + lax.broadcasted_iota(jnp.int32, (tokens, tokens), 0)
    start = jnp.concatenate([starts[...]] * (tokens // starts.shape[1]), axis=1)
    for number, (even, odd) in enumerate(distances):
        first = base - tokens * jnp.where(index % 2 > 0, odd, even)
        key_pos = first + lax.broadcasted_iota(jnp.int32, (tokens, tokens), 1)
        allowed = (key_pos >= start) & (key_pos <= query_pos)
        bias[:, number * tokens : (number + 1) * tokens] = jnp.where(allowed, 0.0, MASKED)


def scores_of(query, keys, bias, head, at):
    tokens = bias.shape[0]
    return [
        lax.dot_general(
            query[:, column(head)], key[:, column(at)], (((1,), (1,)), ((), ())), preferred_element_type=jnp.float32
        )
        * SCORE_SCALE
        + bias[:, number * tokens : (number + 1) * tokens]
        for number, key in enumerate(keys)
    ]


def weighted(weights, blocks, at, ones):
    product = None
    for weight, block in zip(weights, blocks):
        term = dot(weight, jnp.concatenate([block[:, column(at)], ones], axis=1))
        product = term if product is None else product + term
    return product[:, :HEAD_SIZE], product[:, HEAD_SIZE:]


def row_max(scores):
    return jnp.max(functools.reduce(jnp.maximum, scores), axis=1, keepdims=True)


def near_kernel(distances, starts, query, *refs):
    count = len(distances)
    tops, totals, accs, bias = refs[-4:]
    parts = [refs[low : low + count] for low in range(0, len(refs) - 4, count)]
    fill_bias(bias, distances, starts)
    tokens = query.shape[0]
    heads = query.shape[1] // HEAD_SIZE
    kv_part = parts[0][0].shape[1] // (2 * HEAD_SIZE)
    group = heads // (kv_part * len(parts))
    ones = jnp.ones((tokens, HEAD_SIZE), query.dtype)

    def place(head):
        return parts[head // group // kv_part], head // group % kv_part

    def ask(head):
        blocks, at = place(head)
        return scores_of(query, blocks, bias, head, at)

    scores = ask(0)
    for head in range(heads):
        ahead = ask(head + 1) if head + 1 < heads else None
        top = row_max(scores)
        blocks, at = place(head)
        weights = [jnp.exp2(score - top).astype(query.dtype) for score in scores]
        tops[head] = jnp.broadcast_to(top, (tokens, HEAD_SIZE))
        accs[head], totals[head] = weighted(weights, blocks, kv_part + at, ones)
        scores = ahead


def join(scores, blocks, at, state, head, ones, dtype):
    tops, totals, accs = state
    before = tops[head]
    tokens = before.shape[0]
    top = jnp.maximum(jnp.broadcast_to(row_max(scores), before.shape), before)
    factor = jnp.exp2(before - top)
    wide_top = jnp.concatenate([top] * (tokens // HEAD_SIZE), axis=1)
    weights = [jnp.exp2(score - wide_top).astype(dtype) for score in scores]
    acc, total = weighted(weights, blocks, at, ones)
    return top, totals[head] * factor + total, accs[head] * factor + acc


def attend_far(low, skip, query, blocks, state, bias, put):
    tokens = query.shape[0]
    kv_part = blocks[0].shape[1] // (2 * HEAD_SIZE)
    heads = query.shape[1] // HEAD_SIZE // 2
    group = heads // kv_part
    ones = jnp.ones((tokens, HEAD_SIZE), query.dtype)
    scores = scores_of(query, blocks, bias, low, 0)
    for head in range(heads):
        ahead = scores_of(query, blocks, bias, low + head + 1, (head + 1) // group) if head + 1 < heads else None
        put(head, *join(scores, blocks, kv_part + head // group, state, skip + head, ones, query.dtype))
        scores = ahead


def into(attended):
    def put(head, top, total, acc):
        del top
        attended[:, column(head)] = (acc / total).astype(attended.dtype)

    return put


WIDE = 4 * HEAD_SIZE


def mix_first_kernel(distances, starts, query, *refs):
    far = len(distances)
    blocks, state, (weight, summed, attended, bias) = refs[:far], refs[far : far + 3], refs[far + 3 :]
    fill_bias(bias, distances, starts)
    attend_far(0, 0, query, blocks, state, bias, into(attended))
    depth = attended.shape[1]
    for number in range(summed.shape[1] // WIDE):
        at = slice(number * WIDE, (number + 1) * WIDE)
        summed[:, at] = dot(attended[...], weight[:depth, at])


def middle_kernel(low, query, second, first, tops, totals, accs, bias, new_tops, new_totals, new_accs):
    tokens = bias.shape[0]
    late = bias.at[:, pl.ds(bias.shape[1] - 2 * tokens, 2 * tokens)]

    def put(head, top, total, acc):
        new_tops[head], new_totals[head], new_accs[head] = top, total, acc

    attend_far(low, low, query, [first, second], (tops, totals, accs), late, put)


def rows_product(rows, low, attended, weight, summed, wide):
    depth = attended.shape[1]
    at = slice(low, low + wide)
    return summed[rows, at] + dot(attended[rows, :], weight[depth:, at])


def send_columns(low, attended, weight, summed, send):
    theirs = halves(send.shape[0])[1]
    for number in range(send.shape[1] // WIDE):
        result = rows_product(theirs, low + number * WIDE, attended, weight, summed, WIDE)
        send[:, number * WIDE : (number + 1) * WIDE] = result.astype(send.dtype)


def mix_second_kernel(low, query, block, tops, totals, accs, bias, weight, summed, send, attended):
    first = bias.at[:, pl.ds(0, bias.shape[0])]
    attend_far(low, 0, query, [block], (tops, totals, accs), first, into(attended))
    send_columns(0, attended, weight, summed, send)


def own_high_kernel(low, attended, weight, summed, own):
    mine = halves(own.shape[0])[0]
    for number in range(own.shape[1] // WIDE):
        result = rows_product(mine, low + number * WIDE, attended, weight, summed, WIDE)
        own[:, number * WIDE : (number + 1) * WIDE] = result


def own_low_kernel(attended, weight, summed, got, after, mixed):
    del after
    mine = halves(got.shape[0])[0]
    for number in range(got.shape[1] // WIDE):
        at = slice(number * WIDE, (number + 1) * WIDE)
        result = rows_product(mine, number * WIDE, attended, weight, summed, WIDE)
        mixed[:, at] = (result + got[:, at].astype(jnp.float32)).astype(mixed.dtype)


def add_kernel(mixed_low, own, got, mixed_hbm, mixed, sems):
    low = mixed_low.shape[1]
    copies = [pltpu.make_async_copy(mixed_low, mixed_hbm.at[:, pl.ds(0, low)], sems.at[0])]
    copies[0].start()
    for number in range(own.shape[1] // (2 * WIDE)):
        at = slice(number * 2 * WIDE, (number + 1) * (2 * WIDE))
        mixed[:, at] = (own[:, at] + got[:, at].astype(jnp.float32)).astype(mixed.dtype)
        there = mixed_hbm.at[:, pl.ds(low + number * 2 * WIDE, 2 * WIDE)]
        copies.append(pltpu.make_async_copy(mixed.at[:, pl.ds(number * 2 * WIDE, 2 * WIDE)], there, sems.at[number + 1]))
        copies[-1].start()
    for copy in copies:
        copy.wait()


def call(kernel, name, outs, in_specs, flops, nbytes, limit, scratch=(), out_specs=None):
    return pl.pallas_call(
        kernel,
        out_shape=outs,
        in_specs=in_specs,
        out_specs=out_specs or [VMEM] * len(outs),
        scratch_shapes=list(scratch),
        name=name,
        cost_estimate=pl.CostEstimate(flops=flops, bytes_accessed=nbytes, transcendentals=0),
        compiler_params=pltpu.CompilerParams(vmem_limit_bytes=limit << 20),
    )


def in_hbm(array):
    return pltpu.with_memory_space_constraint(array, pltpu.HBM)


def body(input_rows, doc_lengths, w_query, key_weight, value_weight, w_out):
    half, model = input_rows.shape
    tokens = 2 * half
    width_q, width_k = w_query.shape[1], key_weight.shape[1]
    heads = width_q // HEAD_SIZE
    shards = lax.axis_size("seq")
    bf16, f32 = jnp.bfloat16, jnp.float32
    shape = pltpu.VMEM

    other = lax.ppermute(input_rows, "head", SWAP)

    flag = shape((8, HEAD_SIZE), f32)
    table = shape((tokens, HEAD_SIZE), f32)
    part = width_k // 2
    kv_shape = shape((tokens, 2 * part), bf16)
    part_shape = shape((model, part), bf16)
    chunks = 2
    kv_flops = 4 * half * model * part
    total, own, w_key, w_value, cosine, sine, starts = call(
        functools.partial(first_kernel, chunks), "keys_values_own",
        [
            shape((half, 2 * part), f32), shape((half, model), bf16), part_shape, part_shape,
            table, table, shape((tokens, HEAD_SIZE), jnp.int32),
        ],
        [ANY] * 4, kv_flops, 2 * model * width_k, 4,
        [pltpu.SMEM(doc_lengths.shape, jnp.int32), pltpu.SemaphoreType.DMA((2 * chunks + 2,))],
    )(in_hbm(doc_lengths), in_hbm(input_rows), in_hbm(key_weight), in_hbm(value_weight))
    (kv_a,) = call(
        second_kernel, "keys_values", [kv_shape], [VMEM] * 6, kv_flops, 2 * model * width_k, 4,
    )(other, w_key, w_value, total, cosine, sine)

    every = range(shards)
    step_z = [(i, (i + LAYER) % shards) for i in every]
    z_a = lax.ppermute(kv_a, "seq", [(a, b) for a, b in step_z if a < b])

    kv_b, rows, done = call(
        functools.partial(third_kernel, chunks), "keys_values_more", [kv_shape, shape((tokens, model), bf16), flag],
        [VMEM, VMEM, ANY, ANY, VMEM, VMEM], VALUES_COST, 2 * model * width_k, 10,
        [part_shape, part_shape, pltpu.VMEM((tokens, 2 * part), f32), pltpu.SemaphoreType.DMA((2 * chunks,))],
    )(own, other, in_hbm(key_weight), in_hbm(value_weight), cosine, sine)
    z_b = lax.ppermute(kv_b, "seq", step_z)

    def exchange(mine, earlier, after, ways, cost):
        to = call(
            functools.partial(relay_kernel, ways), "relay", [kv_shape] * len(ways), [VMEM] * 3, cost, 2 << 20, 4,
        )(mine, earlier, after)
        return [lax.ppermute(array, "seq", [(i, i ^ way) for i in every]) for way, array in zip(ways, to)], to[0]

    (d_a,), done = exchange(kv_a, z_a, kv_b, (3,), RELAY_COST)
    (x_a, y_a), done = exchange(kv_a, z_a, done, (1, 2), 0)
    far_a = d_a, x_a, y_a
    query, done = call(
        query_kernel, "queries", [shape((tokens, width_q), bf16), flag], [VMEM] * 5,
        2 * tokens * model * width_q, 2 * model * width_q, 8,
    )(rows, w_query, cosine, sine, done)
    (x_b, y_b), _ = exchange(kv_b, z_b, done, (1, 2), 9 << 30)
    near = call(
        functools.partial(near_kernel, ((0, 0), (LAYER, LAYER))), "scores_near", [shape((heads, tokens, HEAD_SIZE), f32)] * 3,
        [VMEM] * 6, 8 * heads * tokens * tokens * HEAD_SIZE, 8 << 20, 12, [pltpu.VMEM((tokens, 2 * tokens), f32)],
    )(starts, query, kv_a, z_a, kv_b, z_b)
    (d_b,), _ = exchange(kv_b, z_b, near[0], (3,), 0)

    far = len(far_a)
    distances = ((1, 3), (3, 1), (2, 2))
    bias_shape = shape((tokens, far * tokens), f32)
    columns = w_out.shape[1]
    attended_shape = shape((tokens, width_q // 2), bf16)
    far_flops = 3 * far * heads * tokens * tokens * HEAD_SIZE
    out_flops = tokens * width_q * columns
    summed, _, bias = call(
        functools.partial(mix_first_kernel, distances), "mix_first",
        [shape((tokens, columns), f32), attended_shape, bias_shape],
        [VMEM] * (6 + far), out_flops + far_flops, 4 << 20, 10,
    )(starts, query, *far_a, *near, w_out)
    middle = call(
        functools.partial(middle_kernel, heads // 2), "attend_middle", [shape((heads // 2, tokens, HEAD_SIZE), f32)] * 3,
        [VMEM] * 7, far_flops // far * 2, 4 << 20, 10,
    )(query, y_b, x_b, *near, bias)

    cut = columns // 2
    send_shape = shape((half, cut), bf16)
    quarter = out_flops // 4
    send, attended = call(
        functools.partial(mix_second_kernel, heads // 2), "mix_second", [send_shape, attended_shape],
        [VMEM] * 8, quarter + far_flops // far, 4 << 20, 10,
    )(query, d_b, *middle, bias, w_out, summed)
    got_low = lax.ppermute(send, "head", SWAP)
    (send,) = call(
        functools.partial(send_columns, cut), "send_high", [send_shape], [VMEM] * 3, quarter, 4 << 20, 6,
    )(attended, w_out, summed)
    got_high = lax.ppermute(send, "head", SWAP)
    (own,) = call(
        functools.partial(own_high_kernel, cut), "own_high", [shape((half, columns - cut), f32)], [VMEM] * 3,
        quarter, 4 << 20, 6,
    )(attended, w_out, summed)
    (mixed,) = call(
        own_low_kernel, "own_low", [send_shape], [VMEM] * 5, quarter, 4 << 20, 6,
    )(attended, w_out, summed, got_low, own)
    (mixed,) = call(
        add_kernel, "add", [pltpu.HBM((half, columns), bf16)], [VMEM] * 3, half * cut, 4 << 20, 4,
        [pltpu.VMEM((half, columns - cut), bf16), pltpu.SemaphoreType.DMA(((columns - cut) // (2 * WIDE) + 1,))], [ANY],
    )(mixed, own, got_high)
    return mixed


def solution(mesh):
    in_specs = (
        P(("seq", "head"), None),
        P(),
        P(None, "head"),
        P(None, "head"),
        P(None, "head"),
        P("head", None),
    )
    out_specs = P(("seq", "head"), None)
    return jax.shard_map(body, mesh=mesh, in_specs=in_specs, out_specs=out_specs, check_vma=False)
```
